32 devices in a mesh: dp: 16 (over z, y, x), tensor: 2 (over core).
Axes of the slice: x: 2, y: 2, z: 4, core: 2. Of those that a mesh axis runs over, the one named last changes fastest.
Arguments:
- hidden: float32 [32768, 768], P('dp'), may hold values from -6 to 6
- cotangent: float32 [32768, 768], P('dp'), may hold values from -6 to 6
- norm_weight: float32 [768], replicated, may hold values from 0.5 to 1.5
- gate_in: bfloat16 [768, 1536], P(None, 'tensor'), may hold values from -0.21875 to 0.21875
- value_in: bfloat16 [768, 1536], P(None, 'tensor'), may hold values from -0.21875 to 0.21875
- state_in: bfloat16 [768, 256], replicated, may hold values from -0.21875 to 0.21875
- step_in: bfloat16 [768, 24], P(None, 'tensor'), may hold values from -0.21875 to 0.21875
- value_kernel: float32 [4, 1536], P(None, 'tensor'), may hold values from -3 to 3
- value_offset: float32 [1536], P('tensor'), may hold values from -0.5 to 0.5
- state_kernel: float32 [4, 256], replicated, may hold values from -3 to 3
- state_offset: float32 [256], replicated, may hold values from -0.5 to 0.5
- step_bias: float32 [24], P('tensor'), may hold values from -5 to -2
- log_decay: float32 [24], P('tensor'), may hold values from -3 to 0
- skip_weight: float32 [24], P('tensor'), may hold values from 0.5 to 1.5
- gated_norm: float32 [1536], P('tensor'), may hold values from 0.5 to 1.5
- out_weight: bfloat16 [1536, 768], P('tensor'), may hold values from -0.15625 to 0.15625
Outputs:
- block_out: float32 [32768, 768], P('dp')
- grad_hidden: float32 [32768, 768], P('dp')
- grad_norm_weight: float32 [768], replicated
- grad_gate_in: float32 [768, 1536], P(None, 'tensor')
- grad_value_in: float32 [768, 1536], P(None, 'tensor')
- grad_state_in: float32 [768, 256], replicated
- grad_step_in: float32 [768, 24], P(None, 'tensor')
- grad_value_kernel: float32 [4, 1536], P(None, 'tensor')
- grad_value_offset: float32 [1536], P('tensor')
- grad_state_kernel: float32 [4, 256], replicated
- grad_state_offset: float32 [256], replicated
- grad_step_bias: float32 [24], P('tensor')
- grad_log_decay: float32 [24], P('tensor')
- grad_skip_weight: float32 [24], P('tensor')
- grad_gated_norm: float32 [1536], P('tensor')
- grad_out_weight: float32 [1536, 768], P('tensor')
The draws below stay inside these ranges and needn't reach their ends.
All inputs are finite; a program needn't handle non-finite values.
Results may differ from the reference program's by a relative error of at most 0.0081.
Values sent between devices are 32-bit elements; how exact they have to be, the bound alone decides.
No kernel may reach another device: no remote copies, remote signals or barrier semaphores. Data moves between devices by JAX's collectives and lax.ppermute only.
A program may use at most 192 MiB of HBM per device.

```python
import jax
import jax.numpy as jnp
from jax import lax

D = 768
HEADS = 24
HEAD_DIM = 64
STATE = 128
CONV_W = 4
BLOCK = 256
LENGTH = 512
SEQ_DEV = 4
DI = 1536
TOKENS = 32768
N_DP = 16


def shard_levels(rng, dims, split, least, high):
    loudness, own = 1.0, jax.random.fold_in(rng, 6)
    for position, parts in split:
        steps = jnp.exp(jax.random.uniform(jax.random.fold_in(own, position), (parts,), jnp.float32, least / len(split), high / len(split)))
        loudness = loudness * jnp.repeat(steps, dims[position] // parts).reshape([-1 if axis == position else 1 for axis in range(len(dims))])
    return loudness


def scatter_about(key, extent, scale, reach, shards=(), held_as=jnp.bfloat16):
    entries = jax.random.normal(key, extent, jnp.float32) * scale
    if len(shards) > 0:
        entries = shard_levels(key, extent, shards, -0.22, 0.18) * entries
    return jnp.clip(entries, min=-reach, max=reach).astype(held_as)


def setup_inputs(seed: int = 0) -> dict:
    keys = jax.random.split(jax.random.key(seed), 17)
    hidden = scatter_about(keys[0], (TOKENS, D), 1.0, 6.0, ((0, 16),), jnp.float32)
    cotangent = scatter_about(keys[1], (TOKENS, D), 1.0, 6.0, ((0, 16),), jnp.float32)
    norm_weight = jnp.clip(1.0 + 0.1 * jax.random.normal(keys[2], (D,), jnp.float32), 0.5, 1.5)
    gate_in = scatter_about(keys[3], (D, DI), D ** -0.5, 0.21875, ((1, 2),))
    value_in = scatter_about(keys[4], (D, DI), D ** -0.5, 0.21875, ((1, 2),))
    state_in = scatter_about(keys[5], (D, 2 * STATE), D ** -0.5, 0.21875)
    step_in = scatter_about(keys[6], (D, HEADS), D ** -0.5, 0.21875, ((1, 2),))
    value_kernel = scatter_about(keys[7], (CONV_W, DI), CONV_W ** -0.5, 3.0, ((1, 2),), jnp.float32)
    value_offset = jnp.clip(jax.random.uniform(keys[8], (DI,), jnp.float32, -0.5, 0.5) * shard_levels(keys[8], (DI,), ((0, 2),), -0.4, 0.0), -0.5, 0.5)
    state_kernel = scatter_about(keys[9], (CONV_W, 2 * STATE), CONV_W ** -0.5, 3.0, (), jnp.float32)
    state_offset = jnp.clip(jax.random.uniform(keys[10], (2 * STATE,), jnp.float32, -0.5, 0.5), -0.5, 0.5)
    step_bias = jnp.clip(-5.0 + 3.0 * jax.random.uniform(keys[11], (HEADS,), jnp.float32) ** shard_levels(keys[11], (HEADS,), ((0, 2),), -0.2, 0.2), -5.0, -2.0)
    log_decay = jnp.clip(-3.0 + 3.0 * jax.random.uniform(keys[12], (HEADS,), jnp.float32) ** shard_levels(keys[12], (HEADS,), ((0, 2),), -0.2, 0.2), -3.0, 0.0)
    skip_weight = jnp.clip(0.5 + 1.0 * jax.random.uniform(keys[13], (HEADS,), jnp.float32) ** shard_levels(keys[13], (HEADS,), ((0, 2),), -0.2, 0.2), 0.5, 1.5)
    gated_norm = jnp.clip(1.0 + 0.1 * jax.random.normal(keys[14], (DI,), jnp.float32), 0.5, 1.5)
    out_weight = scatter_about(keys[15], (DI, D), DI ** -0.5, 0.15625, ((0, 2),))
    return {"hidden": hidden, "cotangent": cotangent, "norm_weight": norm_weight, "gate_in": gate_in, "value_in": value_in, "state_in": state_in, "step_in": step_in, "value_kernel": value_kernel, "value_offset": value_offset, "state_kernel": state_kernel, "state_offset": state_offset, "step_bias": step_bias, "log_decay": log_decay, "skip_weight": skip_weight, "gated_norm": gated_norm, "out_weight": out_weight}


@jax.custom_vjp
def low(v):
    return lax.optimization_barrier(v.astype(jnp.bfloat16)).astype(jnp.float32)

@jax.custom_vjp
def low_back(v):
    return v

def low_keep(v):
    return (low(v), None)

def low_pass(kept, grad):
    return (grad,)

def back_keep(v):
    return (v, None)

def back_low(kept, grad):
    return (low(grad),)
low.defvjp(low_keep, low_pass)
low_back.defvjp(back_keep, back_low)
EPSILON = 1e-05
HIGHEST = lax.Precision.HIGHEST

def conv_silu(series, kernel, kernel_bias):
    tap_count = kernel.shape[0]
    positions = series.shape[1]
    padded = jnp.pad(series, ((0, 0), (tap_count - 1, 0), (0, 0)))
    summed = kernel_bias + kernel[0] * padded[:, 0:positions]
    for offset in range(1, tap_count):
        summed = summed + kernel[offset] * padded[:, offset:offset + positions]
    return jax.nn.silu(summed)

def state_scan(values, write_rows, read_rows, step_sizes, decay_rates):
    block_size = values.shape[1]
    log_steps = step_sizes * decay_rates
    running = jnp.cumsum(log_steps, axis=1)
    causal = jnp.arange(block_size)[:, None] >= jnp.arange(block_size)[None, :]
    log_gaps = running[:, :, None, :] - running[:, None, :, :]
    pair_decay = jnp.exp(jnp.where(causal[None, :, :, None], log_gaps, -1e+30))
    intersections = jnp.einsum('bin,bjn->bij', read_rows, write_rows, precision=HIGHEST)
    mixing = intersections[:, :, :, None] * pair_decay * step_sizes[:, None, :, :]
    within = jnp.einsum('bijh,bjhp->bihp', mixing, values, precision=HIGHEST)
    tail_decay = jnp.exp(running[:, -1:, :] - running) * step_sizes
    block_states = jnp.einsum('bjh,bjhp,bjn->bhpn', tail_decay, values, write_rows, precision=HIGHEST)
    block_decay = jnp.exp(running[:, -1, :])

    def carry_state(carried, element):
        block_state, block_factor = element
        return (block_factor[:, None, None] * carried + block_state, carried)
    initial = jnp.zeros(block_states.shape[1:], jnp.float32)
    final_state, entering = lax.scan(carry_state, initial, (block_states, block_decay))
    across = jnp.einsum('bin,bhpn->bihp', read_rows, entering, precision=HIGHEST) * jnp.exp(running)[:, :, :, None]
    return within + across

def mix_heads(value_raw, step_raw, gate_raw, state_inputs, value_kernel, value_offset, step_bias, log_decay, skip_weight):
    token_count = value_raw.shape[0]
    channels = value_raw.shape[1]
    head_count = step_raw.shape[1]
    sequences = token_count // LENGTH
    blocks = LENGTH // BLOCK
    conv_values = conv_silu(value_raw.reshape(sequences, LENGTH, channels), value_kernel, value_offset)
    step_sizes = jax.nn.softplus(step_raw + step_bias).reshape(sequences, blocks, BLOCK, head_count)
    per_head = conv_values.reshape(sequences, blocks, BLOCK, head_count, HEAD_DIM)
    write_rows = state_inputs[:, :, :STATE].reshape(sequences, blocks, BLOCK, STATE)
    read_rows = state_inputs[:, :, STATE:].reshape(sequences, blocks, BLOCK, STATE)
    decay_rates = -jnp.exp(log_decay)
    scanned = jax.vmap(state_scan, in_axes=(0, 0, 0, 0, None))(per_head, write_rows, read_rows, step_sizes, decay_rates)
    direct = per_head * skip_weight[:, None]
    mixed_rows = scanned.reshape(token_count, channels) + direct.reshape(token_count, channels)
    return mixed_rows * jax.nn.silu(gate_raw)

def forward(hidden, norm_weight, gate_in, value_in, state_in, step_in, value_kernel, value_offset, state_kernel, state_offset, step_bias, log_decay, skip_weight, gated_norm, out_weight):
    row_scale = lax.rsqrt(lax.optimization_barrier(jnp.mean(hidden * hidden, axis=-1, keepdims=True)) + EPSILON)
    normed = low(hidden * row_scale * norm_weight)
    gate_raw = low_back(jnp.dot(normed, gate_in, precision=HIGHEST, preferred_element_type=jnp.float32))
    value_raw = low_back(jnp.dot(normed, value_in, precision=HIGHEST, preferred_element_type=jnp.float32))
    state_raw = low_back(jnp.dot(normed, state_in, precision=HIGHEST, preferred_element_type=jnp.float32))
    step_raw = low_back(jnp.dot(normed, step_in, precision=HIGHEST, preferred_element_type=jnp.float32))
    sequences = hidden.shape[0] // LENGTH
    state_inputs = conv_silu(state_raw.reshape(sequences, LENGTH, 2 * STATE), state_kernel, state_offset)
    gated_rows = mix_heads(value_raw, step_raw, gate_raw, state_inputs, value_kernel, value_offset, step_bias, log_decay, skip_weight)
    gate_scale = lax.rsqrt(lax.optimization_barrier(jnp.mean(gated_rows * gated_rows, axis=-1, keepdims=True)) + EPSILON)
    scaled = low(gated_rows * gate_scale * gated_norm)
    branch = low_back(jnp.dot(scaled, out_weight, precision=HIGHEST, preferred_element_type=jnp.float32))
    return hidden + branch

def reference(hidden, cotangent, norm_weight, gate_in, value_in, state_in, step_in, value_kernel, value_offset, state_kernel, state_offset, step_bias, log_decay, skip_weight, gated_norm, out_weight):
    weights = tuple((weight.astype(jnp.float32) for weight in (norm_weight, gate_in, value_in, state_in, step_in, value_kernel, value_offset, state_kernel, state_offset, step_bias, log_decay, skip_weight, gated_norm, out_weight)))
    hidden_groups = hidden.reshape(N_DP, SEQ_DEV * LENGTH, D)
    upstream_groups = cotangent.reshape(N_DP, SEQ_DEV * LENGTH, D)

    def one_group(totals, pieces):
        group_rows, group_upstream = pieces
        result, pullback = jax.vjp(forward, group_rows, *weights)
        gradients = pullback(group_upstream)
        totals = tuple((summed + gradient for summed, gradient in zip(totals, gradients[1:])))
        return (totals, (result, gradients[0]))
    initial_totals = tuple((jnp.zeros_like(weight) for weight in weights))
    totals, (results, input_grads) = lax.scan(one_group, initial_totals, (hidden_groups, upstream_groups))
    return (results.reshape(TOKENS, D), input_grads.reshape(TOKENS, D), totals[0], totals[1], totals[2], totals[3], totals[4], totals[5], totals[6], totals[7], totals[8], totals[9], totals[10], totals[11], totals[12], totals[13])
```

```python
import functools

import jax
import jax.numpy as jnp
from jax import lax
from jax.experimental import pallas as pl
from jax.experimental.pallas import tpu as pltpu
from jax.sharding import PartitionSpec as P

HEAD_DIM = 64
STATE = 128
LENGTH = 512
STRIP = 128
WIDTH = 256
GROUP_HEADS = WIDTH // HEAD_DIM
EPSILON = 1e-05
F32 = jnp.float32
BF16 = jnp.bfloat16
MIB = 1 << 20


def dot_nn(left, right):
    return lax.dot_general(left, right, (((1,), (0,)), ((), ())), preferred_element_type=F32)


def dot_nt(left, right):
    return lax.dot_general(left, right, (((1,), (1,)), ((), ())), preferred_element_type=F32)


def dot_tn(left, right):
    return lax.dot_general(left, right, (((0,), (0,)), ((), ())), preferred_element_type=F32)


def split2(value):
    high = value.astype(BF16)
    return high, (value - high.astype(F32)).astype(BF16)


def split3(value):
    high = value.astype(BF16)
    rest = value - high.astype(F32)
    middle = rest.astype(BF16)
    return high, middle, (rest - middle.astype(F32)).astype(BF16)


def dot3(dot, left, right):
    left_high, left_low = split2(left)
    right_high, right_low = split2(right)
    return dot(left_high, right_high) + (dot(left_high, right_low) + dot(left_low, right_high))


def sigmoid(value):
    return 1.0 / (1.0 + jnp.exp(-value))


def softplus(value):
    return jnp.maximum(value, 0.0) + jnp.log1p(jnp.exp(-jnp.abs(value)))


def triangular(rows, keep_lower):
    down = lax.broadcasted_iota(jnp.int32, (rows, rows), 0)
    along = lax.broadcasted_iota(jnp.int32, (rows, rows), 1)
    return down >= along if keep_lower else down <= along


def running_sum(value, keep_lower):
    high, middle, low = split3(value)
    packed = (
        high.astype(F32)
        + pltpu.roll(middle.astype(F32), 16, 1)
        + pltpu.roll(low.astype(F32), 32, 1)
    ).astype(BF16)
    ones = jnp.where(triangular(value.shape[0], keep_lower), 1.0, 0.0).astype(BF16)
    sums = dot_nn(ones, packed)
    total = sums + pltpu.roll(sums, 128 - 16, 1) + pltpu.roll(sums, 128 - 32, 1)
    lanes = lax.broadcasted_iota(jnp.int32, total.shape, 1)
    return jnp.where(lanes < 16, total, 0.0)


def spread(columns):
    rows = columns.shape[0]
    lanes = lax.broadcasted_iota(jnp.int32, (rows, 128), 1)
    halves = []
    for pair in range(GROUP_HEADS // 2):
        first = jnp.broadcast_to(columns[:, 2 * pair : 2 * pair + 1], (rows, 128))
        second = jnp.broadcast_to(columns[:, 2 * pair + 1 : 2 * pair + 2], (rows, 128))
        halves.append(jnp.where(lanes < HEAD_DIM, first, second))
    return jnp.concatenate(halves, axis=1)


def head_only(value, head):
    lanes = lax.broadcasted_iota(jnp.int32, value.shape, 1)
    return jnp.where((lanes >= head * HEAD_DIM) & (lanes < (head + 1) * HEAD_DIM), value, 0.0).astype(BF16)


def shifted_down(value, by):
    if by == 0:
        return value
    rows = lax.broadcasted_iota(jnp.int32, value.shape, 0)
    return jnp.where(rows >= by, pltpu.roll(value, by, 0), 0.0)


def shifted_up(value, by):
    if by == 0:
        return value
    count = value.shape[0]
    rows = lax.broadcasted_iota(jnp.int32, value.shape, 0)
    return jnp.where(rows < count - by, pltpu.roll(value, count - by, 0), 0.0)


def convolve(value, kernel, offset):
    taps = kernel.shape[0]
    total = offset + kernel[taps - 1 : taps] * value
    for tap in range(taps - 1):
        total = total + kernel[tap : tap + 1] * shifted_down(value, taps - 1 - tap)
    return total


def convolve_back(grad_out, value, kernel):
    taps = kernel.shape[0]
    grad_in = kernel[taps - 1 : taps] * grad_out
    rows = []
    for tap in range(taps):
        by = taps - 1 - tap
        if by:
            grad_in = grad_in + kernel[tap : tap + 1] * shifted_up(grad_out, by)
        rows.append(jnp.sum(grad_out * shifted_down(value, by), axis=0, keepdims=True))
    rows.append(jnp.sum(grad_out, axis=0, keepdims=True))
    rows.append(jnp.zeros((8 - taps - 1, grad_out.shape[1]), F32))
    return grad_in, jnp.concatenate(rows, axis=0)


def forward_kernel(
    hidden_ref, cotangent_ref, norm_ref, gate_in_ref, value_in_ref, state_in_ref, step_in_ref,
    value_kernel_ref, value_offset_ref, state_kernel_ref, state_offset_ref, heads_ref, skip_ref,
    gated_norm_ref, out_weight_ref,
    normed_ref, state_raw_ref, value_raw_ref, gate_raw_ref, mixed_ref, gated_ref, grad_scaled_ref,
    step_pre_ref, log_ref, sums_ref,
    upstream_s, pair_s, steps_s, log_s, log_t_s, squares_s, terms_s,
):
    group = pl.program_id(1)

    @pl.when(group == 0)
    def _():
        rows = hidden_ref[...]
        scale = lax.rsqrt(jnp.mean(rows * rows, axis=-1, keepdims=True) + EPSILON)
        normed = (rows * scale * norm_ref[...]).astype(BF16)
        normed_ref[...] = normed
        upstream_s[...] = cotangent_ref[...].astype(BF16)
        raw = dot_nn(normed, state_in_ref[...])
        state_raw_ref[...] = raw
        pre = convolve(raw, state_kernel_ref[...], state_offset_ref[...])
        conv = pre * sigmoid(pre)
        pair = dot3(dot_nt, conv[:, STATE:], conv[:, :STATE])
        pair_s[...] = jnp.where(triangular(LENGTH, True), pair, 0.0)
        step_pre = dot_nn(normed, step_in_ref[...]) + heads_ref[0:1, :]
        step_pre_ref[...] = step_pre
        lanes = lax.broadcasted_iota(jnp.int32, step_pre.shape, 1)
        steps = jnp.where(lanes < 12, softplus(step_pre), 0.0)
        log = running_sum(steps * heads_ref[1:2, :], True)
        log_ref[...] = log
        transposed = log.T
        for g in range(steps_s.shape[0]):
            back = (128 - GROUP_HEADS * g) % 128
            steps_s[g] = pltpu.roll(steps, back, 1) if back else steps
            log_s[g] = pltpu.roll(log, back, 1) if back else log
            log_t_s[g] = transposed[GROUP_HEADS * g : GROUP_HEADS * g + 8]
        squares_s[...] = jnp.zeros_like(squares_s)
        terms_s[...] = jnp.zeros_like(terms_s)

    normed = normed_ref[...]
    raw = dot_nn(normed, value_in_ref[...])
    value_raw_ref[...] = raw
    pre = convolve(raw, value_kernel_ref[...], value_offset_ref[...])
    values = pre * sigmoid(pre)
    weighted = values * spread(steps_s[group])
    parts = [head_only(weighted, head) for head in range(GROUP_HEADS)]
    log = log_s[group]
    log_t = log_t_s[group]
    strips = []
    for strip in range(LENGTH // STRIP):
        low, high = strip * STRIP, (strip + 1) * STRIP
        pair = pair_s[low:high, :high]
        weights = []
        for head in range(GROUP_HEADS):
            gap = jnp.minimum(log[low:high, head : head + 1] - log_t[head : head + 1, :high], 0.0)
            weights.append((jnp.exp(gap) * pair).astype(BF16))
        strips.append(
            dot_nn(
                jnp.concatenate(weights, axis=1),
                jnp.concatenate([part[:high] for part in parts], axis=0),
            )
        )
    mixed = jnp.concatenate(strips, axis=0) + skip_ref[...] * values
    mixed_ref[...] = mixed
    gate = dot_nn(normed, gate_in_ref[...])
    gate_raw_ref[...] = gate
    gated = mixed * (gate * sigmoid(gate))
    gated_ref[...] = gated
    grad_scaled = dot_nt(upstream_s[...], out_weight_ref[...])
    grad_scaled_ref[...] = grad_scaled
    squares = gated * gated
    terms = grad_scaled * gated_norm_ref[...] * gated
    squares_s[...] += squares[:, :128] + squares[:, 128:]
    terms_s[...] += terms[:, :128] + terms[:, 128:]

    @pl.when(group == pl.num_programs(1) - 1)
    def _():
        lanes = lax.broadcasted_iota(jnp.int32, (LENGTH, 128), 1)
        both = jnp.where(
            lanes == 0,
            jnp.sum(squares_s[...], axis=1, keepdims=True),
            jnp.where(lanes == 1, jnp.sum(terms_s[...], axis=1, keepdims=True), 0.0),
        )
        sums_ref[...] = both.T[:8]


def const_spec(shape):
    return pl.BlockSpec(shape, lambda *_: (0,) * len(shape))


def run_forward(hidden, cotangent, norm, gate_in, value_in, state_in, step_in, value_kernel, value_offset,
                state_kernel, state_offset, heads, skip, gated_norm, out_weight):
    tokens, width = hidden.shape
    channels = gate_in.shape[1]
    groups = channels // WIDTH
    sequences = tokens // LENGTH
    row = lambda s, g: (s, 0)
    block = lambda s, g: (s, g)
    column = lambda s, g: (0, g)
    wide = jax.ShapeDtypeStruct((tokens, channels), F32)
    narrow = jax.ShapeDtypeStruct((tokens, 128), F32)
    wide_spec = pl.BlockSpec((LENGTH, WIDTH), block)
    narrow_spec = pl.BlockSpec((LENGTH, 128), row)
    return pl.pallas_call(
        forward_kernel,
        grid=(sequences, groups),
        in_specs=[
            pl.BlockSpec((LENGTH, width), row),
            pl.BlockSpec((LENGTH, width), row),
            const_spec((1, width)),
            pl.BlockSpec((width, WIDTH), column),
            pl.BlockSpec((width, WIDTH), column),
            const_spec((width, 2 * STATE)),
            const_spec((width, 128)),
            pl.BlockSpec((value_kernel.shape[0], WIDTH), column),
            pl.BlockSpec((1, WIDTH), column),
            const_spec(state_kernel.shape),
            const_spec((1, 2 * STATE)),
            const_spec((8, 128)),
            pl.BlockSpec((1, WIDTH), column),
            pl.BlockSpec((1, WIDTH), column),
            pl.BlockSpec((WIDTH, width), lambda s, g: (g, 0)),
        ],
        out_specs=[
            pl.BlockSpec((LENGTH, width), row),
            pl.BlockSpec((LENGTH, 2 * STATE), row),
            wide_spec,
            wide_spec,
            wide_spec,
            wide_spec,
            wide_spec,
            narrow_spec,
            narrow_spec,
            pl.BlockSpec((8, LENGTH), lambda s, g: (0, s)),
        ],
        out_shape=[
            jax.ShapeDtypeStruct((tokens, width), BF16),
            jax.ShapeDtypeStruct((tokens, 2 * STATE), F32),
            wide,
            wide,
            wide,
            wide,
            wide,
            narrow,
            narrow,
            jax.ShapeDtypeStruct((8, tokens), F32),
        ],
        scratch_shapes=[
            pltpu.VMEM((LENGTH, width), BF16),
            pltpu.VMEM((LENGTH, LENGTH), F32),
            pltpu.VMEM((groups, LENGTH, 128), F32),
            pltpu.VMEM((groups, LENGTH, 128), F32),
            pltpu.VMEM((groups, 8, LENGTH), F32),
            pltpu.VMEM((LENGTH, 128), F32),
            pltpu.VMEM((LENGTH, 128), F32),
        ],
        compiler_params=pltpu.CompilerParams(vmem_limit_bytes=56 * MIB),
        name="forward_mix",
    )(hidden, cotangent, norm, gate_in, value_in, state_in, step_in, value_kernel, value_offset,
      state_kernel, state_offset, heads, skip, gated_norm, out_weight)


def row_factors(own_ref, other_ref, inner):
    sums = own_ref[...] + other_ref[...]
    columns = jnp.concatenate([sums, jnp.zeros((120, sums.shape[1]), F32)], axis=0).T
    scale = lax.rsqrt(columns[:, 0:1] / inner + EPSILON)
    return scale, columns[:, 1:2] * (scale * scale * scale) / inner


def out_kernel(inner, gated_ref, cotangent_ref, own_ref, other_ref, gated_norm_ref, scaled_ref, grad_ref):
    scale, _ = row_factors(own_ref, other_ref, inner)
    scaled = (gated_ref[...] * scale * gated_norm_ref[...]).astype(BF16)
    scaled_ref[...] = scaled
    grad = dot_tn(scaled, cotangent_ref[...].astype(BF16))

    @pl.when(pl.program_id(0) == 0)
    def _():
        grad_ref[...] = grad

    @pl.when(pl.program_id(0) != 0)
    def _():
        grad_ref[...] += grad


def run_out(gated, cotangent, own, other, gated_norm, inner):
    tokens, channels = gated.shape
    width = cotangent.shape[1]
    row = lambda s: (s, 0)
    return pl.pallas_call(
        functools.partial(out_kernel, inner),
        grid=(tokens // LENGTH,),
        in_specs=[
            pl.BlockSpec((LENGTH, channels), row),
            pl.BlockSpec((LENGTH, width), row),
            pl.BlockSpec((8, LENGTH), lambda s: (0, s)),
            pl.BlockSpec((8, LENGTH), lambda s: (0, s)),
            const_spec((1, channels)),
        ],
        out_specs=[pl.BlockSpec((LENGTH, channels), row), const_spec((channels, width))],
        out_shape=[
            jax.ShapeDtypeStruct((tokens, channels), BF16),
            jax.ShapeDtypeStruct((channels, width), F32),
        ],
        compiler_params=pltpu.CompilerParams(vmem_limit_bytes=56 * MIB),
        name="grad_out_weight",
    )(gated, cotangent, own, other, gated_norm)


def gate_kernel(
    inner, normed_ref, scaled_ref, gated_ref, mixed_ref, gate_ref, grad_scaled_ref, own_ref, other_ref,
    gated_norm_ref, out_weight_ref,
    grad_mixed_ref, gate_low_ref, partial_ref, grad_ref, grad_norm_ref,
):
    first = pl.program_id(0) == 0
    scale, factor = row_factors(own_ref, other_ref, inner)
    normed = normed_ref[...]
    for group in range(gated_ref.shape[1] // WIDTH):
        columns = slice(group * WIDTH, (group + 1) * WIDTH)
        gated = gated_ref[:, columns]
        gate = gate_ref[:, columns]
        scaled_by = grad_scaled_ref[:, columns] * scale
        norm_rows = jnp.sum(scaled_by * gated, axis=0, keepdims=True)
        grad_gated = scaled_by * gated_norm_ref[:, columns] - gated * factor
        s = sigmoid(gate)
        grad_mixed_ref[:, columns] = grad_gated * (gate * s)
        low = (grad_gated * mixed_ref[:, columns] * (s * (1.0 + gate * (1.0 - s)))).astype(BF16)
        gate_low_ref[:, columns] = low
        grad = dot_tn(normed, low)

        @pl.when(first)
        def _():
            grad_ref[:, columns] = grad
            grad_norm_ref[:, columns] = norm_rows

        @pl.when(jnp.logical_not(first))
        def _():
            grad_ref[:, columns] += grad
            grad_norm_ref[:, columns] += norm_rows

    partial_ref[...] = dot_nn(scaled_ref[...], out_weight_ref[...])


def run_gate(normed, scaled, gated, mixed, gate_raw, grad_scaled, own, other, gated_norm, out_weight, inner):
    tokens, channels = gated.shape
    width = normed.shape[1]
    row = lambda s: (s, 0)
    wide = pl.BlockSpec((LENGTH, channels), row)
    return pl.pallas_call(
        functools.partial(gate_kernel, inner),
        grid=(tokens // LENGTH,),
        in_specs=[
            pl.BlockSpec((LENGTH, width), row),
            wide,
            wide,
            wide,
            wide,
            wide,
            pl.BlockSpec((8, LENGTH), lambda s: (0, s)),
            pl.BlockSpec((8, LENGTH), lambda s: (0, s)),
            const_spec((1, channels)),
            const_spec((channels, width)),
        ],
        out_specs=[
            wide,
            wide,
            pl.BlockSpec((LENGTH, width), row),
            const_spec((width, channels)),
            const_spec((1, channels)),
        ],
        out_shape=[
            jax.ShapeDtypeStruct((tokens, channels), F32),
            jax.ShapeDtypeStruct((tokens, channels), BF16),
            jax.ShapeDtypeStruct((tokens, width), F32),
            jax.ShapeDtypeStruct((width, channels), F32),
            jax.ShapeDtypeStruct((1, channels), F32),
        ],
        compiler_params=pltpu.CompilerParams(vmem_limit_bytes=60 * MIB),
        name="grad_gate",
    )(normed, scaled, gated, mixed, gate_raw, grad_scaled, own, other, gated_norm, out_weight)


def scan_back_kernel(
    normed_ref, state_raw_ref, value_raw_ref, grad_mixed_ref, step_pre_ref, log_ref,
    value_kernel_ref, value_offset_ref, state_kernel_ref, state_offset_ref, heads_ref, skip_ref,
    value_low_ref, step_low_ref, grad_state_ref, grad_value_ref, grad_step_ref, rows_ref, head_rows_ref,
    normed_t_s, conv_s, pair_s, grad_pair_s, steps_s, log_s, log_t_s, row_sums_s, column_sums_s, direct_s,
):
    sequence, group = pl.program_id(0), pl.program_id(1)

    @pl.when(group == 0)
    def _():
        normed_t_s[...] = normed_ref[...].T
        raw = state_raw_ref[...]
        pre = convolve(raw, state_kernel_ref[...], state_offset_ref[...])
        conv = pre * sigmoid(pre)
        conv_s[...] = conv
        pair = dot3(dot_nt, conv[:, :STATE], conv[:, STATE:])
        pair_s[...] = jnp.where(triangular(LENGTH, False), pair, 0.0)
        grad_pair_s[...] = jnp.zeros_like(grad_pair_s)
        step_pre = step_pre_ref[...]
        lanes = lax.broadcasted_iota(jnp.int32, step_pre.shape, 1)
        steps = jnp.where(lanes < 12, softplus(step_pre), 0.0)
        log = log_ref[...]
        transposed = log.T
        for g in range(steps_s.shape[0]):
            back = (128 - GROUP_HEADS * g) % 128
            steps_s[g] = pltpu.roll(steps, back, 1) if back else steps
            log_s[g] = pltpu.roll(log, back, 1) if back else log
            log_t_s[g] = transposed[GROUP_HEADS * g : GROUP_HEADS * g + 8]
        column_sums_s[...] = jnp.zeros_like(column_sums_s)
        direct_s[...] = jnp.zeros_like(direct_s)

    raw = value_raw_ref[...]
    kernel = value_kernel_ref[...]
    pre = convolve(raw, kernel, value_offset_ref[...])
    s = sigmoid(pre)
    values = pre * s
    steps = spread(steps_s[group])
    weighted = values * steps
    grad_mixed = grad_mixed_ref[...]
    grad_low = grad_mixed.astype(BF16)
    weighted_parts = [head_only(weighted, head) for head in range(GROUP_HEADS)]
    grad_parts = [head_only(grad_mixed, head) for head in range(GROUP_HEADS)]
    log = log_s[group]
    log_t = log_t_s[group]
    strips = []
    columns = []
    row_sums = [jnp.zeros((1, LENGTH), F32) for _ in range(GROUP_HEADS)]
    for strip in range(LENGTH // STRIP):
        low, high = strip * STRIP, (strip + 1) * STRIP
        pair = pair_s[low:high, low:]
        total = None
        products = []
        sums = []
        for head in range(GROUP_HEADS):
            gap = jnp.minimum(log_t[head : head + 1, low:] - log[low:high, head : head + 1], 0.0)
            decay = jnp.exp(gap)
            weight = decay * pair
            products.append(weight.astype(BF16))
            grad_weight = dot_nt(weighted_parts[head][low:high], grad_low[low:])
            grad_pair = grad_weight * decay
            total = grad_pair if total is None else total + grad_pair
            both = grad_weight * weight
            sums.append(jnp.sum(both, axis=1, keepdims=True))
            along = jnp.sum(both, axis=0, keepdims=True)
            if low:
                along = jnp.concatenate([jnp.zeros((1, low), F32), along], axis=1)
            row_sums[head] = row_sums[head] + along
        grad_pair_s[low:high, low:] += total
        columns.append(sums)
        strips.append(
            dot_nn(
                jnp.concatenate(products, axis=1),
                jnp.concatenate([part[low:] for part in grad_parts], axis=0),
            )
        )
    reached = jnp.concatenate(strips, axis=0)
    row_sums_s[group] = jnp.concatenate(row_sums + [jnp.zeros((8 - GROUP_HEADS, LENGTH), F32)], axis=0)
    lanes = lax.broadcasted_iota(jnp.int32, (LENGTH, 128), 1)
    place = group * GROUP_HEADS
    column_sums = jnp.zeros((LENGTH, 128), F32)
    for head in range(GROUP_HEADS):
        one = jnp.concatenate([sums[head] for sums in columns], axis=0)
        column_sums = jnp.where(lanes == place + head, one, column_sums)
    column_sums_s[...] += column_sums
    down = lax.broadcasted_iota(jnp.int32, (WIDTH, 128), 0)
    across = lax.broadcasted_iota(jnp.int32, (WIDTH, 128), 1)
    start = (across - place) * HEAD_DIM
    picks = jnp.where((down >= start) & (down < start + HEAD_DIM), 1.0, 0.0).astype(BF16)
    direct_high, direct_low = split2(values * reached)
    direct_s[...] += dot_nn(direct_high, picks) + dot_nn(direct_low, picks)

    grad_values = steps * reached + skip_ref[...] * grad_mixed
    grad_pre = grad_values * (s * (1.0 + pre * (1.0 - s)))
    grad_raw, rows = convolve_back(grad_pre, raw, kernel)
    rows = jnp.concatenate([rows[:5], jnp.sum(grad_mixed * values, axis=0, keepdims=True), rows[6:]], axis=0)
    value_low = grad_raw.astype(BF16)
    value_low_ref[...] = value_low
    grad_value = dot_nn(normed_t_s[...], value_low)

    @pl.when(sequence == 0)
    def _():
        grad_value_ref[group] = grad_value
        rows_ref[group] = rows

    @pl.when(sequence != 0)
    def _():
        grad_value_ref[group] += grad_value
        rows_ref[group] += rows

    @pl.when(group == pl.num_programs(1) - 1)
    def _():
        conv = conv_s[...]
        grad_pair = jnp.where(triangular(LENGTH, False), grad_pair_s[...], 0.0)
        grad_write = dot3(dot_nn, grad_pair, conv[:, STATE:])
        grad_read = dot3(dot_tn, grad_pair, conv[:, :STATE])
        grad_state_ref[...] = jnp.concatenate([grad_write, grad_read], axis=1)
        groups = row_sums_s.shape[0]
        row_sums = jnp.concatenate(
            [row_sums_s[g, :GROUP_HEADS] for g in range(groups)]
            + [jnp.zeros((128 - GROUP_HEADS * groups, LENGTH), F32)],
            axis=0,
        ).T
        memory = running_sum(row_sums - column_sums_s[...], False)
        step_pre = step_pre_ref[...]
        rate = heads_ref[1:2, :]
        grad_steps = direct_s[...] + rate * memory
        grad_raw = grad_steps * sigmoid(step_pre)
        grad_raw = jnp.where(lanes < 12, grad_raw, 0.0)
        step_low = grad_raw.astype(BF16)
        step_low_ref[...] = step_low
        grad_step = dot_nn(normed_t_s[...], step_low)
        decay_row = rate * jnp.sum(jnp.where(lanes < 12, softplus(step_pre), 0.0) * memory, axis=0, keepdims=True)
        head_rows = jnp.concatenate(
            [jnp.sum(grad_raw, axis=0, keepdims=True), decay_row, jnp.zeros((6, 128), F32)], axis=0
        )

        @pl.when(sequence == 0)
        def _():
            grad_step_ref[...] = grad_step
            head_rows_ref[...] = head_rows

        @pl.when(sequence != 0)
        def _():
            grad_step_ref[...] += grad_step
            head_rows_ref[...] += head_rows


def run_scan_back(normed, state_raw, value_raw, grad_mixed, step_pre, log, value_kernel, value_offset,
                  state_kernel, state_offset, heads, skip):
    tokens, width = normed.shape
    channels = value_raw.shape[1]
    groups = channels // WIDTH
    row = lambda s, g: (s, 0)
    block = lambda s, g: (s, g)
    column = lambda s, g: (0, g)
    return pl.pallas_call(
        scan_back_kernel,
        grid=(tokens // LENGTH, groups),
        in_specs=[
            pl.BlockSpec((LENGTH, width), row),
            pl.BlockSpec((LENGTH, 2 * STATE), row),
            pl.BlockSpec((LENGTH, WIDTH), block),
            pl.BlockSpec((LENGTH, WIDTH), block),
            pl.BlockSpec((LENGTH, 128), row),
            pl.BlockSpec((LENGTH, 128), row),
            pl.BlockSpec((value_kernel.shape[0], WIDTH), column),
            pl.BlockSpec((1, WIDTH), column),
            const_spec(state_kernel.shape),
            const_spec((1, 2 * STATE)),
            const_spec((8, 128)),
            pl.BlockSpec((1, WIDTH), column),
        ],
        out_specs=[
            pl.BlockSpec((LENGTH, WIDTH), block),
            pl.BlockSpec((LENGTH, 128), row),
            pl.BlockSpec((LENGTH, 2 * STATE), row),
            const_spec((groups, width, WIDTH)),
            const_spec((width, 128)),
            const_spec((groups, 8, WIDTH)),
            const_spec((8, 128)),
        ],
        out_shape=[
            jax.ShapeDtypeStruct((tokens, channels), BF16),
            jax.ShapeDtypeStruct((tokens, 128), BF16),
            jax.ShapeDtypeStruct((tokens, 2 * STATE), F32),
            jax.ShapeDtypeStruct((groups, width, WIDTH), F32),
            jax.ShapeDtypeStruct((width, 128), F32),
            jax.ShapeDtypeStruct((groups, 8, WIDTH), F32),
            jax.ShapeDtypeStruct((8, 128), F32),
        ],
        scratch_shapes=[
            pltpu.VMEM((width, LENGTH), BF16),
            pltpu.VMEM((LENGTH, 2 * STATE), F32),
            pltpu.VMEM((LENGTH, LENGTH), F32),
            pltpu.VMEM((LENGTH, LENGTH), F32),
            pltpu.VMEM((groups, LENGTH, 128), F32),
            pltpu.VMEM((groups, LENGTH, 128), F32),
            pltpu.VMEM((groups, 8, LENGTH), F32),
            pltpu.VMEM((groups, 8, LENGTH), F32),
            pltpu.VMEM((LENGTH, 128), F32),
            pltpu.VMEM((LENGTH, 128), F32),
        ],
        compiler_params=pltpu.CompilerParams(vmem_limit_bytes=60 * MIB),
        name="scan_back",
    )(normed, state_raw, value_raw, grad_mixed, step_pre, log, value_kernel, value_offset, state_kernel,
      state_offset, heads, skip)


def in_kernel(
    core_ref, own_ref, other_ref, state_raw_ref, normed_ref, gate_low_ref, value_low_ref, step_low_ref,
    gate_in_ref, value_in_ref, step_in_ref, state_in_ref, kernel_ref, offset_ref,
    partial_ref, grad_ref, rows_ref,
):
    raw = state_raw_ref[...]
    kernel = kernel_ref[...]
    pre = convolve(raw, kernel, offset_ref[...])
    s = sigmoid(pre)
    grad_pre = (own_ref[...] + other_ref[...]) * (s * (1.0 + pre * (1.0 - s)))
    grad_raw, rows = convolve_back(grad_pre, raw, kernel)
    low = grad_raw.astype(BF16)
    grad = dot_tn(normed_ref[...], low)

    @pl.when(pl.program_id(0) == 0)
    def _():
        grad_ref[...] = grad
        rows_ref[...] = rows

    @pl.when(pl.program_id(0) != 0)
    def _():
        grad_ref[...] += grad
        rows_ref[...] += rows

    partial_ref[...] = (
        dot_nt(gate_low_ref[...], gate_in_ref[...])
        + dot_nt(value_low_ref[...], value_in_ref[...])
        + dot_nt(jnp.concatenate([step_low_ref[...], low], axis=1),
                 jnp.concatenate([step_in_ref[...], state_in_ref[...]], axis=1))
    )


def run_in(core, own, other, state_raw, normed, gate_low, value_low, step_low, gate_in, value_in, step_in,
           state_in, state_kernel, state_offset):
    tokens, width = normed.shape
    channels = value_low.shape[1]
    row = lambda s, c: (s, 0)
    half = lambda s, c: (s, c[0])
    mine = lambda s, c: (0, c[0])
    return pl.pallas_call(
        in_kernel,
        grid_spec=pltpu.PrefetchScalarGridSpec(
            num_scalar_prefetch=1,
            grid=(tokens // LENGTH,),
            in_specs=[
                pl.BlockSpec((LENGTH, STATE), half),
                pl.BlockSpec((LENGTH, STATE), row),
                pl.BlockSpec((LENGTH, STATE), half),
                pl.BlockSpec((LENGTH, width), row),
                pl.BlockSpec((LENGTH, channels), row),
                pl.BlockSpec((LENGTH, channels), row),
                pl.BlockSpec((LENGTH, 128), row),
                const_spec((width, channels)),
                const_spec((width, channels)),
                const_spec((width, 128)),
                pl.BlockSpec((width, STATE), mine),
                pl.BlockSpec((state_kernel.shape[0], STATE), mine),
                pl.BlockSpec((1, STATE), mine),
            ],
            out_specs=[
                pl.BlockSpec((LENGTH, width), row),
                const_spec((width, STATE)),
                const_spec((8, STATE)),
            ],
        ),
        out_shape=[
            jax.ShapeDtypeStruct((tokens, width), F32),
            jax.ShapeDtypeStruct((width, STATE), F32),
            jax.ShapeDtypeStruct((8, STATE), F32),
        ],
        compiler_params=pltpu.CompilerParams(vmem_limit_bytes=60 * MIB),
        name="grad_in",
    )(core, own, other, state_raw, normed, gate_low, value_low, step_low, gate_in, value_in, step_in,
      state_in, state_kernel, state_offset)


def last_kernel(hidden_ref, cotangent_ref, own_ref, other_ref, out_own_ref, out_other_ref, norm_ref,
                block_ref, grad_ref, rows_ref):
    rows = hidden_ref[...]
    block_ref[...] = rows + (out_own_ref[...] + out_other_ref[...])
    scale = lax.rsqrt(jnp.mean(rows * rows, axis=-1, keepdims=True) + EPSILON)
    grad = own_ref[...] + other_ref[...]
    product = grad * norm_ref[...]
    terms = jnp.sum(product * rows, axis=-1, keepdims=True)
    grad_ref[...] = (
        cotangent_ref[...] + product * scale - rows * (terms * (scale * scale * scale) / rows.shape[1])
    )
    norm_rows = jnp.sum(grad * rows * scale, axis=0, keepdims=True)

    @pl.when(pl.program_id(0) == 0)
    def _():
        rows_ref[...] = norm_rows

    @pl.when(pl.program_id(0) != 0)
    def _():
        rows_ref[...] += norm_rows


def run_last(hidden, cotangent, own, other, out_own, out_other, norm):
    tokens, width = hidden.shape
    wide = pl.BlockSpec((LENGTH // 2, width), lambda s: (s, 0))
    return pl.pallas_call(
        last_kernel,
        grid=(2 * tokens // LENGTH,),
        in_specs=[wide] * 6 + [const_spec((1, width))],
        out_specs=[wide, wide, const_spec((1, width))],
        out_shape=[
            jax.ShapeDtypeStruct((tokens, width), F32),
            jax.ShapeDtypeStruct((tokens, width), F32),
            jax.ShapeDtypeStruct((1, width), F32),
        ],
        compiler_params=pltpu.CompilerParams(vmem_limit_bytes=56 * MIB),
        name="grad_hidden",
    )(hidden, cotangent, own, other, out_own, out_other, norm)


SWAP = [(0, 1), (1, 0)]


def swap(value):
    return lax.ppermute(value, "tensor", SWAP)


def body(hidden, cotangent, norm_weight, gate_in, value_in, state_in, step_in, value_kernel, value_offset,
         state_kernel, state_offset, step_bias, log_decay, skip_weight, gated_norm, out_weight):
    core = lax.axis_index("tensor")
    tokens, width = hidden.shape
    channels = gate_in.shape[1]
    heads = step_in.shape[1]
    inner = 2 * channels
    norm = norm_weight.reshape(1, width)
    step_in = jnp.pad(step_in, ((0, 0), (0, 128 - heads)))
    head_rows = jnp.stack([step_bias, -jnp.exp(log_decay)])
    head_rows = jnp.pad(head_rows, ((0, 6), (0, 128 - heads)))
    skip = jnp.repeat(skip_weight, HEAD_DIM).reshape(1, channels)
    value_offset = value_offset.reshape(1, channels)
    state_offset = state_offset.reshape(1, 2 * STATE)
    gated_norm = gated_norm.reshape(1, channels)

    (normed, state_raw, value_raw, gate_raw, mixed, gated, grad_scaled, step_pre, log, sums) = run_forward(
        hidden, cotangent, norm, gate_in, value_in, state_in, step_in, value_kernel, value_offset, state_kernel,
        state_offset, head_rows, skip, gated_norm, out_weight,
    )
    other_sums = swap(sums)
    scaled, grad_out_weight = run_out(gated, cotangent, sums, other_sums, gated_norm, inner)
    grad_mixed, gate_low, partial_out, grad_gate_in, grad_gated_norm = run_gate(
        normed, scaled, gated, mixed, gate_raw, grad_scaled, sums, other_sums, gated_norm, out_weight, inner
    )
    other_out = swap(partial_out)
    value_low, step_low, grad_state, grad_value, grad_step_in, value_rows, grad_heads = run_scan_back(
        normed, state_raw, value_raw, grad_mixed, step_pre, log, value_kernel, value_offset, state_kernel,
        state_offset, head_rows, skip,
    )
    outgoing = jnp.where(core == 0, grad_state[:, STATE:], grad_state[:, :STATE])
    other_state = swap(outgoing)
    core_index = core.astype(jnp.int32).reshape(1)
    partial_in, grad_state_in, state_rows = run_in(
        core_index, grad_state, other_state, state_raw, normed, gate_low, value_low, step_low, gate_in, value_in,
        step_in, state_in, state_kernel, state_offset,
    )
    other_in = swap(partial_in)
    block_out, grad_hidden, grad_norm = run_last(
        hidden, cotangent, partial_in, other_in, partial_out, other_out, norm
    )
    (grad_out_weight, grad_gate_in, grad_value, grad_state_in, grad_step_in, value_rows, state_rows, grad_heads,
     grad_gated_norm, grad_norm) = lax.psum(
        (grad_out_weight, grad_gate_in, grad_value, grad_state_in, grad_step_in, value_rows, state_rows,
         grad_heads, grad_gated_norm, grad_norm), "dp",
    )
    state_all = jnp.concatenate([grad_state_in, state_rows], axis=0)
    state_other = swap(state_all)
    state_all = jnp.where(
        core == 0,
        jnp.concatenate([state_all, state_other], axis=1),
        jnp.concatenate([state_other, state_all], axis=1),
    )
    grad_value_in = jnp.concatenate([grad_value[g] for g in range(grad_value.shape[0])], axis=1)
    value_rows = jnp.concatenate([value_rows[g] for g in range(value_rows.shape[0])], axis=1)
    taps = value_kernel.shape[0]
    return (
        block_out,
        grad_hidden,
        grad_norm.reshape(width),
        grad_gate_in,
        grad_value_in,
        state_all[:width],
        grad_step_in[:, :heads],
        value_rows[:taps],
        value_rows[taps],
        state_all[width : width + taps],
        state_all[width + taps],
        grad_heads[0, :heads],
        grad_heads[1, :heads],
        value_rows[taps + 1].reshape(heads, HEAD_DIM).sum(axis=1),
        grad_gated_norm.reshape(channels),
        grad_out_weight,
    )


def solution(mesh):
    in_specs = (
        P("dp", None),
        P("dp", None),
        P(),
        P(None, "tensor"),
        P(None, "tensor"),
        P(),
        P(None, "tensor"),
        P(None, "tensor"),
        P("tensor"),
        P(),
        P(),
        P("tensor"),
        P("tensor"),
        P("tensor"),
        P("tensor"),
        P("tensor", None),
    )
    out_specs = (
        P("dp", None),
        P("dp", None),
        P(),
        P(None, "tensor"),
        P(None, "tensor"),
        P(),
        P(None, "tensor"),
        P(None, "tensor"),
        P("tensor"),
        P(),
        P(),
        P("tensor"),
        P("tensor"),
        P("tensor"),
        P("tensor"),
        P("tensor", None),
    )
    return jax.shard_map(body, mesh=mesh, in_specs=in_specs, out_specs=out_specs, check_vma=False)
```

```python
import functools

import jax
import jax.numpy as jnp
from jax import lax
from jax.experimental import pallas as pl
from jax.experimental.pallas import tpu as pltpu
from jax.sharding import PartitionSpec as P

HEAD_DIM = 64
STATE = 128
LENGTH = 512
STRIP = 128
WIDTH = 256
GROUP_HEADS = WIDTH // HEAD_DIM
EPSILON = 1e-05
F32 = jnp.float32
BF16 = jnp.bfloat16
MIB = 1 << 20
TAPS = 4
NORM, OFFSET, GAIN, SKIP, KERNEL = range(5)


def dot_nn(left, right):
    return lax.dot_general(left, right, (((1,), (0,)), ((), ())), preferred_element_type=F32)


def dot_nt(left, right):
    return lax.dot_general(left, right, (((1,), (1,)), ((), ())), preferred_element_type=F32)


def dot_tn(left, right):
    return lax.dot_general(left, right, (((0,), (0,)), ((), ())), preferred_element_type=F32)


def split2(value):
    high = value.astype(BF16)
    return high, (value - high.astype(F32)).astype(BF16)


def split3(value):
    high = value.astype(BF16)
    rest = value - high.astype(F32)
    middle = rest.astype(BF16)
    return high, middle, (rest - middle.astype(F32)).astype(BF16)


def dot3(dot, left, right):
    left_high, left_low = split2(left)
    right_high, right_low = split2(right)
    return dot(left_high, right_high) + (dot(left_high, right_low) + dot(left_low, right_high))


def sigmoid(value):
    return 1.0 / (1.0 + jnp.exp(-value))


def softplus(value):
    return jnp.maximum(value, 0.0) + jnp.log1p(jnp.exp(-jnp.abs(value)))


def triangular(rows, keep_lower):
    down = lax.broadcasted_iota(jnp.int32, (rows, rows), 0)
    along = lax.broadcasted_iota(jnp.int32, (rows, rows), 1)
    return down >= along if keep_lower else down <= along


def running_sum(value, keep_lower):
    high, middle, low = split3(value)
    packed = (
        high.astype(F32)
        + pltpu.roll(middle.astype(F32), 16, 1)
        + pltpu.roll(low.astype(F32), 32, 1)
    ).astype(BF16)
    ones = jnp.where(triangular(value.shape[0], keep_lower), 1.0, 0.0).astype(BF16)
    sums = dot_nn(ones, packed)
    total = sums + pltpu.roll(sums, 128 - 16, 1) + pltpu.roll(sums, 128 - 32, 1)
    lanes = lax.broadcasted_iota(jnp.int32, total.shape, 1)
    return jnp.where(lanes < 16, total, 0.0)


def spread(columns):
    rows = columns.shape[0]
    lanes = lax.broadcasted_iota(jnp.int32, (rows, 128), 1)
    halves = []
    for pair in range(GROUP_HEADS // 2):
        first = jnp.broadcast_to(columns[:, 2 * pair : 2 * pair + 1], (rows, 128))
        second = jnp.broadcast_to(columns[:, 2 * pair + 1 : 2 * pair + 2], (rows, 128))
        halves.append(jnp.where(lanes < HEAD_DIM, first, second))
    return jnp.concatenate(halves, axis=1)


def head_only(value, head):
    lanes = lax.broadcasted_iota(jnp.int32, value.shape, 1)
    return jnp.where((lanes >= head * HEAD_DIM) & (lanes < (head + 1) * HEAD_DIM), value, 0.0).astype(BF16)


def shifted_down(value, by):
    if by == 0:
        return value
    rows = lax.broadcasted_iota(jnp.int32, value.shape, 0)
    return jnp.where(rows >= by, pltpu.roll(value, by, 0), 0.0)


def shifted_up(value, by):
    if by == 0:
        return value
    count = value.shape[0]
    rows = lax.broadcasted_iota(jnp.int32, value.shape, 0)
    return jnp.where(rows < count - by, pltpu.roll(value, count - by, 0), 0.0)


def convolve(value, kernel, offset):
    taps = kernel.shape[0]
    total = offset + kernel[taps - 1 : taps] * value
    for tap in range(taps - 1):
        total = total + kernel[tap : tap + 1] * shifted_down(value, taps - 1 - tap)
    return total


def convolve_back(grad_out, value, kernel):
    taps = kernel.shape[0]
    grad_in = kernel[taps - 1 : taps] * grad_out
    rows = []
    for tap in range(taps):
        by = taps - 1 - tap
        if by:
            grad_in = grad_in + kernel[tap : tap + 1] * shifted_up(grad_out, by)
        rows.append(jnp.sum(grad_out * shifted_down(value, by), axis=0, keepdims=True))
    rows.append(jnp.sum(grad_out, axis=0, keepdims=True))
    rows.append(jnp.zeros((8 - taps - 1, grad_out.shape[1]), F32))
    return grad_in, jnp.concatenate(rows, axis=0)


def forward_kernel(
    hidden_ref, cotangent_ref, norm_ref, vectors_ref, state_vectors_ref, heads_ref, gate_in_ref, value_in_ref,
    state_in_ref, step_in_ref, out_weight_ref,
    normed_ref, state_raw_ref, conv_ref, pair_t_ref, value_raw_ref, gate_raw_ref, mixed_ref, gated_ref,
    grad_scaled_ref, step_pre_ref, steps_ref, log_ref, sums_ref,
    upstream_s, pair_s, steps_s, log_s, log_t_s, squares_s, terms_s,
):
    group = pl.program_id(1)

    @pl.when(group == 0)
    def _():
        rows = hidden_ref[...]
        scale = lax.rsqrt(jnp.mean(rows * rows, axis=-1, keepdims=True) + EPSILON)
        normed = (rows * scale * norm_ref[NORM : NORM + 1, :]).astype(BF16)
        normed_ref[...] = normed
        upstream_s[...] = cotangent_ref[...].astype(BF16)
        raw = dot_nn(normed, state_in_ref[...])
        state_raw_ref[...] = raw
        pre = convolve(raw, state_vectors_ref[:TAPS, :], state_vectors_ref[TAPS : TAPS + 1, :])
        conv = pre * sigmoid(pre)
        conv_ref[...] = conv
        pair = dot3(dot_nt, conv[:, STATE:], conv[:, :STATE])
        pair_s[...] = jnp.where(triangular(LENGTH, True), pair, 0.0)
        pair = dot3(dot_nt, conv[:, :STATE], conv[:, STATE:])
        pair_t_ref[...] = jnp.where(triangular(LENGTH, False), pair, 0.0)
        step_pre = dot_nt(normed, step_in_ref[...]) + heads_ref[0:1, :]
        step_pre_ref[...] = step_pre
        lanes = lax.broadcasted_iota(jnp.int32, step_pre.shape, 1)
        steps = jnp.where(lanes < 12, softplus(step_pre), 0.0)
        steps_ref[...] = steps
        log = running_sum(steps * heads_ref[1:2, :], True)
        log_ref[...] = log
        transposed = log.T
        for g in range(steps_s.shape[0]):
            back = (128 - GROUP_HEADS * g) % 128
            steps_s[g] = pltpu.roll(steps, back, 1) if back else steps
            log_s[g] = pltpu.roll(log, back, 1) if back else log
            log_t_s[g] = transposed[GROUP_HEADS * g : GROUP_HEADS * g + 8]
        squares_s[...] = jnp.zeros_like(squares_s)
        terms_s[...] = jnp.zeros_like(terms_s)

    normed = normed_ref[...]
    raw = dot_nn(normed, value_in_ref[...])
    value_raw_ref[...] = raw
    pre = convolve(raw, vectors_ref[KERNEL : KERNEL + TAPS, :], vectors_ref[OFFSET : OFFSET + 1, :])
    values = pre * sigmoid(pre)
    weighted = values * spread(steps_s[group])
    parts = [head_only(weighted, head) for head in range(GROUP_HEADS)]
    log = log_s[group]
    log_t = log_t_s[group]
    strips = []
    for strip in range(LENGTH // STRIP):
        low, high = strip * STRIP, (strip + 1) * STRIP
        pair = pair_s[low:high, :high]
        weights = []
        for head in range(GROUP_HEADS):
            gap = jnp.minimum(log[low:high, head : head + 1] - log_t[head : head + 1, :high], 0.0)
            weights.append((jnp.exp(gap) * pair).astype(BF16))
        strips.append(
            dot_nn(
                jnp.concatenate(weights, axis=1),
                jnp.concatenate([part[:high] for part in parts], axis=0),
            )
        )
    mixed = jnp.concatenate(strips, axis=0) + vectors_ref[SKIP : SKIP + 1, :] * values
    mixed_ref[...] = mixed
    gate = dot_nn(normed, gate_in_ref[...])
    gate_raw_ref[...] = gate
    gated = mixed * (gate * sigmoid(gate))
    gated_ref[...] = gated
    grad_scaled = dot_nt(upstream_s[...], out_weight_ref[...])
    grad_scaled_ref[...] = grad_scaled
    squares = gated * gated
    terms = grad_scaled * vectors_ref[GAIN : GAIN + 1, :] * gated
    squares_s[...] += squares[:, :128] + squares[:, 128:]
    terms_s[...] += terms[:, :128] + terms[:, 128:]

    @pl.when(group == pl.num_programs(1) - 1)
    def _():
        lanes = lax.broadcasted_iota(jnp.int32, (LENGTH, 128), 1)
        both = jnp.where(
            lanes == 0,
            jnp.sum(squares_s[...], axis=1, keepdims=True),
            jnp.where(lanes == 1, jnp.sum(terms_s[...], axis=1, keepdims=True), 0.0),
        )
        sums_ref[...] = both.T[:8]


def cost(micros):
    return pl.CostEstimate(
        flops=int(micros * 3.0e9), transcendentals=0, bytes_accessed=int(micros * 9.0e6)
    )


def const_spec(shape):
    return pl.BlockSpec(shape, lambda *_: (0,) * len(shape))


def shape_of(*dims, dtype=F32):
    return jax.ShapeDtypeStruct(dims, dtype)


def bit_orders(count):
    bits = count.bit_length() - 1
    return list(range(bits)), list(range(1, bits)) + [0]


def cut_shapes(rows, columns):
    return [shape_of(rows // 2, columns)] * 2


def cut_into(source, bits, outs):
    half = source.shape[0] // 2
    outs[0][...] = source[pl.ds(pl.multiple_of((1 - bits[0]) * half, 8), half), :]
    outs[1][...] = source[pl.ds(pl.multiple_of(bits[0] * half, 8), half), :]


def sum_kernel(step, bits, keep_ref, came_ref, send_ref, next_ref):
    half = keep_ref.shape[0] // 2
    other = pl.ds(pl.multiple_of((1 - bits[step]) * half, 8), half)
    mine = pl.ds(pl.multiple_of(bits[step] * half, 8), half)
    send_ref[...] = keep_ref[other, :] + came_ref[other, :]
    next_ref[...] = keep_ref[mine, :] + came_ref[mine, :]


def join_last(bits, own, came, out, start, rows, offset=0):
    out[pl.ds(pl.multiple_of(start + bits[0] * rows, 8), rows), :] = own[offset : offset + rows, :]
    out[pl.ds(pl.multiple_of(start + (1 - bits[0]) * rows, 8), rows), :] = came[offset : offset + rows, :]


def total_kernel(bits, keep_ref, came_ref, out_ref):
    out_ref[...] = keep_ref[...] + came_ref[...]


def join_kernel(step, bits, own_ref, came_ref, out_ref):
    half = own_ref.shape[0]
    out_ref[pl.ds(pl.multiple_of(bits[step] * half, 8), half), :] = own_ref[...]
    out_ref[pl.ds(pl.multiple_of((1 - bits[step]) * half, 8), half), :] = came_ref[...]


def small_call(kernel, scalars, arrays, out_shape, name):
    return pl.pallas_call(
        kernel,
        grid_spec=pltpu.PrefetchScalarGridSpec(
            num_scalar_prefetch=1,
            grid=(1,),
            in_specs=[const_spec(a.shape) for a in arrays],
            out_specs=[const_spec(s.shape) for s in out_shape],
        ),
        out_shape=out_shape,
        compiler_params=pltpu.CompilerParams(vmem_limit_bytes=40 * MIB),
        cost_estimate=cost(0.1),
        name=name,
    )(scalars, *arrays)


def tie(value, *after):
    return lax.optimization_barrier((value, *after))[0]


class Reduction:
    def __init__(self, pieces, bits, count, name):
        self.sent, self.held = pieces
        self.bits, self.count, self.name = bits, count, name
        self.orders = bit_orders(count)
        self.steps = len(self.orders[0])
        self.step = 0
        self.send(0)

    def send(self, step):
        pairs = [
            (2 * i + core, 2 * (i ^ (1 << self.orders[core][step])) + core)
            for i in range(self.count) for core in range(2)
        ]
        self.came = lax.ppermute(self.sent, ("dp", "tensor"), pairs)

    def advance(self, *after):
        if self.step == 2 * self.steps - 1:
            return self.held
        self.step += 1
        steps, step = self.steps, self.step
        held = tie(self.held, *after) if after else self.held
        rows, columns = held.shape
        if step < steps:
            self.sent, self.held = small_call(
                functools.partial(sum_kernel, step), self.bits, [held, self.came],
                [shape_of(rows // 2, columns)] * 2, self.name + "_sum",
            )
            self.send(step)
        elif step == steps:
            (self.held,) = small_call(
                total_kernel, self.bits, [held, self.came], [shape_of(rows, columns)], self.name + "_total"
            )
            self.sent = self.held
            self.send(steps - 1)
        else:
            back = 2 * steps - step
            (self.held,) = small_call(
                functools.partial(join_kernel, back), self.bits, [held, self.came],
                [shape_of(2 * rows, columns)], self.name + "_join",
            )
            self.sent = self.held
            self.send(back - 1)
        return self.held

    def halves(self):
        while self.step < 2 * self.steps - 1:
            self.advance()
        return self.held, self.came


class PlainReduction:
    def __init__(self, pieces, bits, count, name):
        self.sent, self.held = lax.psum(tuple(pieces), "dp")

    def advance(self, *after):
        return self.held

    def halves(self):
        return self.held, self.sent


def run_forward(hidden, cotangent, vectors, state_vectors, heads, gate_in, value_in, state_in, step_in, out_weight):
    tokens, width = hidden.shape
    channels = gate_in.shape[1]
    groups = channels // WIDTH
    sequences = tokens // LENGTH
    row = lambda s, g: (s, 0)
    block = lambda s, g: (s, g)
    column = lambda s, g: (0, g)
    wide = shape_of(tokens, channels)
    narrow = shape_of(tokens, 128)
    wide_spec = pl.BlockSpec((LENGTH, WIDTH), block)
    narrow_spec = pl.BlockSpec((LENGTH, 128), row)
    return pl.pallas_call(
        forward_kernel,
        grid=(sequences, groups),
        in_specs=[
            pl.BlockSpec((LENGTH, width), row),
            pl.BlockSpec((LENGTH, width), row),
            const_spec((8, width)),
            pl.BlockSpec((8, WIDTH), column),
            const_spec((8, 2 * STATE)),
            const_spec((8, 128)),
            pl.BlockSpec((width, WIDTH), column),
            pl.BlockSpec((width, WIDTH), column),
            const_spec((width, 2 * STATE)),
            const_spec((128, width)),
            pl.BlockSpec((WIDTH, width), lambda s, g: (g, 0)),
        ],
        out_specs=[
            pl.BlockSpec((LENGTH, width), row),
            pl.BlockSpec((LENGTH, 2 * STATE), row),
            pl.BlockSpec((LENGTH, 2 * STATE), row),
            pl.BlockSpec((LENGTH, LENGTH), row),
            wide_spec,
            wide_spec,
            wide_spec,
            wide_spec,
            wide_spec,
            narrow_spec,
            narrow_spec,
            narrow_spec,
            pl.BlockSpec((8, LENGTH), lambda s, g: (0, s)),
        ],
        out_shape=[
            shape_of(tokens, width, dtype=BF16),
            shape_of(tokens, 2 * STATE),
            shape_of(tokens, 2 * STATE),
            shape_of(tokens, LENGTH),
            wide,
            wide,
            wide,
            wide,
            wide,
            narrow,
            narrow,
            narrow,
            shape_of(8, tokens),
        ],
        scratch_shapes=[
            pltpu.VMEM((LENGTH, width), BF16),
            pltpu.VMEM((LENGTH, LENGTH), F32),
            pltpu.VMEM((groups, LENGTH, 128), F32),
            pltpu.VMEM((groups, LENGTH, 128), F32),
            pltpu.VMEM((groups, 8, LENGTH), F32),
            pltpu.VMEM((LENGTH, 128), F32),
            pltpu.VMEM((LENGTH, 128), F32),
        ],
        compiler_params=pltpu.CompilerParams(vmem_limit_bytes=56 * MIB),
        cost_estimate=cost(45),
        name="forward_mix",
    )(hidden, cotangent, vectors, vectors, state_vectors, heads, gate_in, value_in, state_in, step_in, out_weight)


def row_factors(own_ref, other_ref, inner):
    sums = own_ref[...] + other_ref[...]
    columns = jnp.concatenate([sums, jnp.zeros((120, sums.shape[1]), F32)], axis=0).T
    scale = lax.rsqrt(columns[:, 0:1] / inner + EPSILON)
    return scale, columns[:, 1:2] * (scale * scale * scale) / inner


def along_rows(column):
    return jnp.broadcast_to(column, (column.shape[0], 128)).T[:8]


def norm_back_kernel(
    inner, digits, normed_ref, gated_ref, mixed_ref, gate_ref, grad_scaled_ref, cotangent_ref, own_ref, other_ref,
    vectors_ref, gate_in_ref, out_weight_ref,
    grad_mixed_ref, gate_low_ref, partial_ref, grad_norm_ref, norm_rows_ref, send_ref, keep_ref, out_s, gate_s,
):
    @pl.when(pl.program_id(0) == 0)
    def _():
        out_s[...] = jnp.zeros_like(out_s)
        gate_s[...] = jnp.zeros_like(gate_s)
        grad_norm_ref[...] = jnp.zeros_like(grad_norm_ref)

    scale, factor = row_factors(own_ref, other_ref, inner)
    normed_t = normed_ref[...].T
    upstream = cotangent_ref[...].astype(BF16)
    partial = None
    for group in range(gated_ref.shape[1] // WIDTH):
        columns = slice(group * WIDTH, (group + 1) * WIDTH)
        gated = gated_ref[:, columns]
        gate = gate_ref[:, columns]
        gain = vectors_ref[GAIN : GAIN + 1, columns]
        scaled = (gated * scale * gain).astype(BF16)
        out_s[columns, :] += dot_tn(scaled, upstream)
        product = dot_nn(scaled, out_weight_ref[columns, :])
        partial = product if partial is None else partial + product
        scaled_by = grad_scaled_ref[:, columns] * scale
        grad_norm_ref[:, columns] += jnp.broadcast_to(
            jnp.sum(scaled_by * gated, axis=0, keepdims=True), (8, WIDTH)
        )
        grad_gated = scaled_by * gain - gated * factor
        s = sigmoid(gate)
        grad_mixed_ref[:, columns] = grad_gated * (gate * s)
        low = (grad_gated * mixed_ref[:, columns] * (s * (1.0 + gate * (1.0 - s)))).astype(BF16)
        gate_low_ref[:, columns] = low
        gate_s[:, columns] += dot_nn(normed_t, low)
    partial_ref[...] = partial

    @pl.when(pl.program_id(0) == pl.num_programs(0) - 1)
    def _():
        half = gate_s.shape[0] // 2
        other = pl.ds(pl.multiple_of((1 - digits[0]) * half, 8), half)
        mine = pl.ds(pl.multiple_of(digits[0] * half, 8), half)
        for k, source in enumerate((out_s, gate_s)):
            send_ref[k * half : (k + 1) * half, :] = source[other, :]
            keep_ref[k * half : (k + 1) * half, :] = source[mine, :]
        norm_rows_ref[...] = along_rows(
            jnp.sum(gate_s[...] * gate_in_ref[...].astype(F32), axis=1, keepdims=True)
        )


def run_norm_back(digits, normed, gated, mixed, gate_raw, grad_scaled, cotangent, own, other, vectors, gate_in,
                  out_weight, inner):
    tokens, channels = gated.shape
    width = normed.shape[1]
    row = lambda s, _: (s, 0)
    wide = pl.BlockSpec((LENGTH, channels), row)
    rows = (width + channels) // 2
    return pl.pallas_call(
        functools.partial(norm_back_kernel, inner),
        grid_spec=pltpu.PrefetchScalarGridSpec(
            num_scalar_prefetch=1,
            grid=(tokens // LENGTH,),
            in_specs=[
                pl.BlockSpec((LENGTH, width), row),
                wide,
                wide,
                wide,
                wide,
                pl.BlockSpec((LENGTH, width), row),
                pl.BlockSpec((8, LENGTH), lambda s, _: (0, s)),
                pl.BlockSpec((8, LENGTH), lambda s, _: (0, s)),
                const_spec((8, channels)),
                const_spec((width, channels)),
                const_spec((channels, width)),
            ],
            out_specs=[
                wide,
                wide,
                pl.BlockSpec((LENGTH, width), row),
                const_spec((8, channels)),
                const_spec((8, width)),
                const_spec((rows, width)),
                const_spec((rows, width)),
            ],
            scratch_shapes=[pltpu.VMEM((channels, width), F32), pltpu.VMEM((width, channels), F32)],
        ),
        out_shape=[
            shape_of(tokens, channels),
            shape_of(tokens, channels, dtype=BF16),
            shape_of(tokens, width),
            shape_of(8, channels),
            shape_of(8, width),
            shape_of(rows, width),
            shape_of(rows, width),
        ],
        compiler_params=pltpu.CompilerParams(vmem_limit_bytes=60 * MIB),
        cost_estimate=cost(26),
        name="norm_back",
    )(digits, normed, gated, mixed, gate_raw, grad_scaled, cotangent, own, other, vectors, gate_in, out_weight)


def scan_back_kernel(
    group, groups, digits, normed_ref, pair_ref, value_raw_ref, grad_mixed_ref, steps_ref, log_ref, vectors_ref,
    value_in_ref, *refs,
):
    first, last = group == 0, group == groups - 1
    refs = list(refs)
    take = lambda count: [refs.pop(0) for _ in range(count)]
    if not first:
        _, grad_pair_before = take(2)
    if group == 1:
        (value_before,) = take(1)
    if last:
        conv_ref, step_pre_ref, heads_ref, step_in_ref = take(4)
        rows_before, columns_before, direct_before = take(group), take(group), take(group)
    (value_low_ref,) = take(1)
    if not last:
        grad_pair_ref, row_sums_ref, column_sums_ref, direct_ref = take(4)
    value_outs = take(2 if group == 1 else 1)
    rows_ref, norm_rows_ref = take(2)
    if last:
        step_low_ref, mine_ref, other_ref, grad_step_ref, head_rows_ref = take(5)
    grad_value_s, grad_pair_s = take(2)
    sequence = pl.program_id(0)

    @pl.when(sequence == 0)
    def _():
        grad_value_s[...] = jnp.zeros_like(grad_value_s)
        rows_ref[...] = jnp.zeros_like(rows_ref)
        if last:
            grad_step_ref[...] = jnp.zeros_like(grad_step_ref)
            head_rows_ref[...] = jnp.zeros_like(head_rows_ref)

    place = group * GROUP_HEADS
    back = (128 - place) % 128
    group_steps, log = steps_ref[...], log_ref[...]
    log_t = log.T[place : place + GROUP_HEADS]
    if back:
        group_steps, log = pltpu.roll(group_steps, back, 1), pltpu.roll(log, back, 1)
    raw = value_raw_ref[...]
    kernel = vectors_ref[KERNEL : KERNEL + TAPS, :]
    pre = convolve(raw, kernel, vectors_ref[OFFSET : OFFSET + 1, :])
    s = sigmoid(pre)
    values = pre * s
    steps = spread(group_steps)
    weighted = values * steps
    grad_mixed = grad_mixed_ref[...]
    grad_low = grad_mixed.astype(BF16)
    weighted_parts = [head_only(weighted, head) for head in range(GROUP_HEADS)]
    grad_parts = [head_only(grad_mixed, head) for head in range(GROUP_HEADS)]
    strips = []
    columns = []
    row_sums = [jnp.zeros((1, LENGTH), F32) for _ in range(GROUP_HEADS)]
    for strip in range(LENGTH // STRIP):
        low, high = strip * STRIP, (strip + 1) * STRIP
        pair = pair_ref[low:high, low:]
        total = None
        products = []
        sums = []
        for head in range(GROUP_HEADS):
            gap = jnp.minimum(log_t[head : head + 1, low:] - log[low:high, head : head + 1], 0.0)
            decay = jnp.exp(gap)
            weight = decay * pair
            products.append(weight.astype(BF16))
            grad_weight = dot_nt(weighted_parts[head][low:high], grad_low[low:])
            grad_pair = grad_weight * decay
            total = grad_pair if total is None else total + grad_pair
            both = grad_weight * weight
            sums.append(jnp.sum(both, axis=1, keepdims=True))
            along = jnp.sum(both, axis=0, keepdims=True)
            if low:
                along = jnp.concatenate([jnp.zeros((1, low), F32), along], axis=1)
            row_sums[head] = row_sums[head] + along
        if not first:
            total = total + grad_pair_before[low:high, low:]
        if last:
            grad_pair_s[low:high, low:] = total
        else:
            grad_pair_ref[low:high, low:] = total
        columns.append(sums)
        strips.append(
            dot_nn(
                jnp.concatenate(products, axis=1),
                jnp.concatenate([part[low:] for part in grad_parts], axis=0),
            )
        )
    reached = jnp.concatenate(strips, axis=0)
    lanes = lax.broadcasted_iota(jnp.int32, (LENGTH, 128), 1)
    column_sums = jnp.zeros((LENGTH, 128), F32)
    for head in range(GROUP_HEADS):
        one = jnp.concatenate([sums[head] for sums in columns], axis=0)
        column_sums = jnp.where(lanes == place + head, one, column_sums)
    down = lax.broadcasted_iota(jnp.int32, (WIDTH, 128), 0)
    across = lax.broadcasted_iota(jnp.int32, (WIDTH, 128), 1)
    start = (across - place) * HEAD_DIM
    picks = jnp.where((down >= start) & (down < start + HEAD_DIM), 1.0, 0.0).astype(BF16)
    direct_high, direct_low = split2(values * reached)
    direct = dot_nn(direct_high, picks) + dot_nn(direct_low, picks)

    grad_values = steps * reached + vectors_ref[SKIP : SKIP + 1, :] * grad_mixed
    grad_pre = grad_values * (s * (1.0 + pre * (1.0 - s)))
    grad_raw, rows = convolve_back(grad_pre, raw, kernel)
    skip_rows = jnp.sum(grad_mixed * values, axis=0, keepdims=True)
    rows_ref[...] += jnp.concatenate([rows[: TAPS + 1], skip_rows, rows[TAPS + 2 :]], axis=0)
    value_low = grad_raw.astype(BF16)
    value_low_ref[...] = value_low
    grad_value_s[...] += dot_tn(value_low, normed_ref[...])

    if not last:
        row_sums_ref[...] = jnp.concatenate(row_sums + [jnp.zeros((8 - GROUP_HEADS, LENGTH), F32)], axis=0)
        column_sums_ref[...] = column_sums
        direct_ref[...] = direct
    else:
        conv = conv_ref[...]
        grad_pair = jnp.where(triangular(LENGTH, False), grad_pair_s[...], 0.0)
        grad_write = dot3(dot_nn, grad_pair, conv[:, STATE:])
        grad_read = dot3(dot_tn, grad_pair, conv[:, :STATE])
        core = digits[digits.shape[0] - 1]
        mine_ref[...] = jnp.where(core == 0, grad_write, grad_read)
        other_ref[...] = jnp.where(core == 0, grad_read, grad_write)
        for before in columns_before:
            column_sums = column_sums + before[...]
        for before in direct_before:
            direct = direct + before[...]
        row_sums = jnp.concatenate(
            [before[:GROUP_HEADS, :] for before in rows_before]
            + row_sums
            + [jnp.zeros((128 - GROUP_HEADS * groups, LENGTH), F32)],
            axis=0,
        ).T
        memory = running_sum(row_sums - column_sums, False)
        step_pre = step_pre_ref[...]
        rate = heads_ref[1:2, :]
        grad_raw = jnp.where(lanes < 12, (direct + rate * memory) * sigmoid(step_pre), 0.0)
        step_low = grad_raw.astype(BF16)
        step_low_ref[...] = step_low
        grad_step_ref[...] += dot_tn(step_low, normed_ref[...])[:16]
        decay_row = rate * jnp.sum(steps_ref[...] * memory, axis=0, keepdims=True)
        head_rows_ref[...] += jnp.concatenate(
            [jnp.sum(grad_raw, axis=0, keepdims=True), decay_row, jnp.zeros((6, 128), F32)], axis=0
        )

    @pl.when(sequence == pl.num_programs(0) - 1)
    def _():
        grad_value = grad_value_s[...].T
        norm_column = jnp.sum(grad_value * value_in_ref[...].astype(F32), axis=1, keepdims=True)
        norm_rows = along_rows(norm_column)
        if last:
            product = grad_step_ref[...] * step_in_ref[:16, :].astype(F32)
            norm_rows = norm_rows + jnp.broadcast_to(jnp.sum(product, axis=0, keepdims=True), norm_rows.shape)
        norm_rows_ref[...] = norm_rows
        if group == 1:
            send_ref, keep_ref = value_outs
            half = send_ref.shape[0]
            other = pl.ds(pl.multiple_of((1 - digits[0]) * half, 8), half)
            mine = pl.ds(pl.multiple_of(digits[0] * half, 8), half)
            send_ref[:, :WIDTH] = value_before[other, :]
            keep_ref[:, :WIDTH] = value_before[mine, :]
            low, high = grad_value[:half], grad_value[half:]
            send_ref[:, WIDTH:] = jnp.where(digits[0] == 0, high, low)
            keep_ref[:, WIDTH:] = jnp.where(digits[0] == 0, low, high)
        else:
            value_outs[0][...] = grad_value


def run_scan_back(group, groups, digits, normed, pair, value_raw, grad_mixed, steps, log, vectors, value_in,
                  value_low, grad_pair, first_value, extra):
    tokens, width = normed.shape
    channels = value_raw.shape[1]
    first, last = group == 0, group == groups - 1
    row = lambda s, _: (s, 0)
    block = lambda s, _: (s, group)
    column = lambda s, _: (0, group)
    along = lambda s, _: (0, s)
    whole_row = lambda array: pl.BlockSpec((LENGTH, array.shape[1]), row)
    narrow = pl.BlockSpec((LENGTH, 128), row)
    sums = pl.BlockSpec((8, LENGTH), along)
    arrays = [normed, pair, value_raw, grad_mixed, steps, log, vectors, value_in]
    in_specs = [
        whole_row(normed),
        whole_row(pair),
        pl.BlockSpec((LENGTH, WIDTH), block),
        pl.BlockSpec((LENGTH, WIDTH), block),
        narrow,
        narrow,
        pl.BlockSpec((8, WIDTH), column),
        pl.BlockSpec((width, WIDTH), column),
    ]
    aliases = {}
    if not first:
        aliases = {1 + len(arrays): 0}
        arrays += [value_low, grad_pair]
        in_specs += [pl.BlockSpec(memory_space=pl.ANY), whole_row(grad_pair)]
    if group == 1:
        arrays.append(first_value)
        in_specs.append(const_spec(first_value.shape))
    if last:
        conv, step_pre, heads, step_in, row_sums, column_sums, direct = extra
        arrays += [conv, step_pre, heads, step_in, *row_sums, *column_sums, *direct]
        in_specs += [whole_row(conv), narrow, const_spec(heads.shape), const_spec(step_in.shape)]
        in_specs += [sums] * group + [narrow] * (2 * group)
    shapes, specs = [shape_of(tokens, channels, dtype=BF16)], [pl.BlockSpec((LENGTH, WIDTH), block)]
    if not last:
        shapes += [shape_of(tokens, LENGTH), shape_of(8, tokens), shape_of(tokens, 128), shape_of(tokens, 128)]
        specs += [pl.BlockSpec((LENGTH, LENGTH), row), sums, narrow, narrow]
    totals = [shape_of(width // 2, 2 * WIDTH)] * 2 if group == 1 else [shape_of(width, WIDTH)]
    totals += [shape_of(8, WIDTH), shape_of(8, width)]
    shapes += totals
    specs += [const_spec(total.shape) for total in totals]
    if last:
        shapes += [shape_of(tokens, 128, dtype=BF16), shape_of(tokens, STATE), shape_of(tokens, STATE)]
        shapes += [shape_of(16, width), shape_of(8, 128)]
        specs += [narrow] * 3 + [const_spec((16, width)), const_spec((8, 128))]
    return pl.pallas_call(
        functools.partial(scan_back_kernel, group, groups),
        grid_spec=pltpu.PrefetchScalarGridSpec(
            num_scalar_prefetch=1,
            grid=(tokens // LENGTH,),
            in_specs=in_specs,
            out_specs=specs,
            scratch_shapes=[pltpu.VMEM((WIDTH, width), F32), pltpu.VMEM((LENGTH, LENGTH), F32)],
        ),
        out_shape=shapes,
        input_output_aliases=aliases,
        compiler_params=pltpu.CompilerParams(vmem_limit_bytes=60 * MIB),
        cost_estimate=cost(22),
        name="scan_back",
    )(digits, *arrays)


PACK_ROWS = 2560
SHARED_ROWS = 824


def pack_plan(width):
    chunks = width // 128
    plan, start = {}, 0
    for name, rows, parts in (
        ("state", width, 1), ("state_rows", 8, 1), ("norm", 8, chunks), ("value", width, WIDTH // 128),
        ("step", 16, chunks), ("value_rows", 8, chunks), ("gain", 8, chunks), ("heads", 8, 1),
    ):
        plan[name] = [(start + part * rows, start + (part + 1) * rows, part * 128) for part in range(parts)]
        start += rows * parts
    assert start == PACK_ROWS
    return plan


def state_kernel(
    digits, mine_ref, came_ref, raw_ref, normed_ref, state_in_ref, vectors_ref, value_ref, step_ref, gain_ref,
    heads_ref, *refs,
):
    refs = list(refs)
    value_rows, norm_rows = refs[:3], refs[3:7]
    low_ref, send_ref, keep_ref, grad_s, rows_s, packed = refs[7:]

    @pl.when(pl.program_id(0) == 0)
    def _():
        grad_s[...] = jnp.zeros_like(grad_s)
        rows_s[...] = jnp.zeros_like(rows_s)

    raw = raw_ref[...]
    kernel = vectors_ref[:TAPS, :]
    pre = convolve(raw, kernel, vectors_ref[TAPS : TAPS + 1, :])
    s = sigmoid(pre)
    grad_pre = (mine_ref[...] + came_ref[...]) * (s * (1.0 + pre * (1.0 - s)))
    grad_raw, rows = convolve_back(grad_pre, raw, kernel)
    low = grad_raw.astype(BF16)
    low_ref[...] = low
    grad_s[...] += dot_tn(low, normed_ref[...])
    rows_s[...] += rows

    @pl.when(pl.program_id(0) == pl.num_programs(0) - 1)
    def _():
        grad = grad_s[...].T
        norm = along_rows(jnp.sum(grad * state_in_ref[...].astype(F32), axis=1, keepdims=True))
        for part in norm_rows:
            norm = norm + part[...]
        sources = {
            "state": grad, "state_rows": rows_s[...], "norm": norm, "value": value_ref[...], "step": step_ref[...],
            "value_rows": jnp.concatenate([part[...] for part in value_rows], axis=1), "gain": gain_ref[...],
            "heads": heads_ref[...],
        }
        for name, parts in pack_plan(normed_ref.shape[1]).items():
            for start, stop, lane in parts:
                packed[start:stop, :] = sources[name][:, lane : lane + 128]
        cut_into(packed, digits, (send_ref, keep_ref))


def run_state(digits, core, mine, came, state_raw, normed, state_in, state_vectors, value, step, gain, heads,
              value_rows, norm_rows):
    tokens, width = normed.shape
    row = lambda s, *_: (s, 0)
    at = digits.shape[0] - 1
    half = lambda s, d: (s, d[at])
    column = lambda s, d: (0, d[at])
    consts = [value, step, gain, heads, *value_rows, *norm_rows]
    return pl.pallas_call(
        state_kernel,
        grid_spec=pltpu.PrefetchScalarGridSpec(
            num_scalar_prefetch=1,
            grid=(tokens // LENGTH,),
            in_specs=[
                pl.BlockSpec((LENGTH, STATE), row),
                pl.BlockSpec((LENGTH, STATE), row),
                pl.BlockSpec((LENGTH, STATE), half),
                pl.BlockSpec((LENGTH, width), row),
                pl.BlockSpec((width, STATE), column),
                pl.BlockSpec((8, STATE), column),
            ]
            + [const_spec(array.shape) for array in consts],
            out_specs=[pl.BlockSpec((LENGTH, STATE), row)] + [const_spec((PACK_ROWS // 2, 128))] * 2,
            scratch_shapes=[
                pltpu.VMEM((STATE, width), F32),
                pltpu.VMEM((8, STATE), F32),
                pltpu.VMEM((PACK_ROWS, 128), F32),
            ],
        ),
        out_shape=[shape_of(tokens, STATE, dtype=BF16)] + cut_shapes(PACK_ROWS, 128),
        compiler_params=pltpu.CompilerParams(vmem_limit_bytes=60 * MIB),
        cost_estimate=cost(8),
        name="state_back",
    )(digits, mine, came, state_raw, normed, state_in, state_vectors, *consts)


def in_kernel(core, gate_low_ref, value_low_ref, step_low_ref, state_low_ref, gate_in_ref, value_in_ref, step_in_ref,
              state_in_ref, partial_ref):
    partial_ref[...] = (
        dot_nt(gate_low_ref[...], gate_in_ref[...])
        + dot_nt(value_low_ref[...], value_in_ref[...])
        + dot_nn(step_low_ref[...], step_in_ref[...])
        + dot_nt(state_low_ref[...], state_in_ref[...])
    )


def run_in(part, parts, core, gate_low, value_low, step_low, state_low, gate_in, value_in, step_in, state_in):
    tokens, channels = gate_low.shape
    width = gate_in.shape[0]
    count = tokens // LENGTH // parts
    row = lambda s, c: (s + part * count, 0)
    return pl.pallas_call(
        in_kernel,
        grid_spec=pltpu.PrefetchScalarGridSpec(
            num_scalar_prefetch=1,
            grid=(count,),
            in_specs=[
                pl.BlockSpec((LENGTH, channels), row),
                pl.BlockSpec((LENGTH, channels), row),
                pl.BlockSpec((LENGTH, 128), row),
                pl.BlockSpec((LENGTH, STATE), row),
                const_spec((width, channels)),
                const_spec((width, channels)),
                const_spec((128, width)),
                pl.BlockSpec((width, STATE), lambda s, c: (0, c[0])),
            ],
            out_specs=pl.BlockSpec((LENGTH, width), lambda s, c: (s, 0)),
        ),
        out_shape=shape_of(count * LENGTH, width),
        compiler_params=pltpu.CompilerParams(vmem_limit_bytes=60 * MIB),
        cost_estimate=cost(7.5),
        name="grad_in",
    )(core, gate_low, value_low, step_low, state_low, gate_in, value_in, step_in, state_in)


def last_kernel(hidden_ref, cotangent_ref, own_ref, other_ref, out_own_ref, out_other_ref, norm_ref, *refs):
    block_ref, grad_ref = refs[-2:]
    rows = hidden_ref[...]
    block_ref[...] = rows + (out_own_ref[...] + out_other_ref[...])
    scale = lax.rsqrt(jnp.mean(rows * rows, axis=-1, keepdims=True) + EPSILON)
    product = (own_ref[...] + other_ref[...]) * norm_ref[NORM : NORM + 1, :]
    terms = jnp.sum(product * rows, axis=-1, keepdims=True)
    grad_ref[...] = (
        cotangent_ref[...] + product * scale - rows * (terms * (scale * scale * scale) / rows.shape[1])
    )


def run_last(part, parts, before, hidden, cotangent, own, other, out_own, out_other, norm):
    tokens, width = hidden.shape
    cycle = parts * own.shape[0] // tokens
    rows = LENGTH // 4
    steps = tokens // rows // parts
    far = pl.BlockSpec((rows, width), lambda s: (s + part * steps, 0))
    near = pl.BlockSpec((rows, width), lambda s: (s + part % cycle * steps, 0))
    return pl.pallas_call(
        last_kernel,
        grid=(steps,),
        in_specs=[far, far, near, near, far, far, const_spec((8, width))]
        + [pl.BlockSpec(memory_space=pl.ANY)] * len(before),
        out_specs=[far, far],
        out_shape=[shape_of(tokens, width), shape_of(tokens, width)],
        input_output_aliases={7 + k: k for k in range(len(before))},
        compiler_params=pltpu.CompilerParams(vmem_limit_bytes=56 * MIB),
        cost_estimate=cost(5.5),
        name="grad_hidden",
    )(hidden, cotangent, own, other, out_own, out_other, norm, *before)


def join_weights_kernel(bits, own_ref, came_ref, out_ref, gate_ref):
    half = own_ref.shape[0] // 2
    join_last(bits, own_ref, came_ref, out_ref, 0, half, 0)
    join_last(bits, own_ref, came_ref, gate_ref, 0, half, half)


def join_small_kernel(bits, own_ref, came_ref, out_ref, shared_ref):
    join_last(bits, own_ref, came_ref, out_ref, 0, own_ref.shape[0])
    shared_ref[...] = out_ref[:SHARED_ROWS, :]


def finish_kernel(digits, own_ref, came_ref, small_ref, other_ref, vectors_ref, value_ref, state_ref, norm_ref,
                  step_ref, kernel_ref, offset_ref, state_kernel_ref, state_offset_ref, bias_ref, decay_ref,
                  skip_ref, gain_ref):
    heads = step_ref.shape[0]
    first = digits[digits.shape[0] - 1] == 0
    width = value_ref.shape[0]
    plan = pack_plan(width)
    half = own_ref.shape[0]
    mine = pl.ds(pl.multiple_of(digits[0] * half, 8), half)
    other = pl.ds(pl.multiple_of((1 - digits[0]) * half, 8), half)
    value_ref[mine, : 2 * WIDTH] = own_ref[...]
    value_ref[other, : 2 * WIDTH] = came_ref[...]
    for start, stop, lane in plan["value"]:
        value_ref[:, 2 * WIDTH + lane : 2 * WIDTH + lane + 128] = small_ref[start:stop, :]
    ((start, stop, _),) = plan["state"]
    here, there = small_ref[start:stop, :], other_ref[start:stop, :]
    state_ref[:, :STATE] = jnp.where(first, here, there)
    state_ref[:, STATE:] = jnp.where(first, there, here)
    ((start, stop, _),) = plan["state_rows"]
    here, there = small_ref[start:stop, :], other_ref[start:stop, :]
    rows = jnp.concatenate([jnp.where(first, here, there), jnp.where(first, there, here)], axis=1)
    state_kernel_ref[...] = rows[:TAPS]
    state_offset_ref[...] = rows[TAPS : TAPS + 1].reshape(2 * STATE)
    whole = lambda name: jnp.concatenate([small_ref[start:stop, :] for start, stop, _ in plan[name]], axis=1)
    norm = whole("norm") + jnp.concatenate([other_ref[start:stop, :] for start, stop, _ in plan["norm"]], axis=1)
    norm_ref[...] = (norm[0:1] / vectors_ref[NORM : NORM + 1, :]).reshape(width)
    step_ref[...] = whole("step")[:heads]
    rows = whole("value_rows")
    kernel_ref[...] = rows[:TAPS]
    offset_ref[...] = rows[TAPS : TAPS + 1].reshape(width)
    gain_ref[...] = whole("gain")[0:1].reshape(width)
    rows_of_heads = whole("heads")
    bias_ref[...] = rows_of_heads[0:1, :heads].reshape(heads)
    decay_ref[...] = rows_of_heads[1:2, :heads].reshape(heads)
    down = lax.broadcasted_iota(jnp.int32, (width, 128), 0)
    begin = lax.broadcasted_iota(jnp.int32, (width, 128), 1) * HEAD_DIM
    picks = jnp.where((down >= begin) & (down < begin + HEAD_DIM), 1.0, 0.0).astype(BF16)
    high, middle, low = split3(rows)
    skip_rows = dot_nn(high, picks) + dot_nn(middle, picks) + dot_nn(low, picks)
    skip_ref[...] = skip_rows[TAPS + 1 : TAPS + 2, :heads].reshape(heads)


def prepare_kernel(
    norm_ref, offset_ref, gain_ref, skip_ref, kernel_ref, state_kernel_ref, state_offset_ref, bias_ref, decay_ref,
    step_ref, vectors_ref, state_vectors_ref, heads_ref, step_rows_ref,
):
    heads = step_ref.shape[0]
    width = norm_ref.shape[0]
    row = lambda ref: ref[...].reshape(1, ref.shape[0])
    vectors_ref[NORM : NORM + 1, :] = row(norm_ref)
    vectors_ref[OFFSET : OFFSET + 1, :] = row(offset_ref)
    vectors_ref[GAIN : GAIN + 1, :] = row(gain_ref)
    vectors_ref[KERNEL : KERNEL + TAPS, :] = kernel_ref[...]
    state_vectors_ref[...] = jnp.zeros_like(state_vectors_ref)
    state_vectors_ref[:TAPS, :] = state_kernel_ref[...]
    state_vectors_ref[TAPS : TAPS + 1, :] = row(state_offset_ref)
    heads_ref[...] = jnp.zeros_like(heads_ref)
    heads_ref[0:1, :heads] = row(bias_ref)
    heads_ref[1:2, :heads] = -jnp.exp(row(decay_ref))
    heads_ref[2:3, :heads] = row(skip_ref)
    lanes = lax.broadcasted_iota(jnp.int32, (128, width), 1)
    start = lax.broadcasted_iota(jnp.int32, (128, width), 0) * HEAD_DIM
    picks = jnp.where((lanes >= start) & (lanes < start + HEAD_DIM), 1.0, 0.0).astype(BF16)
    high, middle, low = split3(heads_ref[...])
    spread_rows = dot_nn(high, picks) + dot_nn(middle, picks) + dot_nn(low, picks)
    vectors_ref[SKIP : SKIP + 1, :] = spread_rows[2:3]
    step_rows_ref[...] = jnp.concatenate(
        [step_ref[...].astype(F32), jnp.zeros((128 - heads, width), F32)], axis=0
    ).astype(BF16)


def run_prepare(*arrays):
    width = arrays[0].shape[0]
    shapes = [shape_of(8, width), shape_of(8, 2 * STATE), shape_of(8, 128), shape_of(128, width, dtype=BF16)]
    return pl.pallas_call(
        prepare_kernel,
        out_shape=shapes,
        cost_estimate=cost(2),
        name="prepare",
    )(*arrays)


SWAP = [(0, 1), (1, 0)]
IN_PARTS = 2
LAST_PARTS = 4


def swap(value):
    return lax.ppermute(value, "tensor", SWAP)


def body(hidden, cotangent, norm_weight, gate_in, value_in, state_in, step_in, value_kernel, value_offset,
         state_kernel, state_offset, step_bias, log_decay, skip_weight, gated_norm, out_weight):
    core = lax.axis_index("tensor").astype(jnp.int32)
    tokens, width = hidden.shape
    channels = gate_in.shape[1]
    heads = step_in.shape[1]
    inner = 2 * channels
    count = lax.axis_size("dp")
    core_index = core.reshape(1)
    if count & (count - 1) == 0 and width % (8 * count) == 0 and PACK_ROWS % (8 * count) == 0:
        reduction = Reduction
        position = lax.axis_index("dp").astype(jnp.int32)
        bits = [
            jnp.where(core == 0, (position >> low) & 1, (position >> high) & 1)
            for low, high in zip(*bit_orders(count), strict=True)
        ]
    else:
        reduction = PlainReduction
        bits = [jnp.int32(0)]
    digits = jnp.stack(bits + [core])
    vectors, state_vectors, head_rows, step_rows = run_prepare(
        norm_weight, value_offset, gated_norm, skip_weight, value_kernel, state_kernel, state_offset, step_bias,
        log_decay, step_in.T,
    )

    (normed, state_raw, conv, pair_t, value_raw, gate_raw, mixed, gated, grad_scaled, step_pre, steps, log, sums) = run_forward(
        hidden, cotangent, vectors, state_vectors, head_rows, gate_in, value_in, state_in, step_rows, out_weight
    )
    grad_mixed, gate_low, partial_out, grad_gain, norm_gate, *pieces = run_norm_back(
        digits, normed, gated, mixed, gate_raw, grad_scaled, cotangent, sums, swap(sums), vectors, gate_in, out_weight, inner
    )
    weights_sum = reduction(pieces, digits, count, "weights")
    other_out = swap(partial_out)
    groups = channels // WIDTH
    value_low = grad_pair = first_value = None
    row_sums, column_sums, direct, value_rows, norm_rows = [], [], [], [], [norm_gate]
    ready = normed
    for group in range(groups):
        last = group == groups - 1
        extra = (conv, step_pre, head_rows, step_rows, row_sums, column_sums, direct) if last else None
        results = list(run_scan_back(
            group, groups, digits, ready, pair_t, value_raw, grad_mixed, steps, log, vectors, value_in, value_low,
            grad_pair, first_value, extra,
        ))
        value_low = results.pop(0)
        if not last:
            grad_pair = results.pop(0)
            for kept in (row_sums, column_sums, direct):
                kept.append(results.pop(0))
        if group == 1:
            pieces = [results.pop(0), results.pop(0)]
            value_sum = reduction(pieces, digits, count, "value")
        else:
            first_value = results.pop(0)
        value_rows.append(results.pop(0))
        norm_rows.append(results.pop(0))
        ready = tie(normed, weights_sum.advance(value_low))
    step_low, mine, outgoing, grad_step, grad_heads = results
    came = swap(tie(outgoing, weights_sum.held, value_sum.advance(value_low)))
    state_low, *pieces = run_state(
        digits, core, mine, came, state_raw, ready, state_in, state_vectors, first_value, grad_step, grad_gain,
        grad_heads, value_rows, norm_rows,
    )
    small_sum = reduction(pieces, digits, count, "small")
    value_sum.advance(state_low)
    weights_sum.advance(state_low)
    partials = []
    for part in range(IN_PARTS):
        low = tie(state_low, value_sum.held, weights_sum.held, small_sum.held)
        partial_in = run_in(
            part, IN_PARTS, core_index, gate_low, value_low, step_low, low, gate_in, value_in, step_rows, state_in
        )
        partials.append((partial_in, swap(partial_in)))
        small_sum.advance(partial_in)
        value_sum.advance(partial_in)
        if part:
            weights_sum.advance(partial_in)
    results = []
    for part in range(LAST_PARTS):
        ready = tie(vectors, value_sum.held, weights_sum.held, small_sum.held)
        results = run_last(
            part, LAST_PARTS, results, hidden, cotangent, *partials[part * IN_PARTS // LAST_PARTS], partial_out,
            other_out, ready,
        )
        small_sum.advance(results[0])
        if part % 2:
            weights_sum.advance(results[0])
        else:
            value_sum.advance(results[0])
    block_out, grad_hidden = results
    grad_out_weight, grad_gate_in = small_call(
        join_weights_kernel, digits, list(weights_sum.halves()), [shape_of(channels, width), shape_of(width, channels)], "weights_last"
    )
    value_halves = value_sum.halves()
    small, shared = small_call(
        join_small_kernel, digits, list(small_sum.halves()), [shape_of(PACK_ROWS, 128), shape_of(SHARED_ROWS, 128)], "small_last"
    )
    (grad_value_in, grad_state_in, grad_norm, grad_step_in, grad_value_kernel, grad_value_offset, grad_state_kernel,
     grad_state_offset, grad_step_bias, grad_log_decay, grad_skip, grad_gain) = small_call(
        finish_kernel, digits, [*value_halves, small, swap(shared), tie(vectors, grad_out_weight)],
        [shape_of(width, channels), shape_of(width, 2 * STATE), shape_of(width), shape_of(heads, width),
         shape_of(TAPS, channels), shape_of(channels), shape_of(TAPS, 2 * STATE), shape_of(2 * STATE),
         shape_of(heads), shape_of(heads), shape_of(heads), shape_of(channels)], "finish",
    )
    return (
        block_out,
        grad_hidden,
        grad_norm,
        grad_gate_in,
        grad_value_in,
        grad_state_in,
        grad_step_in.T,
        grad_value_kernel,
        grad_value_offset,
        grad_state_kernel,
        grad_state_offset,
        grad_step_bias,
        grad_log_decay,
        grad_skip,
        grad_gain,
        grad_out_weight,
    )


def solution(mesh):
    in_specs = (
        P("dp", None),
        P("dp", None),
        P(),
        P(None, "tensor"),
        P(None, "tensor"),
        P(),
        P(None, "tensor"),
        P(None, "tensor"),
        P("tensor"),
        P(),
        P(),
        P("tensor"),
        P("tensor"),
        P("tensor"),
        P("tensor"),
        P("tensor", None),
    )
    out_specs = (
        P("dp", None),
        P("dp", None),
        P(),
        P(None, "tensor"),
        P(None, "tensor"),
        P(),
        P(None, "tensor"),
        P(None, "tensor"),
        P("tensor"),
        P(),
        P(),
        P("tensor"),
        P("tensor"),
        P("tensor"),
        P("tensor"),
        P("tensor", None),
    )
    return jax.shard_map(body, mesh=mesh, in_specs=in_specs, out_specs=out_specs, check_vma=False)
```

```python
import functools

import jax
import jax.numpy as jnp
from jax import lax
from jax.experimental import pallas as pl
from jax.experimental.pallas import tpu as pltpu
from jax.sharding import PartitionSpec as P

HEAD_DIM = 64
STATE = 128
LENGTH = 512
STRIP = 128
WIDTH = 256
GROUP_HEADS = WIDTH // HEAD_DIM
EPSILON = 1e-05
F32 = jnp.float32
BF16 = jnp.bfloat16
MIB = 1 << 20
TAPS = 4
NORM, OFFSET, GAIN, SKIP, KERNEL = range(5)


def dot_nn(left, right):
    return lax.dot_general(left, right, (((1,), (0,)), ((), ())), preferred_element_type=F32)


def dot_nt(left, right):
    return lax.dot_general(left, right, (((1,), (1,)), ((), ())), preferred_element_type=F32)


def dot_tn(left, right):
    return lax.dot_general(left, right, (((0,), (0,)), ((), ())), preferred_element_type=F32)


def split2(value):
    high = value.astype(BF16)
    return high, (value - high.astype(F32)).astype(BF16)


def split3(value):
    high = value.astype(BF16)
    rest = value - high.astype(F32)
    middle = rest.astype(BF16)
    return high, middle, (rest - middle.astype(F32)).astype(BF16)


def dot3(dot, left, right):
    left_high, left_low = split2(left)
    right_high, right_low = split2(right)
    return dot(left_high, right_high) + (dot(left_high, right_low) + dot(left_low, right_high))


def sigmoid(value):
    return 1.0 / (1.0 + jnp.exp(-value))


def softplus(value):
    return jnp.maximum(value, 0.0) + jnp.log1p(jnp.exp(-jnp.abs(value)))


def triangular(rows, keep_lower):
    down = lax.broadcasted_iota(jnp.int32, (rows, rows), 0)
    along = lax.broadcasted_iota(jnp.int32, (rows, rows), 1)
    return down >= along if keep_lower else down <= along


def running_sum(value, keep_lower):
    high, middle, low = split3(value)
    packed = (
        high.astype(F32)
        + pltpu.roll(middle.astype(F32), 16, 1)
        + pltpu.roll(low.astype(F32), 32, 1)
    ).astype(BF16)
    ones = jnp.where(triangular(value.shape[0], keep_lower), 1.0, 0.0).astype(BF16)
    sums = dot_nn(ones, packed)
    total = sums + pltpu.roll(sums, 128 - 16, 1) + pltpu.roll(sums, 128 - 32, 1)
    lanes = lax.broadcasted_iota(jnp.int32, total.shape, 1)
    return jnp.where(lanes < 16, total, 0.0)


def spread(columns):
    rows = columns.shape[0]
    lanes = lax.broadcasted_iota(jnp.int32, (rows, 128), 1)
    halves = []
    for pair in range(GROUP_HEADS // 2):
        first = jnp.broadcast_to(columns[:, 2 * pair : 2 * pair + 1], (rows, 128))
        second = jnp.broadcast_to(columns[:, 2 * pair + 1 : 2 * pair + 2], (rows, 128))
        halves.append(jnp.where(lanes < HEAD_DIM, first, second))
    return jnp.concatenate(halves, axis=1)


def head_only(value, head):
    lanes = lax.broadcasted_iota(jnp.int32, value.shape, 1)
    return jnp.where((lanes >= head * HEAD_DIM) & (lanes < (head + 1) * HEAD_DIM), value, 0.0).astype(BF16)


def shifted_down(value, by):
    if by == 0:
        return value
    rows = lax.broadcasted_iota(jnp.int32, value.shape, 0)
    return jnp.where(rows >= by, pltpu.roll(value, by, 0), 0.0)


def shifted_up(value, by):
    if by == 0:
        return value
    count = value.shape[0]
    rows = lax.broadcasted_iota(jnp.int32, value.shape, 0)
    return jnp.where(rows < count - by, pltpu.roll(value, count - by, 0), 0.0)


def convolve(value, kernel, offset):
    taps = kernel.shape[0]
    total = offset + kernel[taps - 1 : taps] * value
    for tap in range(taps - 1):
        total = total + kernel[tap : tap + 1] * shifted_down(value, taps - 1 - tap)
    return total


def convolve_back(grad_out, value, kernel):
    taps = kernel.shape[0]
    grad_in = kernel[taps - 1 : taps] * grad_out
    rows = []
    for tap in range(taps):
        by = taps - 1 - tap
        if by:
            grad_in = grad_in + kernel[tap : tap + 1] * shifted_up(grad_out, by)
        rows.append(jnp.sum(grad_out * shifted_down(value, by), axis=0, keepdims=True))
    rows.append(jnp.sum(grad_out, axis=0, keepdims=True))
    rows.append(jnp.zeros((8 - taps - 1, grad_out.shape[1]), F32))
    return grad_in, jnp.concatenate(rows, axis=0)


def forward_kernel(
    hidden_ref, cotangent_ref, norm_ref, vectors_ref, state_vectors_ref, heads_ref, gate_in_ref, value_in_ref,
    state_in_ref, step_in_ref, out_weight_ref,
    normed_ref, state_raw_ref, conv_ref, pair_t_ref, value_raw_ref, gate_raw_ref, mixed_ref, gated_ref,
    grad_scaled_ref, step_pre_ref, steps_ref, log_ref, sums_ref,
    upstream_s, pair_s, steps_s, log_s, log_t_s, squares_s, terms_s,
):
    group = pl.program_id(1)

    @pl.when(group == 0)
    def _():
        rows = hidden_ref[...]
        scale = lax.rsqrt(jnp.mean(rows * rows, axis=-1, keepdims=True) + EPSILON)
        normed = (rows * scale * norm_ref[NORM : NORM + 1, :]).astype(BF16)
        normed_ref[...] = normed
        upstream_s[...] = cotangent_ref[...].astype(BF16)
        raw = dot_nn(normed, state_in_ref[...])
        state_raw_ref[...] = raw
        pre = convolve(raw, state_vectors_ref[:TAPS, :], state_vectors_ref[TAPS : TAPS + 1, :])
        conv = pre * sigmoid(pre)
        conv_ref[...] = conv
        pair = dot3(dot_nt, conv[:, STATE:], conv[:, :STATE])
        pair_s[...] = jnp.where(triangular(LENGTH, True), pair, 0.0)
        pair = dot3(dot_nt, conv[:, :STATE], conv[:, STATE:])
        pair_t_ref[...] = jnp.where(triangular(LENGTH, False), pair, 0.0)
        step_pre = dot_nt(normed, step_in_ref[...]) + heads_ref[0:1, :]
        step_pre_ref[...] = step_pre
        lanes = lax.broadcasted_iota(jnp.int32, step_pre.shape, 1)
        steps = jnp.where(lanes < 12, softplus(step_pre), 0.0)
        steps_ref[...] = steps
        log = running_sum(steps * heads_ref[1:2, :], True)
        log_ref[...] = log
        transposed = log.T
        for g in range(steps_s.shape[0]):
            back = (128 - GROUP_HEADS * g) % 128
            steps_s[g] = pltpu.roll(steps, back, 1) if back else steps
            log_s[g] = pltpu.roll(log, back, 1) if back else log
            log_t_s[g] = transposed[GROUP_HEADS * g : GROUP_HEADS * g + 8]
        squares_s[...] = jnp.zeros_like(squares_s)
        terms_s[...] = jnp.zeros_like(terms_s)

    normed = normed_ref[...]
    raw = dot_nn(normed, value_in_ref[...])
    value_raw_ref[...] = raw
    pre = convolve(raw, vectors_ref[KERNEL : KERNEL + TAPS, :], vectors_ref[OFFSET : OFFSET + 1, :])
    values = pre * sigmoid(pre)
    weighted = values * spread(steps_s[group])
    parts = [head_only(weighted, head) for head in range(GROUP_HEADS)]
    log = log_s[group]
    log_t = log_t_s[group]
    strips = []
    for strip in range(LENGTH // STRIP):
        low, high = strip * STRIP, (strip + 1) * STRIP
        pair = pair_s[low:high, :high]
        weights = []
        for head in range(GROUP_HEADS):
            gap = jnp.minimum(log[low:high, head : head + 1] - log_t[head : head + 1, :high], 0.0)
            weights.append((jnp.exp(gap) * pair).astype(BF16))
        strips.append(
            dot_nn(
                jnp.concatenate(weights, axis=1),
                jnp.concatenate([part[:high] for part in parts], axis=0),
            )
        )
    mixed = jnp.concatenate(strips, axis=0) + vectors_ref[SKIP : SKIP + 1, :] * values
    mixed_ref[...] = mixed
    gate = dot_nn(normed, gate_in_ref[...])
    gate_raw_ref[...] = gate
    gated = mixed * (gate * sigmoid(gate))
    gated_ref[...] = gated
    grad_scaled = dot_nt(upstream_s[...], out_weight_ref[...])
    grad_scaled_ref[...] = grad_scaled
    squares = gated * gated
    terms = grad_scaled * vectors_ref[GAIN : GAIN + 1, :] * gated
    squares_s[...] += squares[:, :128] + squares[:, 128:]
    terms_s[...] += terms[:, :128] + terms[:, 128:]

    @pl.when(group == pl.num_programs(1) - 1)
    def _():
        lanes = lax.broadcasted_iota(jnp.int32, (LENGTH, 128), 1)
        both = jnp.where(
            lanes == 0,
            jnp.sum(squares_s[...], axis=1, keepdims=True),
            jnp.where(lanes == 1, jnp.sum(terms_s[...], axis=1, keepdims=True), 0.0),
        )
        sums_ref[...] = both.T[:8]


def cost(micros):
    return pl.CostEstimate(
        flops=int(micros * 7.0e9), transcendentals=0, bytes_accessed=int(micros * 2.1e7)
    )


def const_spec(shape):
    return pl.BlockSpec(shape, lambda *_: (0,) * len(shape))


def shape_of(*dims, dtype=F32):
    return jax.ShapeDtypeStruct(dims, dtype)


def bit_orders(count):
    bits = count.bit_length() - 1
    return list(range(bits)), list(range(1, bits)) + [0]


def cut_shapes(rows, columns):
    return [shape_of(rows // 2, columns)] * 2


def cut_into(source, bits, outs):
    half = source.shape[0] // 2
    outs[0][...] = source[pl.ds(pl.multiple_of((1 - bits[0]) * half, 8), half), :]
    outs[1][...] = source[pl.ds(pl.multiple_of(bits[0] * half, 8), half), :]


def sum_kernel(step, bits, keep_ref, came_ref, send_ref, next_ref):
    half = keep_ref.shape[0] // 2
    other = pl.ds(pl.multiple_of((1 - bits[step]) * half, 8), half)
    mine = pl.ds(pl.multiple_of(bits[step] * half, 8), half)
    send_ref[...] = keep_ref[other, :] + came_ref[other, :]
    next_ref[...] = keep_ref[mine, :] + came_ref[mine, :]


def join_last(bits, own, came, out, start, rows, offset=0):
    out[pl.ds(pl.multiple_of(start + bits[0] * rows, 8), rows), :] = own[offset : offset + rows, :]
    out[pl.ds(pl.multiple_of(start + (1 - bits[0]) * rows, 8), rows), :] = came[offset : offset + rows, :]


def total_kernel(bits, keep_ref, came_ref, out_ref):
    out_ref[...] = keep_ref[...] + came_ref[...]


def join_kernel(step, bits, own_ref, came_ref, out_ref):
    half = own_ref.shape[0]
    out_ref[pl.ds(pl.multiple_of(bits[step] * half, 8), half), :] = own_ref[...]
    out_ref[pl.ds(pl.multiple_of((1 - bits[step]) * half, 8), half), :] = came_ref[...]


def small_call(kernel, scalars, arrays, out_shape, name):
    return pl.pallas_call(
        kernel,
        grid_spec=pltpu.PrefetchScalarGridSpec(
            num_scalar_prefetch=1,
            grid=(1,),
            in_specs=[const_spec(a.shape) for a in arrays],
            out_specs=[const_spec(s.shape) for s in out_shape],
        ),
        out_shape=out_shape,
        compiler_params=pltpu.CompilerParams(vmem_limit_bytes=40 * MIB),
        cost_estimate=cost(0.02),
        name=name,
    )(scalars, *arrays)


def tie(value, *after):
    return lax.optimization_barrier((value, *after))[0]


class Reduction:
    def __init__(self, pieces, bits, count, name):
        self.sent, self.held = pieces
        self.bits, self.count, self.name = bits, count, name
        self.orders = bit_orders(count)
        self.steps = len(self.orders[0])
        self.step = 0
        self.send(0)

    def send(self, step):
        pairs = [
            (2 * i + core, 2 * (i ^ (1 << self.orders[core][step])) + core)
            for i in range(self.count) for core in range(2)
        ]
        self.came = lax.ppermute(self.sent, ("dp", "tensor"), pairs)

    def advance(self, *after):
        if self.step == 2 * self.steps - 1:
            return self.held
        self.step += 1
        steps, step = self.steps, self.step
        held = tie(self.held, *after) if after else self.held
        rows, columns = held.shape
        if step < steps:
            self.sent, self.held = small_call(
                functools.partial(sum_kernel, step), self.bits, [held, self.came],
                [shape_of(rows // 2, columns)] * 2, self.name + "_sum",
            )
            self.send(step)
        elif step == steps:
            (self.held,) = small_call(
                total_kernel, self.bits, [held, self.came], [shape_of(rows, columns)], self.name + "_total"
            )
            self.sent = self.held
            self.send(steps - 1)
        else:
            back = 2 * steps - step
            (self.held,) = small_call(
                functools.partial(join_kernel, back), self.bits, [held, self.came],
                [shape_of(2 * rows, columns)], self.name + "_join",
            )
            self.sent = self.held
            self.send(back - 1)
        return self.held

    def halves(self):
        while self.step < 2 * self.steps - 1:
            self.advance()
        return self.held, self.came


class PlainReduction:
    def __init__(self, pieces, bits, count, name):
        self.sent, self.held = lax.psum(tuple(pieces), "dp")

    def advance(self, *after):
        return self.held

    def halves(self):
        return self.held, self.sent


def run_forward(hidden, cotangent, vectors, state_vectors, heads, gate_in, value_in, state_in, step_in, out_weight):
    tokens, width = hidden.shape
    channels = gate_in.shape[1]
    groups = channels // WIDTH
    sequences = tokens // LENGTH
    row = lambda s, g: (s, 0)
    block = lambda s, g: (s, g)
    column = lambda s, g: (0, g)
    wide = shape_of(tokens, channels)
    narrow = shape_of(tokens, 128)
    wide_spec = pl.BlockSpec((LENGTH, WIDTH), block)
    narrow_spec = pl.BlockSpec((LENGTH, 128), row)
    return pl.pallas_call(
        forward_kernel,
        grid=(sequences, groups),
        in_specs=[
            pl.BlockSpec((LENGTH, width), row),
            pl.BlockSpec((LENGTH, width), row),
            const_spec((8, width)),
            pl.BlockSpec((8, WIDTH), column),
            const_spec((8, 2 * STATE)),
            const_spec((8, 128)),
            pl.BlockSpec((width, WIDTH), column),
            pl.BlockSpec((width, WIDTH), column),
            const_spec((width, 2 * STATE)),
            const_spec((128, width)),
            pl.BlockSpec((WIDTH, width), lambda s, g: (g, 0)),
        ],
        out_specs=[
            pl.BlockSpec((LENGTH, width), row),
            pl.BlockSpec((LENGTH, 2 * STATE), row),
            pl.BlockSpec((LENGTH, 2 * STATE), row),
            pl.BlockSpec((LENGTH, LENGTH), row),
            wide_spec,
            wide_spec,
            wide_spec,
            wide_spec,
            wide_spec,
            narrow_spec,
            narrow_spec,
            narrow_spec,
            pl.BlockSpec((8, LENGTH), lambda s, g: (0, s)),
        ],
        out_shape=[
            shape_of(tokens, width, dtype=BF16),
            shape_of(tokens, 2 * STATE),
            shape_of(tokens, 2 * STATE),
            shape_of(tokens, LENGTH),
            wide,
            wide,
            wide,
            wide,
            wide,
            narrow,
            narrow,
            narrow,
            shape_of(8, tokens),
        ],
        scratch_shapes=[
            pltpu.VMEM((LENGTH, width), BF16),
            pltpu.VMEM((LENGTH, LENGTH), F32),
            pltpu.VMEM((groups, LENGTH, 128), F32),
            pltpu.VMEM((groups, LENGTH, 128), F32),
            pltpu.VMEM((groups, 8, LENGTH), F32),
            pltpu.VMEM((LENGTH, 128), F32),
            pltpu.VMEM((LENGTH, 128), F32),
        ],
        compiler_params=pltpu.CompilerParams(vmem_limit_bytes=56 * MIB),
        cost_estimate=cost(45),
        name="forward_mix",
    )(hidden, cotangent, vectors, vectors, state_vectors, heads, gate_in, value_in, state_in, step_in, out_weight)


def row_factors(own_ref, other_ref, inner):
    sums = own_ref[...] + other_ref[...]
    columns = jnp.concatenate([sums, jnp.zeros((120, sums.shape[1]), F32)], axis=0).T
    scale = lax.rsqrt(columns[:, 0:1] / inner + EPSILON)
    return scale, columns[:, 1:2] * (scale * scale * scale) / inner


def along_rows(column):
    return jnp.broadcast_to(column, (column.shape[0], 128)).T[:8]


def norm_back_kernel(
    inner, digits, normed_ref, gated_ref, mixed_ref, gate_ref, grad_scaled_ref, cotangent_ref, own_ref, other_ref,
    vectors_ref, gate_in_ref, out_weight_ref,
    grad_mixed_ref, gate_low_ref, partial_ref, grad_norm_ref, norm_rows_ref, send_ref, keep_ref, out_s, gate_s,
):
    @pl.when(pl.program_id(0) == 0)
    def _():
        out_s[...] = jnp.zeros_like(out_s)
        gate_s[...] = jnp.zeros_like(gate_s)
        grad_norm_ref[...] = jnp.zeros_like(grad_norm_ref)

    scale, factor = row_factors(own_ref, other_ref, inner)
    normed_t = normed_ref[...].T
    upstream = cotangent_ref[...].astype(BF16)
    partial = None
    for group in range(gated_ref.shape[1] // WIDTH):
        columns = slice(group * WIDTH, (group + 1) * WIDTH)
        gated = gated_ref[:, columns]
        gate = gate_ref[:, columns]
        gain = vectors_ref[GAIN : GAIN + 1, columns]
        scaled = (gated * scale * gain).astype(BF16)
        out_s[columns, :] += dot_tn(scaled, upstream)
        product = dot_nn(scaled, out_weight_ref[columns, :])
        partial = product if partial is None else partial + product
        scaled_by = grad_scaled_ref[:, columns] * scale
        grad_norm_ref[:, columns] += jnp.broadcast_to(
            jnp.sum(scaled_by * gated, axis=0, keepdims=True), (8, WIDTH)
        )
        grad_gated = scaled_by * gain - gated * factor
        s = sigmoid(gate)
        grad_mixed_ref[:, columns] = grad_gated * (gate * s)
        low = (grad_gated * mixed_ref[:, columns] * (s * (1.0 + gate * (1.0 - s)))).astype(BF16)
        gate_low_ref[:, columns] = low
        gate_s[:, columns] += dot_nn(normed_t, low)
    partial_ref[...] = partial

    @pl.when(pl.program_id(0) == pl.num_programs(0) - 1)
    def _():
        half = gate_s.shape[0] // 2
        other = pl.ds(pl.multiple_of((1 - digits[0]) * half, 8), half)
        mine = pl.ds(pl.multiple_of(digits[0] * half, 8), half)
        for k, source in enumerate((out_s, gate_s)):
            send_ref[k * half : (k + 1) * half, :] = source[other, :]
            keep_ref[k * half : (k + 1) * half, :] = source[mine, :]
        norm_rows_ref[...] = along_rows(
            jnp.sum(gate_s[...] * gate_in_ref[...].astype(F32), axis=1, keepdims=True)
        )


def run_norm_back(digits, normed, gated, mixed, gate_raw, grad_scaled, cotangent, own, other, vectors, gate_in,
                  out_weight, inner):
    tokens, channels = gated.shape
    width = normed.shape[1]
    row = lambda s, _: (s, 0)
    wide = pl.BlockSpec((LENGTH, channels), row)
    rows = (width + channels) // 2
    return pl.pallas_call(
        functools.partial(norm_back_kernel, inner),
        grid_spec=pltpu.PrefetchScalarGridSpec(
            num_scalar_prefetch=1,
            grid=(tokens // LENGTH,),
            in_specs=[
                pl.BlockSpec((LENGTH, width), row),
                wide,
                wide,
                wide,
                wide,
                pl.BlockSpec((LENGTH, width), row),
                pl.BlockSpec((8, LENGTH), lambda s, _: (0, s)),
                pl.BlockSpec((8, LENGTH), lambda s, _: (0, s)),
                const_spec((8, channels)),
                const_spec((width, channels)),
                const_spec((channels, width)),
            ],
            out_specs=[
                wide,
                wide,
                pl.BlockSpec((LENGTH, width), row),
                const_spec((8, channels)),
                const_spec((8, width)),
                const_spec((rows, width)),
                const_spec((rows, width)),
            ],
            scratch_shapes=[pltpu.VMEM((channels, width), F32), pltpu.VMEM((width, channels), F32)],
        ),
        out_shape=[
            shape_of(tokens, channels),
            shape_of(tokens, channels, dtype=BF16),
            shape_of(tokens, width),
            shape_of(8, channels),
            shape_of(8, width),
            shape_of(rows, width),
            shape_of(rows, width),
        ],
        compiler_params=pltpu.CompilerParams(vmem_limit_bytes=60 * MIB),
        cost_estimate=cost(26),
        name="norm_back",
    )(digits, normed, gated, mixed, gate_raw, grad_scaled, cotangent, own, other, vectors, gate_in, out_weight)


def scan_back_kernel(
    group, groups, part, parts, digits, normed_ref, pair_ref, value_raw_ref, grad_mixed_ref, steps_ref, log_ref,
    vectors_ref, value_in_ref, *refs,
):
    first, last, final = group == 0, group == groups - 1, part == parts - 1
    refs = list(refs)
    take = lambda count: [refs.pop(0) for _ in range(count)]
    if part or not first:
        take(1)
    if not first:
        (grad_pair_before,) = take(1)
    if group == 1 and final:
        (value_before,) = take(1)
    if last:
        conv_ref, step_pre_ref, heads_ref, step_in_ref = take(4)
        rows_before, columns_before, direct_before = take(group), take(group), take(group)
    if part:
        take(3 if last else 4)
        totals_before = take(4 if last else 2)
    (value_low_ref,) = take(1)
    if last:
        step_low_ref, mine_ref, other_ref = take(3)
    else:
        grad_pair_ref, row_sums_ref, column_sums_ref, direct_ref = take(4)
    (rows_ref,) = take(1)
    if last:
        grad_step_ref, head_rows_ref = take(2)
    if final:
        value_outs = take(2 if group == 1 else 1)
        (norm_rows_ref,) = take(1)
    else:
        (value_total_ref,) = take(1)
    grad_value_s, grad_pair_s = take(2)
    sequence = pl.program_id(0)

    @pl.when(sequence == 0)
    def _():
        totals = [grad_value_s, rows_ref] + ([grad_step_ref, head_rows_ref] if last else [])
        for k, total in enumerate(totals):
            total[...] = totals_before[k][...] if part else jnp.zeros_like(total)

    place = group * GROUP_HEADS
    back = (128 - place) % 128
    group_steps, log = steps_ref[...], log_ref[...]
    log_t = log.T[place : place + GROUP_HEADS]
    if back:
        group_steps, log = pltpu.roll(group_steps, back, 1), pltpu.roll(log, back, 1)
    raw = value_raw_ref[...]
    kernel = vectors_ref[KERNEL : KERNEL + TAPS, :]
    pre = convolve(raw, kernel, vectors_ref[OFFSET : OFFSET + 1, :])
    s = sigmoid(pre)
    values = pre * s
    steps = spread(group_steps)
    weighted = values * steps
    grad_mixed = grad_mixed_ref[...]
    grad_low = grad_mixed.astype(BF16)
    weighted_parts = [head_only(weighted, head) for head in range(GROUP_HEADS)]
    grad_parts = [head_only(grad_mixed, head) for head in range(GROUP_HEADS)]
    strips = []
    columns = []
    row_sums = [jnp.zeros((1, LENGTH), F32) for _ in range(GROUP_HEADS)]
    for strip in range(LENGTH // STRIP):
        low, high = strip * STRIP, (strip + 1) * STRIP
        pair = pair_ref[low:high, low:]
        total = None
        products = []
        sums = []
        for head in range(GROUP_HEADS):
            gap = jnp.minimum(log_t[head : head + 1, low:] - log[low:high, head : head + 1], 0.0)
            decay = jnp.exp(gap)
            weight = decay * pair
            products.append(weight.astype(BF16))
            grad_weight = dot_nt(weighted_parts[head][low:high], grad_low[low:])
            grad_pair = grad_weight * decay
            total = grad_pair if total is None else total + grad_pair
            both = grad_weight * weight
            sums.append(jnp.sum(both, axis=1, keepdims=True))
            along = jnp.sum(both, axis=0, keepdims=True)
            if low:
                along = jnp.concatenate([jnp.zeros((1, low), F32), along], axis=1)
            row_sums[head] = row_sums[head] + along
        if not first:
            total = total + grad_pair_before[low:high, low:]
        if last:
            grad_pair_s[low:high, low:] = total
        else:
            grad_pair_ref[low:high, low:] = total
        columns.append(sums)
        strips.append(
            dot_nn(
                jnp.concatenate(products, axis=1),
                jnp.concatenate([part[low:] for part in grad_parts], axis=0),
            )
        )
    reached = jnp.concatenate(strips, axis=0)
    lanes = lax.broadcasted_iota(jnp.int32, (LENGTH, 128), 1)
    column_sums = jnp.zeros((LENGTH, 128), F32)
    for head in range(GROUP_HEADS):
        one = jnp.concatenate([sums[head] for sums in columns], axis=0)
        column_sums = jnp.where(lanes == place + head, one, column_sums)
    down = lax.broadcasted_iota(jnp.int32, (WIDTH, 128), 0)
    across = lax.broadcasted_iota(jnp.int32, (WIDTH, 128), 1)
    start = (across - place) * HEAD_DIM
    picks = jnp.where((down >= start) & (down < start + HEAD_DIM), 1.0, 0.0).astype(BF16)
    direct_high, direct_low = split2(values * reached)
    direct = dot_nn(direct_high, picks) + dot_nn(direct_low, picks)

    grad_values = steps * reached + vectors_ref[SKIP : SKIP + 1, :] * grad_mixed
    grad_pre = grad_values * (s * (1.0 + pre * (1.0 - s)))
    grad_raw, rows = convolve_back(grad_pre, raw, kernel)
    skip_rows = jnp.sum(grad_mixed * values, axis=0, keepdims=True)
    rows_ref[...] += jnp.concatenate([rows[: TAPS + 1], skip_rows, rows[TAPS + 2 :]], axis=0)
    value_low = grad_raw.astype(BF16)
    value_low_ref[...] = value_low
    grad_value_s[...] += dot_tn(value_low, normed_ref[...])

    if not last:
        row_sums_ref[...] = jnp.concatenate(row_sums + [jnp.zeros((8 - GROUP_HEADS, LENGTH), F32)], axis=0)
        column_sums_ref[...] = column_sums
        direct_ref[...] = direct
    else:
        conv = conv_ref[...]
        grad_pair = jnp.where(triangular(LENGTH, False), grad_pair_s[...], 0.0)
        grad_write = dot3(dot_nn, grad_pair, conv[:, STATE:])
        grad_read = dot3(dot_tn, grad_pair, conv[:, :STATE])
        core = digits[digits.shape[0] - 1]
        mine_ref[...] = jnp.where(core == 0, grad_write, grad_read)
        other_ref[...] = jnp.where(core == 0, grad_read, grad_write)
        for before in columns_before:
            column_sums = column_sums + before[...]
        for before in direct_before:
            direct = direct + before[...]
        row_sums = jnp.concatenate(
            [before[:GROUP_HEADS, :] for before in rows_before]
            + row_sums
            + [jnp.zeros((128 - GROUP_HEADS * groups, LENGTH), F32)],
            axis=0,
        ).T
        memory = running_sum(row_sums - column_sums, False)
        step_pre = step_pre_ref[...]
        rate = heads_ref[1:2, :]
        grad_raw = jnp.where(lanes < 12, (direct + rate * memory) * sigmoid(step_pre), 0.0)
        step_low = grad_raw.astype(BF16)
        step_low_ref[...] = step_low
        grad_step_ref[...] += dot_tn(step_low, normed_ref[...])[:16]
        decay_row = rate * jnp.sum(steps_ref[...] * memory, axis=0, keepdims=True)
        head_rows_ref[...] += jnp.concatenate(
            [jnp.sum(grad_raw, axis=0, keepdims=True), decay_row, jnp.zeros((6, 128), F32)], axis=0
        )

    @pl.when(sequence == pl.num_programs(0) - 1)
    def _():
        if not final:
            value_total_ref[...] = grad_value_s[...]
            return
        grad_value = grad_value_s[...].T
        norm_column = jnp.sum(grad_value * value_in_ref[...].astype(F32), axis=1, keepdims=True)
        norm_rows = along_rows(norm_column)
        if last:
            product = grad_step_ref[...] * step_in_ref[:16, :].astype(F32)
            norm_rows = norm_rows + jnp.broadcast_to(jnp.sum(product, axis=0, keepdims=True), norm_rows.shape)
        norm_rows_ref[...] = norm_rows
        if group == 1:
            send_ref, keep_ref = value_outs
            half = send_ref.shape[0]
            other = pl.ds(pl.multiple_of((1 - digits[0]) * half, 8), half)
            mine = pl.ds(pl.multiple_of(digits[0] * half, 8), half)
            send_ref[:, :WIDTH] = value_before[other, :]
            keep_ref[:, :WIDTH] = value_before[mine, :]
            low, high = grad_value[:half], grad_value[half:]
            send_ref[:, WIDTH:] = jnp.where(digits[0] == 0, high, low)
            keep_ref[:, WIDTH:] = jnp.where(digits[0] == 0, low, high)
        else:
            value_outs[0][...] = grad_value


def run_scan_back(group, groups, part, parts, digits, normed, pair, value_raw, grad_mixed, steps, log, vectors,
                  value_in, value_low, grad_pair, first_value, extra, before):
    tokens, width = normed.shape
    channels = value_raw.shape[1]
    count = tokens // LENGTH // parts
    first, last, final = group == 0, group == groups - 1, part == parts - 1
    row = lambda s, _: (s + part * count, 0)
    block = lambda s, _: (s + part * count, group)
    column = lambda s, _: (0, group)
    along = lambda s, _: (0, s + part * count)
    whole_row = lambda array: pl.BlockSpec((LENGTH, array.shape[1]), row)
    narrow = pl.BlockSpec((LENGTH, 128), row)
    sums = pl.BlockSpec((8, LENGTH), along)
    elsewhere = pl.BlockSpec(memory_space=pl.ANY)
    arrays = [normed, pair, value_raw, grad_mixed, steps, log, vectors, value_in]
    in_specs = [
        whole_row(normed),
        whole_row(pair),
        pl.BlockSpec((LENGTH, WIDTH), block),
        pl.BlockSpec((LENGTH, WIDTH), block),
        narrow,
        narrow,
        pl.BlockSpec((8, WIDTH), column),
        pl.BlockSpec((width, WIDTH), column),
    ]
    aliases = {}
    if part or not first:
        aliases[1 + len(arrays)] = 0
        arrays.append(value_low)
        in_specs.append(elsewhere)
    if not first:
        arrays.append(grad_pair)
        in_specs.append(whole_row(grad_pair))
    if group == 1 and final:
        arrays.append(first_value)
        in_specs.append(const_spec(first_value.shape))
    if last:
        conv, step_pre, heads, step_in, row_sums, column_sums, direct = extra
        arrays += [conv, step_pre, heads, step_in, *row_sums, *column_sums, *direct]
        in_specs += [whole_row(conv), narrow, const_spec(heads.shape), const_spec(step_in.shape)]
        in_specs += [sums] * group + [narrow] * (2 * group)
    if last:
        wholes = [shape_of(tokens, 128, dtype=BF16), shape_of(tokens, STATE), shape_of(tokens, STATE)]
        whole_specs = [narrow] * 3
    else:
        wholes = [shape_of(tokens, LENGTH), shape_of(8, tokens), shape_of(tokens, 128), shape_of(tokens, 128)]
        whole_specs = [pl.BlockSpec((LENGTH, LENGTH), row), sums, narrow, narrow]
    if part:
        for k in range(len(wholes)):
            aliases[1 + len(arrays) + k] = 1 + k
        arrays += before
        in_specs += [elsewhere] * len(wholes) + [const_spec(array.shape) for array in before[len(wholes) :]]
    totals = [shape_of(8, WIDTH)]
    if last:
        totals += [shape_of(16, width), shape_of(8, 128)]
    if not final:
        totals += [shape_of(WIDTH, width)]
    else:
        totals += [shape_of(width // 2, 2 * WIDTH)] * 2 if group == 1 else [shape_of(width, WIDTH)]
        totals += [shape_of(8, width)]
    return pl.pallas_call(
        functools.partial(scan_back_kernel, group, groups, part, parts),
        grid_spec=pltpu.PrefetchScalarGridSpec(
            num_scalar_prefetch=1,
            grid=(count,),
            in_specs=in_specs,
            out_specs=[pl.BlockSpec((LENGTH, WIDTH), block)]
            + whole_specs
            + [const_spec(total.shape) for total in totals],
            scratch_shapes=[pltpu.VMEM((WIDTH, width), F32), pltpu.VMEM((LENGTH, LENGTH), F32)],
        ),
        out_shape=[shape_of(tokens, channels, dtype=BF16)] + wholes + totals,
        input_output_aliases=aliases,
        compiler_params=pltpu.CompilerParams(vmem_limit_bytes=60 * MIB),
        cost_estimate=cost(22 / parts),
        name="scan_back",
    )(digits, *arrays)


PACK_ROWS = 2560
SHARED_ROWS = 824


def pack_plan(width):
    chunks = width // 128
    plan, start = {}, 0
    for name, rows, parts in (
        ("state", width, 1), ("state_rows", 8, 1), ("norm", 8, chunks), ("value", width, WIDTH // 128),
        ("step", 16, chunks), ("value_rows", 8, chunks), ("gain", 8, chunks), ("heads", 8, 1),
    ):
        plan[name] = [(start + part * rows, start + (part + 1) * rows, part * 128) for part in range(parts)]
        start += rows * parts
    assert start == PACK_ROWS
    return plan


def state_kernel(
    digits, mine_ref, came_ref, raw_ref, normed_ref, state_in_ref, vectors_ref, value_ref, step_ref, gain_ref,
    heads_ref, *refs,
):
    refs = list(refs)
    value_rows, norm_rows = refs[:3], refs[3:7]
    low_ref, send_ref, keep_ref, grad_s, rows_s, packed = refs[7:]

    @pl.when(pl.program_id(0) == 0)
    def _():
        grad_s[...] = jnp.zeros_like(grad_s)
        rows_s[...] = jnp.zeros_like(rows_s)

    raw = raw_ref[...]
    kernel = vectors_ref[:TAPS, :]
    pre = convolve(raw, kernel, vectors_ref[TAPS : TAPS + 1, :])
    s = sigmoid(pre)
    grad_pre = (mine_ref[...] + came_ref[...]) * (s * (1.0 + pre * (1.0 - s)))
    grad_raw, rows = convolve_back(grad_pre, raw, kernel)
    low = grad_raw.astype(BF16)
    low_ref[...] = low
    grad_s[...] += dot_tn(low, normed_ref[...])
    rows_s[...] += rows

    @pl.when(pl.program_id(0) == pl.num_programs(0) - 1)
    def _():
        grad = grad_s[...].T
        norm = along_rows(jnp.sum(grad * state_in_ref[...].astype(F32), axis=1, keepdims=True))
        for part in norm_rows:
            norm = norm + part[...]
        sources = {
            "state": grad, "state_rows": rows_s[...], "norm": norm, "value": value_ref[...], "step": step_ref[...],
            "value_rows": jnp.concatenate([part[...] for part in value_rows], axis=1), "gain": gain_ref[...],
            "heads": heads_ref[...],
        }
        for name, parts in pack_plan(normed_ref.shape[1]).items():
            for start, stop, lane in parts:
                packed[start:stop, :] = sources[name][:, lane : lane + 128]
        half = send_ref.shape[0]
        pltpu.sync_copy(packed.at[pl.ds(pl.multiple_of((1 - digits[0]) * half, 8), half), :], send_ref)
        pltpu.sync_copy(packed.at[pl.ds(pl.multiple_of(digits[0] * half, 8), half), :], keep_ref)


def run_state(digits, core, mine, came, state_raw, normed, state_in, state_vectors, value, step, gain, heads,
              value_rows, norm_rows):
    tokens, width = normed.shape
    row = lambda s, *_: (s, 0)
    at = digits.shape[0] - 1
    half = lambda s, d: (s, d[at])
    column = lambda s, d: (0, d[at])
    consts = [value, step, gain, heads, *value_rows, *norm_rows]
    return pl.pallas_call(
        state_kernel,
        grid_spec=pltpu.PrefetchScalarGridSpec(
            num_scalar_prefetch=1,
            grid=(tokens // LENGTH,),
            in_specs=[
                pl.BlockSpec((LENGTH, STATE), row),
                pl.BlockSpec((LENGTH, STATE), row),
                pl.BlockSpec((LENGTH, STATE), half),
                pl.BlockSpec((LENGTH, width), row),
                pl.BlockSpec((width, STATE), column),
                pl.BlockSpec((8, STATE), column),
            ]
            + [const_spec(array.shape) for array in consts],
            out_specs=[pl.BlockSpec((LENGTH, STATE), row)] + [pl.BlockSpec(memory_space=pltpu.HBM)] * 2,
            scratch_shapes=[
                pltpu.VMEM((STATE, width), F32),
                pltpu.VMEM((8, STATE), F32),
                pltpu.VMEM((PACK_ROWS, 128), F32),
            ],
        ),
        out_shape=[shape_of(tokens, STATE, dtype=BF16)] + cut_shapes(PACK_ROWS, 128),
        compiler_params=pltpu.CompilerParams(vmem_limit_bytes=60 * MIB),
        cost_estimate=cost(8),
        name="state_back",
    )(digits, mine, came, state_raw, normed, state_in, state_vectors, *consts)


def in_kernel(core, gate_low_ref, value_low_ref, step_low_ref, state_low_ref, gate_in_ref, value_in_ref, step_in_ref,
              state_in_ref, partial_ref):
    partial_ref[...] = (
        dot_nt(gate_low_ref[...], gate_in_ref[...])
        + dot_nt(value_low_ref[...], value_in_ref[...])
        + dot_nn(step_low_ref[...], step_in_ref[...])
        + dot_nt(state_low_ref[...], state_in_ref[...])
    )


def run_in(part, parts, core, gate_low, value_low, step_low, state_low, gate_in, value_in, step_in, state_in):
    tokens, channels = gate_low.shape
    width = gate_in.shape[0]
    count = tokens // LENGTH // parts
    row = lambda s, c: (s + part * count, 0)
    return pl.pallas_call(
        in_kernel,
        grid_spec=pltpu.PrefetchScalarGridSpec(
            num_scalar_prefetch=1,
            grid=(count,),
            in_specs=[
                pl.BlockSpec((LENGTH, channels), row),
                pl.BlockSpec((LENGTH, channels), row),
                pl.BlockSpec((LENGTH, 128), row),
                pl.BlockSpec((LENGTH, STATE), row),
                const_spec((width, channels)),
                const_spec((width, channels)),
                const_spec((128, width)),
                pl.BlockSpec((width, STATE), lambda s, c: (0, c[0])),
            ],
            out_specs=pl.BlockSpec((LENGTH, width), lambda s, c: (s, 0)),
        ),
        out_shape=shape_of(count * LENGTH, width),
        compiler_params=pltpu.CompilerParams(vmem_limit_bytes=60 * MIB),
        cost_estimate=cost(7.5),
        name="grad_in",
    )(core, gate_low, value_low, step_low, state_low, gate_in, value_in, step_in, state_in)


def last_kernel(hidden_ref, cotangent_ref, own_ref, other_ref, out_own_ref, out_other_ref, norm_ref, *refs):
    block_ref, grad_ref = refs[-2:]
    rows = hidden_ref[...]
    block_ref[...] = rows + (out_own_ref[...] + out_other_ref[...])
    scale = lax.rsqrt(jnp.mean(rows * rows, axis=-1, keepdims=True) + EPSILON)
    product = (own_ref[...] + other_ref[...]) * norm_ref[NORM : NORM + 1, :]
    terms = jnp.sum(product * rows, axis=-1, keepdims=True)
    grad_ref[...] = (
        cotangent_ref[...] + product * scale - rows * (terms * (scale * scale * scale) / rows.shape[1])
    )


def run_last(part, parts, before, hidden, cotangent, own, other, out_own, out_other, norm):
    tokens, width = hidden.shape
    cycle = parts * own.shape[0] // tokens
    rows = LENGTH // 4
    steps = tokens // rows // parts
    far = pl.BlockSpec((rows, width), lambda s: (s + part * steps, 0))
    near = pl.BlockSpec((rows, width), lambda s: (s + part % cycle * steps, 0))
    return pl.pallas_call(
        last_kernel,
        grid=(steps,),
        in_specs=[far, far, near, near, far, far, const_spec((8, width))]
        + [pl.BlockSpec(memory_space=pl.ANY)] * len(before),
        out_specs=[far, far],
        out_shape=[shape_of(tokens, width), shape_of(tokens, width)],
        input_output_aliases={7 + k: k for k in range(len(before))},
        compiler_params=pltpu.CompilerParams(vmem_limit_bytes=56 * MIB),
        cost_estimate=cost(5.5),
        name="grad_hidden",
    )(hidden, cotangent, own, other, out_own, out_other, norm, *before)


def join_weights_kernel(bits, own_ref, came_ref, out_ref, gate_ref):
    half = own_ref.shape[0] // 2
    join_last(bits, own_ref, came_ref, out_ref, 0, half, 0)
    join_last(bits, own_ref, came_ref, gate_ref, 0, half, half)


def join_small_kernel(bits, own_ref, came_ref, out_ref, shared_ref):
    join_last(bits, own_ref, came_ref, out_ref, 0, own_ref.shape[0])
    shared_ref[...] = out_ref[:SHARED_ROWS, :]


def finish_kernel(digits, own_ref, came_ref, small_ref, other_ref, vectors_ref, value_ref, state_ref, norm_ref,
                  step_ref, kernel_ref, offset_ref, state_kernel_ref, state_offset_ref, bias_ref, decay_ref,
                  skip_ref, gain_ref):
    heads = step_ref.shape[0]
    first = digits[digits.shape[0] - 1] == 0
    width = value_ref.shape[0]
    plan = pack_plan(width)
    half = own_ref.shape[0]
    mine = pl.ds(pl.multiple_of(digits[0] * half, 8), half)
    other = pl.ds(pl.multiple_of((1 - digits[0]) * half, 8), half)
    value_ref[mine, : 2 * WIDTH] = own_ref[...]
    value_ref[other, : 2 * WIDTH] = came_ref[...]
    for start, stop, lane in plan["value"]:
        value_ref[:, 2 * WIDTH + lane : 2 * WIDTH + lane + 128] = small_ref[start:stop, :]
    ((start, stop, _),) = plan["state"]
    here, there = small_ref[start:stop, :], other_ref[start:stop, :]
    state_ref[:, :STATE] = jnp.where(first, here, there)
    state_ref[:, STATE:] = jnp.where(first, there, here)
    ((start, stop, _),) = plan["state_rows"]
    here, there = small_ref[start:stop, :], other_ref[start:stop, :]
    rows = jnp.concatenate([jnp.where(first, here, there), jnp.where(first, there, here)], axis=1)
    state_kernel_ref[...] = rows[:TAPS]
    state_offset_ref[...] = rows[TAPS : TAPS + 1].reshape(2 * STATE)
    whole = lambda name: jnp.concatenate([small_ref[start:stop, :] for start, stop, _ in plan[name]], axis=1)
    norm = whole("norm") + jnp.concatenate([other_ref[start:stop, :] for start, stop, _ in plan["norm"]], axis=1)
    norm_ref[...] = (norm[0:1] / vectors_ref[NORM : NORM + 1, :]).reshape(width)
    step_ref[...] = whole("step")[:heads]
    rows = whole("value_rows")
    kernel_ref[...] = rows[:TAPS]
    offset_ref[...] = rows[TAPS : TAPS + 1].reshape(width)
    gain_ref[...] = whole("gain")[0:1].reshape(width)
    rows_of_heads = whole("heads")
    bias_ref[...] = rows_of_heads[0:1, :heads].reshape(heads)
    decay_ref[...] = rows_of_heads[1:2, :heads].reshape(heads)
    down = lax.broadcasted_iota(jnp.int32, (width, 128), 0)
    begin = lax.broadcasted_iota(jnp.int32, (width, 128), 1) * HEAD_DIM
    picks = jnp.where((down >= begin) & (down < begin + HEAD_DIM), 1.0, 0.0).astype(BF16)
    high, middle, low = split3(rows)
    skip_rows = dot_nn(high, picks) + dot_nn(middle, picks) + dot_nn(low, picks)
    skip_ref[...] = skip_rows[TAPS + 1 : TAPS + 2, :heads].reshape(heads)


def prepare_kernel(
    norm_ref, offset_ref, gain_ref, skip_ref, kernel_ref, state_kernel_ref, state_offset_ref, bias_ref, decay_ref,
    step_ref, vectors_ref, state_vectors_ref, heads_ref, step_rows_ref,
):
    heads = step_ref.shape[0]
    width = norm_ref.shape[0]
    row = lambda ref: ref[...].reshape(1, ref.shape[0])
    vectors_ref[NORM : NORM + 1, :] = row(norm_ref)
    vectors_ref[OFFSET : OFFSET + 1, :] = row(offset_ref)
    vectors_ref[GAIN : GAIN + 1, :] = row(gain_ref)
    vectors_ref[KERNEL : KERNEL + TAPS, :] = kernel_ref[...]
    state_vectors_ref[...] = jnp.zeros_like(state_vectors_ref)
    state_vectors_ref[:TAPS, :] = state_kernel_ref[...]
    state_vectors_ref[TAPS : TAPS + 1, :] = row(state_offset_ref)
    heads_ref[...] = jnp.zeros_like(heads_ref)
    heads_ref[0:1, :heads] = row(bias_ref)
    heads_ref[1:2, :heads] = -jnp.exp(row(decay_ref))
    heads_ref[2:3, :heads] = row(skip_ref)
    lanes = lax.broadcasted_iota(jnp.int32, (128, width), 1)
    start = lax.broadcasted_iota(jnp.int32, (128, width), 0) * HEAD_DIM
    picks = jnp.where((lanes >= start) & (lanes < start + HEAD_DIM), 1.0, 0.0).astype(BF16)
    high, middle, low = split3(heads_ref[...])
    spread_rows = dot_nn(high, picks) + dot_nn(middle, picks) + dot_nn(low, picks)
    vectors_ref[SKIP : SKIP + 1, :] = spread_rows[2:3]
    step_rows_ref[...] = jnp.concatenate(
        [step_ref[...].astype(F32), jnp.zeros((128 - heads, width), F32)], axis=0
    ).astype(BF16)


def run_prepare(*arrays):
    width = arrays[0].shape[0]
    shapes = [shape_of(8, width), shape_of(8, 2 * STATE), shape_of(8, 128), shape_of(128, width, dtype=BF16)]
    return pl.pallas_call(
        prepare_kernel,
        out_shape=shapes,
        cost_estimate=cost(2),
        name="prepare",
    )(*arrays)


SWAP = [(0, 1), (1, 0)]
SCAN_PARTS = (1, 1, 2)
IN_PARTS = 2
LAST_PARTS = 4


def swap(value):
    return lax.ppermute(value, "tensor", SWAP)


def body(hidden, cotangent, norm_weight, gate_in, value_in, state_in, step_in, value_kernel, value_offset,
         state_kernel, state_offset, step_bias, log_decay, skip_weight, gated_norm, out_weight):
    core = lax.axis_index("tensor").astype(jnp.int32)
    tokens, width = hidden.shape
    channels = gate_in.shape[1]
    heads = step_in.shape[1]
    inner = 2 * channels
    count = lax.axis_size("dp")
    core_index = core.reshape(1)
    if count & (count - 1) == 0 and width % (8 * count) == 0 and PACK_ROWS % (8 * count) == 0:
        reduction = Reduction
        position = lax.axis_index("dp").astype(jnp.int32)
        bits = [
            jnp.where(core == 0, (position >> low) & 1, (position >> high) & 1)
            for low, high in zip(*bit_orders(count), strict=True)
        ]
    else:
        reduction = PlainReduction
        bits = [jnp.int32(0)]
    digits = jnp.stack(bits + [core])
    vectors, state_vectors, head_rows, step_rows = run_prepare(
        norm_weight, value_offset, gated_norm, skip_weight, value_kernel, state_kernel, state_offset, step_bias,
        log_decay, step_in.T,
    )

    (normed, state_raw, conv, pair_t, value_raw, gate_raw, mixed, gated, grad_scaled, step_pre, steps, log, sums) = run_forward(
        hidden, cotangent, vectors, state_vectors, head_rows, gate_in, value_in, state_in, step_rows, out_weight
    )
    grad_mixed, gate_low, partial_out, grad_gain, norm_gate, *pieces = run_norm_back(
        digits, normed, gated, mixed, gate_raw, grad_scaled, cotangent, sums, swap(sums), vectors, gate_in, out_weight, inner
    )
    weights_sum = reduction(pieces, digits, count, "weights")
    other_out = swap(partial_out)
    groups = channels // WIDTH
    value_low = grad_pair = first_value = None
    row_sums, column_sums, direct, value_rows, norm_rows = [], [], [], [], [norm_gate]
    ready = normed
    for group in range(groups):
        last = group == groups - 1
        extra = (conv, step_pre, head_rows, step_rows, row_sums, column_sums, direct) if last else None
        before = []
        parts = SCAN_PARTS[group % len(SCAN_PARTS)]
        for part in range(parts):
            value_low, *results = run_scan_back(
                group, groups, part, parts, digits, ready, pair_t, value_raw, grad_mixed, steps, log, vectors,
                value_in, value_low, grad_pair, first_value, extra, before,
            )
            wholes, totals = (results[:3], results[3:]) if last else (results[:4], results[4:])
            if part < parts - 1:
                before = [*wholes, totals[-1], *totals[:-1]]
            weights_sum.advance(value_low)
            if last:
                value_sum.advance(value_low)
            ready = tie(normed, value_low, weights_sum.held, other_out, *([value_sum.held] if last else []))
        value_rows.append(totals.pop(0))
        norm_rows.append(totals.pop(-1))
        if last:
            step_low, mine, outgoing = wholes
            grad_step, grad_heads, first_value = totals
        else:
            grad_pair = wholes[0]
            for kept, whole in zip((row_sums, column_sums, direct), wholes[1:], strict=True):
                kept.append(whole)
            if group == 1:
                value_sum = reduction(totals, digits, count, "value")
            else:
                (first_value,) = totals
    came = swap(tie(outgoing, weights_sum.held, value_sum.held))
    state_low, *pieces = run_state(
        digits, core, mine, came, state_raw, ready, state_in, state_vectors, first_value, grad_step, grad_gain,
        grad_heads, value_rows, norm_rows,
    )
    small_sum = reduction(pieces, digits, count, "small")
    value_sum.advance(state_low)
    weights_sum.advance(state_low)
    partials = []
    for part in range(IN_PARTS):
        low = tie(state_low, value_sum.held, weights_sum.held, small_sum.held)
        partial_in = run_in(
            part, IN_PARTS, core_index, gate_low, value_low, step_low, low, gate_in, value_in, step_rows, state_in
        )
        partials.append((partial_in, swap(partial_in)))
        small_sum.advance(partial_in)
        weights_sum.advance(partial_in)
        value_sum.advance(partial_in)
    results = []
    for part in range(LAST_PARTS):
        ready = tie(vectors, value_sum.held, weights_sum.held, small_sum.held)
        results = run_last(
            part, LAST_PARTS, results, hidden, cotangent, *partials[part * IN_PARTS // LAST_PARTS], partial_out,
            other_out, ready,
        )
        small_sum.advance(results[0])
        weights_sum.advance(results[0])
        value_sum.advance(results[0])
    block_out, grad_hidden = results
    grad_out_weight, grad_gate_in = small_call(
        join_weights_kernel, digits, list(weights_sum.halves()), [shape_of(channels, width), shape_of(width, channels)], "weights_last"
    )
    value_halves = value_sum.halves()
    small_sum.advance(value_halves[1])
    small, shared = small_call(
        join_small_kernel, digits, list(small_sum.halves()), [shape_of(PACK_ROWS, 128), shape_of(SHARED_ROWS, 128)], "small_last"
    )
    (grad_value_in, grad_state_in, grad_norm, grad_step_in, grad_value_kernel, grad_value_offset, grad_state_kernel,
     grad_state_offset, grad_step_bias, grad_log_decay, grad_skip, grad_gain) = small_call(
        finish_kernel, digits, [*value_halves, small, swap(shared), tie(vectors, grad_out_weight)],
        [shape_of(width, channels), shape_of(width, 2 * STATE), shape_of(width), shape_of(heads, width),
         shape_of(TAPS, channels), shape_of(channels), shape_of(TAPS, 2 * STATE), shape_of(2 * STATE),
         shape_of(heads), shape_of(heads), shape_of(heads), shape_of(channels)], "finish",
    )
    return (
        block_out,
        grad_hidden,
        grad_norm,
        grad_gate_in,
        grad_value_in,
        grad_state_in,
        grad_step_in.T,
        grad_value_kernel,
        grad_value_offset,
        grad_state_kernel,
        grad_state_offset,
        grad_step_bias,
        grad_log_decay,
        grad_skip,
        grad_gain,
        grad_out_weight,
    )


def solution(mesh):
    in_specs = (
        P("dp", None),
        P("dp", None),
        P(),
        P(None, "tensor"),
        P(None, "tensor"),
        P(),
        P(None, "tensor"),
        P(None, "tensor"),
        P("tensor"),
        P(),
        P(),
        P("tensor"),
        P("tensor"),
        P("tensor"),
        P("tensor"),
        P("tensor", None),
    )
    out_specs = (
        P("dp", None),
        P("dp", None),
        P(),
        P(None, "tensor"),
        P(None, "tensor"),
        P(),
        P(None, "tensor"),
        P(None, "tensor"),
        P("tensor"),
        P(),
        P(),
        P("tensor"),
        P("tensor"),
        P("tensor"),
        P("tensor"),
        P("tensor", None),
    )
    return jax.shard_map(body, mesh=mesh, in_specs=in_specs, out_specs=out_specs, check_vma=False)
```

```python
import functools

import jax
import jax.numpy as jnp
from jax import lax
from jax.experimental import pallas as pl
from jax.experimental.pallas import tpu as pltpu
from jax.sharding import PartitionSpec as P

HEAD_DIM = 64
STATE = 128
LENGTH = 512
STRIP = 128
WIDTH = 256
GROUP_HEADS = WIDTH // HEAD_DIM
EPSILON = 1e-05
F32 = jnp.float32
BF16 = jnp.bfloat16
MIB = 1 << 20
TAPS = 4
NORM, OFFSET, GAIN, SKIP, KERNEL = range(5)


def dot_nn(left, right):
    return lax.dot_general(left, right, (((1,), (0,)), ((), ())), preferred_element_type=F32)


def dot_nt(left, right):
    return lax.dot_general(left, right, (((1,), (1,)), ((), ())), preferred_element_type=F32)


def dot_tn(left, right):
    return lax.dot_general(left, right, (((0,), (0,)), ((), ())), preferred_element_type=F32)


def split2(value):
    high = value.astype(BF16)
    return high, (value - high.astype(F32)).astype(BF16)


def split3(value):
    high = value.astype(BF16)
    rest = value - high.astype(F32)
    middle = rest.astype(BF16)
    return high, middle, (rest - middle.astype(F32)).astype(BF16)


def dot3(dot, left, right):
    left_high, left_low = split2(left)
    right_high, right_low = split2(right)
    return dot(left_high, right_high) + (dot(left_high, right_low) + dot(left_low, right_high))


def sigmoid(value):
    return 1.0 / (1.0 + jnp.exp(-value))


def softplus(value):
    return jnp.maximum(value, 0.0) + jnp.log1p(jnp.exp(-jnp.abs(value)))


def triangular(rows, keep_lower):
    down = lax.broadcasted_iota(jnp.int32, (rows, rows), 0)
    along = lax.broadcasted_iota(jnp.int32, (rows, rows), 1)
    return down >= along if keep_lower else down <= along


def running_sum(value, keep_lower):
    high, middle, low = split3(value)
    packed = (
        high.astype(F32)
        + pltpu.roll(middle.astype(F32), 16, 1)
        + pltpu.roll(low.astype(F32), 32, 1)
    ).astype(BF16)
    ones = jnp.where(triangular(value.shape[0], keep_lower), 1.0, 0.0).astype(BF16)
    sums = dot_nn(ones, packed)
    total = sums + pltpu.roll(sums, 128 - 16, 1) + pltpu.roll(sums, 128 - 32, 1)
    lanes = lax.broadcasted_iota(jnp.int32, total.shape, 1)
    return jnp.where(lanes < 16, total, 0.0)


def spread(columns):
    rows = columns.shape[0]
    lanes = lax.broadcasted_iota(jnp.int32, (rows, 128), 1)
    halves = []
    for pair in range(GROUP_HEADS // 2):
        first = jnp.broadcast_to(columns[:, 2 * pair : 2 * pair + 1], (rows, 128))
        second = jnp.broadcast_to(columns[:, 2 * pair + 1 : 2 * pair + 2], (rows, 128))
        halves.append(jnp.where(lanes < HEAD_DIM, first, second))
    return jnp.concatenate(halves, axis=1)


def head_only(value, head):
    lanes = lax.broadcasted_iota(jnp.int32, value.shape, 1)
    return jnp.where((lanes >= head * HEAD_DIM) & (lanes < (head + 1) * HEAD_DIM), value, 0.0).astype(BF16)


def shifted_down(value, by):
    if by == 0:
        return value
    rows = lax.broadcasted_iota(jnp.int32, value.shape, 0)
    return jnp.where(rows >= by, pltpu.roll(value, by, 0), 0.0)


def shifted_up(value, by):
    if by == 0:
        return value
    count = value.shape[0]
    rows = lax.broadcasted_iota(jnp.int32, value.shape, 0)
    return jnp.where(rows < count - by, pltpu.roll(value, count - by, 0), 0.0)


def convolve(value, kernel, offset):
    taps = kernel.shape[0]
    total = offset + kernel[taps - 1 : taps] * value
    for tap in range(taps - 1):
        total = total + kernel[tap : tap + 1] * shifted_down(value, taps - 1 - tap)
    return total


def convolve_back(grad_out, value, kernel):
    taps = kernel.shape[0]
    grad_in = kernel[taps - 1 : taps] * grad_out
    rows = []
    for tap in range(taps):
        by = taps - 1 - tap
        if by:
            grad_in = grad_in + kernel[tap : tap + 1] * shifted_up(grad_out, by)
        rows.append(jnp.sum(grad_out * shifted_down(value, by), axis=0, keepdims=True))
    rows.append(jnp.sum(grad_out, axis=0, keepdims=True))
    rows.append(jnp.zeros((8 - taps - 1, grad_out.shape[1]), F32))
    return grad_in, jnp.concatenate(rows, axis=0)


def forward_kernel(
    hidden_ref, cotangent_ref, norm_ref, vectors_ref, state_vectors_ref, heads_ref, gate_in_ref, value_in_ref,
    state_in_ref, step_in_ref, out_weight_ref,
    normed_ref, state_raw_ref, conv_ref, pair_t_ref, value_raw_ref, gate_raw_ref, mixed_ref, gated_ref,
    grad_scaled_ref, step_pre_ref, steps_ref, log_ref, sums_ref,
    upstream_s, pair_s, steps_s, log_s, log_t_s, squares_s, terms_s,
):
    group = pl.program_id(1)

    @pl.when(group == 0)
    def _():
        rows = hidden_ref[...]
        scale = lax.rsqrt(jnp.mean(rows * rows, axis=-1, keepdims=True) + EPSILON)
        normed = (rows * scale * norm_ref[NORM : NORM + 1, :]).astype(BF16)
        normed_ref[...] = normed
        upstream_s[...] = cotangent_ref[...].astype(BF16)
        raw = dot_nn(normed, state_in_ref[...])
        state_raw_ref[...] = raw
        pre = convolve(raw, state_vectors_ref[:TAPS, :], state_vectors_ref[TAPS : TAPS + 1, :])
        conv = pre * sigmoid(pre)
        conv_ref[...] = conv
        pair = dot3(dot_nt, conv[:, STATE:], conv[:, :STATE])
        pair_s[...] = jnp.where(triangular(LENGTH, True), pair, 0.0)
        pair = dot3(dot_nt, conv[:, :STATE], conv[:, STATE:])
        pair_t_ref[...] = jnp.where(triangular(LENGTH, False), pair, 0.0)
        step_pre = dot_nt(normed, step_in_ref[...]) + heads_ref[0:1, :]
        step_pre_ref[...] = step_pre
        lanes = lax.broadcasted_iota(jnp.int32, step_pre.shape, 1)
        steps = jnp.where(lanes < 12, softplus(step_pre), 0.0)
        steps_ref[...] = steps
        log = running_sum(steps * heads_ref[1:2, :], True)
        log_ref[...] = log
        transposed = log.T
        for g in range(steps_s.shape[0]):
            back = (128 - GROUP_HEADS * g) % 128
            steps_s[g] = pltpu.roll(steps, back, 1) if back else steps
            log_s[g] = pltpu.roll(log, back, 1) if back else log
            log_t_s[g] = transposed[GROUP_HEADS * g : GROUP_HEADS * g + 8]
        squares_s[...] = jnp.zeros_like(squares_s)
        terms_s[...] = jnp.zeros_like(terms_s)

    normed = normed_ref[...]
    raw = dot_nn(normed, value_in_ref[...])
    value_raw_ref[...] = raw
    pre = convolve(raw, vectors_ref[KERNEL : KERNEL + TAPS, :], vectors_ref[OFFSET : OFFSET + 1, :])
    values = pre * sigmoid(pre)
    weighted = values * spread(steps_s[group])
    parts = [head_only(weighted, head) for head in range(GROUP_HEADS)]
    log = log_s[group]
    log_t = log_t_s[group]
    strips = []
    for strip in range(LENGTH // STRIP):
        low, high = strip * STRIP, (strip + 1) * STRIP
        pair = pair_s[low:high, :high]
        weights = []
        for head in range(GROUP_HEADS):
            gap = jnp.minimum(log[low:high, head : head + 1] - log_t[head : head + 1, :high], 0.0)
            weights.append((jnp.exp(gap) * pair).astype(BF16))
        strips.append(
            dot_nn(
                jnp.concatenate(weights, axis=1),
                jnp.concatenate([part[:high] for part in parts], axis=0),
            )
        )
    mixed = jnp.concatenate(strips, axis=0) + vectors_ref[SKIP : SKIP + 1, :] * values
    mixed_ref[...] = mixed
    gate = dot_nn(normed, gate_in_ref[...])
    gate_raw_ref[...] = gate
    gated = mixed * (gate * sigmoid(gate))
    gated_ref[...] = gated
    grad_scaled = dot_nt(upstream_s[...], out_weight_ref[...])
    grad_scaled_ref[...] = grad_scaled
    squares = gated * gated
    terms = grad_scaled * vectors_ref[GAIN : GAIN + 1, :] * gated
    squares_s[...] += squares[:, :128] + squares[:, 128:]
    terms_s[...] += terms[:, :128] + terms[:, 128:]

    @pl.when(group == pl.num_programs(1) - 1)
    def _():
        lanes = lax.broadcasted_iota(jnp.int32, (LENGTH, 128), 1)
        both = jnp.where(
            lanes == 0,
            jnp.sum(squares_s[...], axis=1, keepdims=True),
            jnp.where(lanes == 1, jnp.sum(terms_s[...], axis=1, keepdims=True), 0.0),
        )
        sums_ref[...] = both.T[:8]


def cost(micros):
    return pl.CostEstimate(
        flops=int(micros * 7.0e9), transcendentals=0, bytes_accessed=int(micros * 2.1e7)
    )


def const_spec(shape):
    return pl.BlockSpec(shape, lambda *_: (0,) * len(shape))


def shape_of(*dims, dtype=F32):
    return jax.ShapeDtypeStruct(dims, dtype)


def bit_orders(count):
    bits = count.bit_length() - 1
    return list(range(bits)), list(range(1, bits)) + [0]


def cut_shapes(rows, columns):
    return [shape_of(rows // 2, columns)] * 2


def cut_into(source, bits, outs):
    half = source.shape[0] // 2
    outs[0][...] = source[pl.ds(pl.multiple_of((1 - bits[0]) * half, 8), half), :]
    outs[1][...] = source[pl.ds(pl.multiple_of(bits[0] * half, 8), half), :]


def sum_kernel(step, bits, keep_ref, came_ref, send_ref, next_ref):
    half = keep_ref.shape[0] // 2
    other = pl.ds(pl.multiple_of((1 - bits[step]) * half, 8), half)
    mine = pl.ds(pl.multiple_of(bits[step] * half, 8), half)
    send_ref[...] = keep_ref[other, :] + came_ref[other, :]
    next_ref[...] = keep_ref[mine, :] + came_ref[mine, :]


def join_last(bits, own, came, out, start, rows, offset=0):
    out[pl.ds(pl.multiple_of(start + bits[0] * rows, 8), rows), :] = own[offset : offset + rows, :]
    out[pl.ds(pl.multiple_of(start + (1 - bits[0]) * rows, 8), rows), :] = came[offset : offset + rows, :]


def total_kernel(bits, keep_ref, came_ref, out_ref):
    out_ref[...] = keep_ref[...] + came_ref[...]


def join_kernel(step, bits, own_ref, came_ref, out_ref):
    half = own_ref.shape[0]
    out_ref[pl.ds(pl.multiple_of(bits[step] * half, 8), half), :] = own_ref[...]
    out_ref[pl.ds(pl.multiple_of((1 - bits[step]) * half, 8), half), :] = came_ref[...]


def small_call(kernel, scalars, arrays, out_shape, name):
    return pl.pallas_call(
        kernel,
        grid_spec=pltpu.PrefetchScalarGridSpec(
            num_scalar_prefetch=1,
            grid=(1,),
            in_specs=[const_spec(a.shape) for a in arrays],
            out_specs=[const_spec(s.shape) for s in out_shape],
        ),
        out_shape=out_shape,
        compiler_params=pltpu.CompilerParams(vmem_limit_bytes=40 * MIB),
        cost_estimate=cost(0.02),
        name=name,
    )(scalars, *arrays)


def tie(value, *after):
    return lax.optimization_barrier((value, *after))[0]


class Reduction:
    def __init__(self, pieces, bits, count, name):
        self.sent, self.held = pieces
        self.bits, self.count, self.name = bits, count, name
        self.orders = bit_orders(count)
        self.steps = len(self.orders[0])
        self.step = 0
        self.send(0)

    def send(self, step):
        pairs = [
            (2 * i + core, 2 * (i ^ (1 << self.orders[core][step])) + core)
            for i in range(self.count) for core in range(2)
        ]
        self.came = lax.ppermute(self.sent, ("dp", "tensor"), pairs)

    def advance(self, *after):
        if self.step == 2 * self.steps - 1:
            return self.held
        self.step += 1
        steps, step = self.steps, self.step
        held = tie(self.held, *after) if after else self.held
        rows, columns = held.shape
        if step < steps:
            self.sent, self.held = small_call(
                functools.partial(sum_kernel, step), self.bits, [held, self.came],
                [shape_of(rows // 2, columns)] * 2, self.name + "_sum",
            )
            self.send(step)
        elif step == steps:
            (self.held,) = small_call(
                total_kernel, self.bits, [held, self.came], [shape_of(rows, columns)], self.name + "_total"
            )
            self.sent = self.held
            self.send(steps - 1)
        else:
            back = 2 * steps - step
            (self.held,) = small_call(
                functools.partial(join_kernel, back), self.bits, [held, self.came],
                [shape_of(2 * rows, columns)], self.name + "_join",
            )
            self.sent = self.held
            self.send(back - 1)
        return self.held

    def halves(self):
        while self.step < 2 * self.steps - 1:
            self.advance()
        return self.held, self.came


class PlainReduction:
    def __init__(self, pieces, bits, count, name):
        self.sent, self.held = lax.psum(tuple(pieces), "dp")

    def advance(self, *after):
        return self.held

    def halves(self):
        return self.held, self.sent


def run_forward(hidden, cotangent, vectors, state_vectors, heads, gate_in, value_in, state_in, step_in, out_weight):
    tokens, width = hidden.shape
    channels = gate_in.shape[1]
    groups = channels // WIDTH
    sequences = tokens // LENGTH
    row = lambda s, g: (s, 0)
    block = lambda s, g: (s, g)
    column = lambda s, g: (0, g)
    wide = shape_of(tokens, channels)
    narrow = shape_of(tokens, 128)
    wide_spec = pl.BlockSpec((LENGTH, WIDTH), block)
    narrow_spec = pl.BlockSpec((LENGTH, 128), row)
    return pl.pallas_call(
        forward_kernel,
        grid=(sequences, groups),
        in_specs=[
            pl.BlockSpec((LENGTH, width), row),
            pl.BlockSpec((LENGTH, width), row),
            const_spec((8, width)),
            pl.BlockSpec((8, WIDTH), column),
            const_spec((8, 2 * STATE)),
            const_spec((8, 128)),
            pl.BlockSpec((width, WIDTH), column),
            pl.BlockSpec((width, WIDTH), column),
            const_spec((width, 2 * STATE)),
            const_spec((128, width)),
            pl.BlockSpec((WIDTH, width), lambda s, g: (g, 0)),
        ],
        out_specs=[
            pl.BlockSpec((LENGTH, width), row),
            pl.BlockSpec((LENGTH, 2 * STATE), row),
            pl.BlockSpec((LENGTH, 2 * STATE), row),
            pl.BlockSpec((LENGTH, LENGTH), row),
            wide_spec,
            wide_spec,
            wide_spec,
            wide_spec,
            wide_spec,
            narrow_spec,
            narrow_spec,
            narrow_spec,
            pl.BlockSpec((8, LENGTH), lambda s, g: (0, s)),
        ],
        out_shape=[
            shape_of(tokens, width, dtype=BF16),
            shape_of(tokens, 2 * STATE),
            shape_of(tokens, 2 * STATE),
            shape_of(tokens, LENGTH),
            wide,
            wide,
            wide,
            wide,
            wide,
            narrow,
            narrow,
            narrow,
            shape_of(8, tokens),
        ],
        scratch_shapes=[
            pltpu.VMEM((LENGTH, width), BF16),
            pltpu.VMEM((LENGTH, LENGTH), F32),
            pltpu.VMEM((groups, LENGTH, 128), F32),
            pltpu.VMEM((groups, LENGTH, 128), F32),
            pltpu.VMEM((groups, 8, LENGTH), F32),
            pltpu.VMEM((LENGTH, 128), F32),
            pltpu.VMEM((LENGTH, 128), F32),
        ],
        compiler_params=pltpu.CompilerParams(vmem_limit_bytes=56 * MIB),
        cost_estimate=cost(45),
        name="forward_mix",
    )(hidden, cotangent, vectors, vectors, state_vectors, heads, gate_in, value_in, state_in, step_in, out_weight)


def row_factors(own_ref, other_ref, inner):
    sums = own_ref[...] + other_ref[...]
    columns = jnp.concatenate([sums, jnp.zeros((120, sums.shape[1]), F32)], axis=0).T
    scale = lax.rsqrt(columns[:, 0:1] / inner + EPSILON)
    return scale, columns[:, 1:2] * (scale * scale * scale) / inner


def along_rows(column):
    return jnp.broadcast_to(column, (column.shape[0], 128)).T[:8]


def norm_back_kernel(
    inner, digits, normed_ref, gated_ref, mixed_ref, gate_ref, grad_scaled_ref, cotangent_ref, own_ref, other_ref,
    vectors_ref, gate_in_ref, out_weight_ref,
    grad_mixed_ref, gate_low_ref, partial_ref, grad_norm_ref, norm_rows_ref, send_ref, keep_ref, out_s, gate_s,
):
    @pl.when(pl.program_id(0) == 0)
    def _():
        out_s[...] = jnp.zeros_like(out_s)
        gate_s[...] = jnp.zeros_like(gate_s)
        grad_norm_ref[...] = jnp.zeros_like(grad_norm_ref)

    scale, factor = row_factors(own_ref, other_ref, inner)
    normed_t = normed_ref[...].T
    upstream = cotangent_ref[...].astype(BF16)
    partial = None
    for group in range(gated_ref.shape[1] // WIDTH):
        columns = slice(group * WIDTH, (group + 1) * WIDTH)
        gated = gated_ref[:, columns]
        gate = gate_ref[:, columns]
        gain = vectors_ref[GAIN : GAIN + 1, columns]
        scaled = (gated * scale * gain).astype(BF16)
        out_s[columns, :] += dot_tn(scaled, upstream)
        product = dot_nn(scaled, out_weight_ref[columns, :])
        partial = product if partial is None else partial + product
        scaled_by = grad_scaled_ref[:, columns] * scale
        grad_norm_ref[:, columns] += jnp.broadcast_to(
            jnp.sum(scaled_by * gated, axis=0, keepdims=True), (8, WIDTH)
        )
        grad_gated = scaled_by * gain - gated * factor
        s = sigmoid(gate)
        grad_mixed_ref[:, columns] = grad_gated * (gate * s)
        low = (grad_gated * mixed_ref[:, columns] * (s * (1.0 + gate * (1.0 - s)))).astype(BF16)
        gate_low_ref[:, columns] = low
        gate_s[:, columns] += dot_nn(normed_t, low)
    partial_ref[...] = partial

    @pl.when(pl.program_id(0) == pl.num_programs(0) - 1)
    def _():
        half = gate_s.shape[0] // 2
        other = pl.ds(pl.multiple_of((1 - digits[0]) * half, 8), half)
        mine = pl.ds(pl.multiple_of(digits[0] * half, 8), half)
        for k, source in enumerate((out_s, gate_s)):
            send_ref[k * half : (k + 1) * half, :] = source[other, :]
            keep_ref[k * half : (k + 1) * half, :] = source[mine, :]
        norm_rows_ref[...] = along_rows(
            jnp.sum(gate_s[...] * gate_in_ref[...].astype(F32), axis=1, keepdims=True)
        )


def run_norm_back(digits, normed, gated, mixed, gate_raw, grad_scaled, cotangent, own, other, vectors, gate_in,
                  out_weight, inner):
    tokens, channels = gated.shape
    width = normed.shape[1]
    row = lambda s, _: (s, 0)
    wide = pl.BlockSpec((LENGTH, channels), row)
    rows = (width + channels) // 2
    return pl.pallas_call(
        functools.partial(norm_back_kernel, inner),
        grid_spec=pltpu.PrefetchScalarGridSpec(
            num_scalar_prefetch=1,
            grid=(tokens // LENGTH,),
            in_specs=[
                pl.BlockSpec((LENGTH, width), row),
                wide,
                wide,
                wide,
                wide,
                pl.BlockSpec((LENGTH, width), row),
                pl.BlockSpec((8, LENGTH), lambda s, _: (0, s)),
                pl.BlockSpec((8, LENGTH), lambda s, _: (0, s)),
                const_spec((8, channels)),
                const_spec((width, channels)),
                const_spec((channels, width)),
            ],
            out_specs=[
                wide,
                wide,
                pl.BlockSpec((LENGTH, width), row),
                const_spec((8, channels)),
                const_spec((8, width)),
                const_spec((rows, width)),
                const_spec((rows, width)),
            ],
            scratch_shapes=[pltpu.VMEM((channels, width), F32), pltpu.VMEM((width, channels), F32)],
        ),
        out_shape=[
            shape_of(tokens, channels),
            shape_of(tokens, channels, dtype=BF16),
            shape_of(tokens, width),
            shape_of(8, channels),
            shape_of(8, width),
            shape_of(rows, width),
            shape_of(rows, width),
        ],
        compiler_params=pltpu.CompilerParams(vmem_limit_bytes=60 * MIB),
        cost_estimate=cost(26),
        name="norm_back",
    )(digits, normed, gated, mixed, gate_raw, grad_scaled, cotangent, own, other, vectors, gate_in, out_weight)


def scan_back_kernel(
    group, groups, part, parts, digits, normed_ref, pair_ref, value_raw_ref, grad_mixed_ref, steps_ref, log_ref,
    vectors_ref, value_in_ref, *refs,
):
    first, last, final = group == 0, group == groups - 1, part == parts - 1
    refs = list(refs)
    take = lambda count: [refs.pop(0) for _ in range(count)]
    if part or not first:
        take(1)
    if not first:
        (grad_pair_before,) = take(1)
    if group == 1 and final:
        (value_before,) = take(1)
    if last:
        conv_ref, step_pre_ref, heads_ref, step_in_ref = take(4)
        rows_before, columns_before, direct_before = take(group), take(group), take(group)
    if part:
        take(3 if last else 4)
        totals_before = take(4 if last else 2)
    (value_low_ref,) = take(1)
    if last:
        step_low_ref, mine_ref, other_ref = take(3)
    else:
        grad_pair_ref, row_sums_ref, column_sums_ref, direct_ref = take(4)
    (rows_ref,) = take(1)
    if last:
        grad_step_ref, head_rows_ref = take(2)
    if final:
        value_outs = take(2 if group == 1 else 1)
        (norm_rows_ref,) = take(1)
    else:
        (value_total_ref,) = take(1)
    grad_value_s, grad_pair_s = take(2)
    sequence = pl.program_id(0)

    @pl.when(sequence == 0)
    def _():
        totals = [grad_value_s, rows_ref] + ([grad_step_ref, head_rows_ref] if last else [])
        for k, total in enumerate(totals):
            total[...] = totals_before[k][...] if part else jnp.zeros_like(total)

    place = group * GROUP_HEADS
    back = (128 - place) % 128
    group_steps, log = steps_ref[...], log_ref[...]
    log_t = log.T[place : place + GROUP_HEADS]
    if back:
        group_steps, log = pltpu.roll(group_steps, back, 1), pltpu.roll(log, back, 1)
    raw = value_raw_ref[...]
    kernel = vectors_ref[KERNEL : KERNEL + TAPS, :]
    pre = convolve(raw, kernel, vectors_ref[OFFSET : OFFSET + 1, :])
    s = sigmoid(pre)
    values = pre * s
    steps = spread(group_steps)
    weighted = values * steps
    grad_mixed = grad_mixed_ref[...]
    grad_low = grad_mixed.astype(BF16)
    weighted_parts = [head_only(weighted, head) for head in range(GROUP_HEADS)]
    grad_parts = [head_only(grad_mixed, head) for head in range(GROUP_HEADS)]
    strips = []
    columns = []
    row_sums = [jnp.zeros((1, LENGTH), F32) for _ in range(GROUP_HEADS)]
    for strip in range(LENGTH // STRIP):
        low, high = strip * STRIP, (strip + 1) * STRIP
        pair = pair_ref[low:high, low:]
        total = None
        products = []
        sums = []
        for head in range(GROUP_HEADS):
            gap = jnp.minimum(log_t[head : head + 1, low:] - log[low:high, head : head + 1], 0.0)
            decay = jnp.exp(gap)
            weight = decay * pair
            products.append(weight.astype(BF16))
            grad_weight = dot_nt(weighted_parts[head][low:high], grad_low[low:])
            grad_pair = grad_weight * decay
            total = grad_pair if total is None else total + grad_pair
            both = grad_weight * weight
            sums.append(jnp.sum(both, axis=1, keepdims=True))
            along = jnp.sum(both, axis=0, keepdims=True)
            if low:
                along = jnp.concatenate([jnp.zeros((1, low), F32), along], axis=1)
            row_sums[head] = row_sums[head] + along
        if not first:
            total = total + grad_pair_before[low:high, low:]
        if last:
            grad_pair_s[low:high, low:] = total
        else:
            grad_pair_ref[low:high, low:] = total
        columns.append(sums)
        strips.append(
            dot_nn(
                jnp.concatenate(products, axis=1),
                jnp.concatenate([part[low:] for part in grad_parts], axis=0),
            )
        )
    reached = jnp.concatenate(strips, axis=0)
    lanes = lax.broadcasted_iota(jnp.int32, (LENGTH, 128), 1)
    column_sums = jnp.zeros((LENGTH, 128), F32)
    for head in range(GROUP_HEADS):
        one = jnp.concatenate([sums[head] for sums in columns], axis=0)
        column_sums = jnp.where(lanes == place + head, one, column_sums)
    down = lax.broadcasted_iota(jnp.int32, (WIDTH, 128), 0)
    across = lax.broadcasted_iota(jnp.int32, (WIDTH, 128), 1)
    start = (across - place) * HEAD_DIM
    picks = jnp.where((down >= start) & (down < start + HEAD_DIM), 1.0, 0.0).astype(BF16)
    direct_high, direct_low = split2(values * reached)
    direct = dot_nn(direct_high, picks) + dot_nn(direct_low, picks)

    grad_values = steps * reached + vectors_ref[SKIP : SKIP + 1, :] * grad_mixed
    grad_pre = grad_values * (s * (1.0 + pre * (1.0 - s)))
    grad_raw, rows = convolve_back(grad_pre, raw, kernel)
    skip_rows = jnp.sum(grad_mixed * values, axis=0, keepdims=True)
    rows_ref[...] += jnp.concatenate([rows[: TAPS + 1], skip_rows, rows[TAPS + 2 :]], axis=0)
    value_low = grad_raw.astype(BF16)
    value_low_ref[...] = value_low
    grad_value_s[...] += dot_tn(value_low, normed_ref[...])

    if not last:
        row_sums_ref[...] = jnp.concatenate(row_sums + [jnp.zeros((8 - GROUP_HEADS, LENGTH), F32)], axis=0)
        column_sums_ref[...] = column_sums
        direct_ref[...] = direct
    else:
        conv = conv_ref[...]
        grad_pair = jnp.where(triangular(LENGTH, False), grad_pair_s[...], 0.0)
        grad_write = dot3(dot_nn, grad_pair, conv[:, STATE:])
        grad_read = dot3(dot_tn, grad_pair, conv[:, :STATE])
        core = digits[digits.shape[0] - 1]
        mine_ref[...] = jnp.where(core == 0, grad_write, grad_read)
        other_ref[...] = jnp.where(core == 0, grad_read, grad_write)
        for before in columns_before:
            column_sums = column_sums + before[...]
        for before in direct_before:
            direct = direct + before[...]
        row_sums = jnp.concatenate(
            [before[:GROUP_HEADS, :] for before in rows_before]
            + row_sums
            + [jnp.zeros((128 - GROUP_HEADS * groups, LENGTH), F32)],
            axis=0,
        ).T
        memory = running_sum(row_sums - column_sums, False)
        step_pre = step_pre_ref[...]
        rate = heads_ref[1:2, :]
        grad_raw = jnp.where(lanes < 12, (direct + rate * memory) * sigmoid(step_pre), 0.0)
        step_low = grad_raw.astype(BF16)
        step_low_ref[...] = step_low
        grad_step_ref[...] += dot_tn(step_low, normed_ref[...])[:16]
        decay_row = rate * jnp.sum(steps_ref[...] * memory, axis=0, keepdims=True)
        head_rows_ref[...] += jnp.concatenate(
            [jnp.sum(grad_raw, axis=0, keepdims=True), decay_row, jnp.zeros((6, 128), F32)], axis=0
        )

    @pl.when(sequence == pl.num_programs(0) - 1)
    def _():
        if not final:
            value_total_ref[...] = grad_value_s[...]
            return
        grad_value = grad_value_s[...].T
        norm_column = jnp.sum(grad_value * value_in_ref[...].astype(F32), axis=1, keepdims=True)
        norm_rows = along_rows(norm_column)
        if last:
            product = grad_step_ref[...] * step_in_ref[:16, :].astype(F32)
            norm_rows = norm_rows + jnp.broadcast_to(jnp.sum(product, axis=0, keepdims=True), norm_rows.shape)
        norm_rows_ref[...] = norm_rows
        if group == 1:
            send_ref, keep_ref = value_outs
            half = send_ref.shape[0]
            other = pl.ds(pl.multiple_of((1 - digits[0]) * half, 8), half)
            mine = pl.ds(pl.multiple_of(digits[0] * half, 8), half)
            send_ref[:, :WIDTH] = value_before[other, :]
            keep_ref[:, :WIDTH] = value_before[mine, :]
            low, high = grad_value[:half], grad_value[half:]
            send_ref[:, WIDTH:] = jnp.where(digits[0] == 0, high, low)
            keep_ref[:, WIDTH:] = jnp.where(digits[0] == 0, low, high)
        else:
            value_outs[0][...] = grad_value


def run_scan_back(group, groups, part, parts, digits, normed, pair, value_raw, grad_mixed, steps, log, vectors,
                  value_in, value_low, grad_pair, first_value, extra, before):
    tokens, width = normed.shape
    channels = value_raw.shape[1]
    count = tokens // LENGTH // parts
    first, last, final = group == 0, group == groups - 1, part == parts - 1
    row = lambda s, _: (s + part * count, 0)
    block = lambda s, _: (s + part * count, group)
    column = lambda s, _: (0, group)
    along = lambda s, _: (0, s + part * count)
    whole_row = lambda array: pl.BlockSpec((LENGTH, array.shape[1]), row)
    narrow = pl.BlockSpec((LENGTH, 128), row)
    sums = pl.BlockSpec((8, LENGTH), along)
    elsewhere = pl.BlockSpec(memory_space=pl.ANY)
    arrays = [normed, pair, value_raw, grad_mixed, steps, log, vectors, value_in]
    in_specs = [
        whole_row(normed),
        whole_row(pair),
        pl.BlockSpec((LENGTH, WIDTH), block),
        pl.BlockSpec((LENGTH, WIDTH), block),
        narrow,
        narrow,
        pl.BlockSpec((8, WIDTH), column),
        pl.BlockSpec((width, WIDTH), column),
    ]
    aliases = {}
    if part or not first:
        aliases[1 + len(arrays)] = 0
        arrays.append(value_low)
        in_specs.append(elsewhere)
    if not first:
        arrays.append(grad_pair)
        in_specs.append(whole_row(grad_pair))
    if group == 1 and final:
        arrays.append(first_value)
        in_specs.append(const_spec(first_value.shape))
    if last:
        conv, step_pre, heads, step_in, row_sums, column_sums, direct = extra
        arrays += [conv, step_pre, heads, step_in, *row_sums, *column_sums, *direct]
        in_specs += [whole_row(conv), narrow, const_spec(heads.shape), const_spec(step_in.shape)]
        in_specs += [sums] * group + [narrow] * (2 * group)
    if last:
        wholes = [shape_of(tokens, 128, dtype=BF16), shape_of(tokens, STATE), shape_of(tokens, STATE)]
        whole_specs = [narrow] * 3
    else:
        wholes = [shape_of(tokens, LENGTH), shape_of(8, tokens), shape_of(tokens, 128), shape_of(tokens, 128)]
        whole_specs = [pl.BlockSpec((LENGTH, LENGTH), row), sums, narrow, narrow]
    if part:
        for k in range(len(wholes)):
            aliases[1 + len(arrays) + k] = 1 + k
        arrays += before
        in_specs += [elsewhere] * len(wholes) + [const_spec(array.shape) for array in before[len(wholes) :]]
    totals = [shape_of(8, WIDTH)]
    if last:
        totals += [shape_of(16, width), shape_of(8, 128)]
    if not final:
        totals += [shape_of(WIDTH, width)]
    else:
        totals += [shape_of(width // 2, 2 * WIDTH)] * 2 if group == 1 else [shape_of(width, WIDTH)]
        totals += [shape_of(8, width)]
    return pl.pallas_call(
        functools.partial(scan_back_kernel, group, groups, part, parts),
        grid_spec=pltpu.PrefetchScalarGridSpec(
            num_scalar_prefetch=1,
            grid=(count,),
            in_specs=in_specs,
            out_specs=[pl.BlockSpec((LENGTH, WIDTH), block)]
            + whole_specs
            + [const_spec(total.shape) for total in totals],
            scratch_shapes=[pltpu.VMEM((WIDTH, width), F32), pltpu.VMEM((LENGTH, LENGTH), F32)],
        ),
        out_shape=[shape_of(tokens, channels, dtype=BF16)] + wholes + totals,
        input_output_aliases=aliases,
        compiler_params=pltpu.CompilerParams(vmem_limit_bytes=60 * MIB),
        cost_estimate=cost(22 / parts),
        name="scan_back",
    )(digits, *arrays)


PACK_ROWS = 2560
SHARED_ROWS = 824


def pack_plan(width):
    chunks = width // 128
    plan, start = {}, 0
    for name, rows, parts in (
        ("state", width, 1), ("state_rows", 8, 1), ("norm", 8, chunks), ("value", width, WIDTH // 128),
        ("step", 16, chunks), ("value_rows", 8, chunks), ("gain", 8, chunks), ("heads", 8, 1),
    ):
        plan[name] = [(start + part * rows, start + (part + 1) * rows, part * 128) for part in range(parts)]
        start += rows * parts
    assert start == PACK_ROWS
    return plan


def state_kernel(
    digits, mine_ref, came_ref, raw_ref, normed_ref, state_in_ref, vectors_ref, value_ref, step_ref, gain_ref,
    heads_ref, *refs,
):
    refs = list(refs)
    value_rows, norm_rows = refs[:3], refs[3:7]
    low_ref, send_ref, keep_ref, grad_s, rows_s, packed = refs[7:]

    @pl.when(pl.program_id(0) == 0)
    def _():
        grad_s[...] = jnp.zeros_like(grad_s)
        rows_s[...] = jnp.zeros_like(rows_s)

    raw = raw_ref[...]
    kernel = vectors_ref[:TAPS, :]
    pre = convolve(raw, kernel, vectors_ref[TAPS : TAPS + 1, :])
    s = sigmoid(pre)
    grad_pre = (mine_ref[...] + came_ref[...]) * (s * (1.0 + pre * (1.0 - s)))
    grad_raw, rows = convolve_back(grad_pre, raw, kernel)
    low = grad_raw.astype(BF16)
    low_ref[...] = low
    grad_s[...] += dot_tn(low, normed_ref[...])
    rows_s[...] += rows

    @pl.when(pl.program_id(0) == pl.num_programs(0) - 1)
    def _():
        grad = grad_s[...].T
        norm = along_rows(jnp.sum(grad * state_in_ref[...].astype(F32), axis=1, keepdims=True))
        for part in norm_rows:
            norm = norm + part[...]
        sources = {
            "state": grad, "state_rows": rows_s[...], "norm": norm, "value": value_ref[...], "step": step_ref[...],
            "value_rows": jnp.concatenate([part[...] for part in value_rows], axis=1), "gain": gain_ref[...],
            "heads": heads_ref[...],
        }
        for name, parts in pack_plan(normed_ref.shape[1]).items():
            for start, stop, lane in parts:
                packed[start:stop, :] = sources[name][:, lane : lane + 128]
        half = send_ref.shape[0]
        pltpu.sync_copy(packed.at[pl.ds(pl.multiple_of((1 - digits[0]) * half, 8), half), :], send_ref)
        pltpu.sync_copy(packed.at[pl.ds(pl.multiple_of(digits[0] * half, 8), half), :], keep_ref)


def run_state(digits, core, mine, came, state_raw, normed, state_in, state_vectors, value, step, gain, heads,
              value_rows, norm_rows):
    tokens, width = normed.shape
    row = lambda s, *_: (s, 0)
    at = digits.shape[0] - 1
    half = lambda s, d: (s, d[at])
    column = lambda s, d: (0, d[at])
    consts = [value, step, gain, heads, *value_rows, *norm_rows]
    return pl.pallas_call(
        state_kernel,
        grid_spec=pltpu.PrefetchScalarGridSpec(
            num_scalar_prefetch=1,
            grid=(tokens // LENGTH,),
            in_specs=[
                pl.BlockSpec((LENGTH, STATE), row),
                pl.BlockSpec((LENGTH, STATE), row),
                pl.BlockSpec((LENGTH, STATE), half),
                pl.BlockSpec((LENGTH, width), row),
                pl.BlockSpec((width, STATE), column),
                pl.BlockSpec((8, STATE), column),
            ]
            + [const_spec(array.shape) for array in consts],
            out_specs=[pl.BlockSpec((LENGTH, STATE), row)] + [pl.BlockSpec(memory_space=pltpu.HBM)] * 2,
            scratch_shapes=[
                pltpu.VMEM((STATE, width), F32),
                pltpu.VMEM((8, STATE), F32),
                pltpu.VMEM((PACK_ROWS, 128), F32),
            ],
        ),
        out_shape=[shape_of(tokens, STATE, dtype=BF16)] + cut_shapes(PACK_ROWS, 128),
        compiler_params=pltpu.CompilerParams(vmem_limit_bytes=60 * MIB),
        cost_estimate=cost(8),
        name="state_back",
    )(digits, mine, came, state_raw, normed, state_in, state_vectors, *consts)


def in_kernel(core, gate_low_ref, value_low_ref, step_low_ref, state_low_ref, gate_in_ref, value_in_ref, step_in_ref,
              state_in_ref, partial_ref):
    partial_ref[...] = (
        dot_nt(gate_low_ref[...], gate_in_ref[...])
        + dot_nt(value_low_ref[...], value_in_ref[...])
        + dot_nn(step_low_ref[...], step_in_ref[...])
        + dot_nt(state_low_ref[...], state_in_ref[...])
    )


def run_in(part, parts, core, gate_low, value_low, step_low, state_low, gate_in, value_in, step_in, state_in):
    tokens, channels = gate_low.shape
    width = gate_in.shape[0]
    count = tokens // LENGTH // parts
    row = lambda s, c: (s + part * count, 0)
    return pl.pallas_call(
        in_kernel,
        grid_spec=pltpu.PrefetchScalarGridSpec(
            num_scalar_prefetch=1,
            grid=(count,),
            in_specs=[
                pl.BlockSpec((LENGTH, channels), row),
                pl.BlockSpec((LENGTH, channels), row),
                pl.BlockSpec((LENGTH, 128), row),
                pl.BlockSpec((LENGTH, STATE), row),
                const_spec((width, channels)),
                const_spec((width, channels)),
                const_spec((128, width)),
                pl.BlockSpec((width, STATE), lambda s, c: (0, c[0])),
            ],
            out_specs=pl.BlockSpec((LENGTH, width), lambda s, c: (s, 0)),
        ),
        out_shape=shape_of(count * LENGTH, width),
        compiler_params=pltpu.CompilerParams(vmem_limit_bytes=60 * MIB),
        cost_estimate=cost(7.5),
        name="grad_in",
    )(core, gate_low, value_low, step_low, state_low, gate_in, value_in, step_in, state_in)


def last_kernel(hidden_ref, cotangent_ref, own_ref, other_ref, out_own_ref, out_other_ref, norm_ref, *refs):
    block_ref, grad_ref = refs[-2:]
    rows = hidden_ref[...]
    block_ref[...] = rows + (out_own_ref[...] + out_other_ref[...])
    scale = lax.rsqrt(jnp.mean(rows * rows, axis=-1, keepdims=True) + EPSILON)
    product = (own_ref[...] + other_ref[...]) * norm_ref[NORM : NORM + 1, :]
    terms = jnp.sum(product * rows, axis=-1, keepdims=True)
    grad_ref[...] = (
        cotangent_ref[...] + product * scale - rows * (terms * (scale * scale * scale) / rows.shape[1])
    )


def run_last(part, parts, before, hidden, cotangent, own, other, out_own, out_other, norm):
    tokens, width = hidden.shape
    cycle = parts * own.shape[0] // tokens
    rows = LENGTH // 4
    steps = tokens // rows // parts
    far = pl.BlockSpec((rows, width), lambda s: (s + part * steps, 0))
    near = pl.BlockSpec((rows, width), lambda s: (s + part % cycle * steps, 0))
    return pl.pallas_call(
        last_kernel,
        grid=(steps,),
        in_specs=[far, far, near, near, far, far, const_spec((8, width))]
        + [pl.BlockSpec(memory_space=pl.ANY)] * len(before),
        out_specs=[far, far],
        out_shape=[shape_of(tokens, width), shape_of(tokens, width)],
        input_output_aliases={7 + k: k for k in range(len(before))},
        compiler_params=pltpu.CompilerParams(vmem_limit_bytes=56 * MIB),
        cost_estimate=cost(5.5),
        name="grad_hidden",
    )(hidden, cotangent, own, other, out_own, out_other, norm, *before)


def join_weights_kernel(bits, own_ref, came_ref, out_ref, gate_ref):
    half = own_ref.shape[0] // 2
    join_last(bits, own_ref, came_ref, out_ref, 0, half, 0)
    join_last(bits, own_ref, came_ref, gate_ref, 0, half, half)


def join_small_kernel(bits, own_ref, came_ref, out_ref, shared_ref):
    join_last(bits, own_ref, came_ref, out_ref, 0, own_ref.shape[0])
    shared_ref[...] = out_ref[:SHARED_ROWS, :]


def finish_kernel(digits, own_ref, came_ref, small_ref, other_ref, vectors_ref, value_ref, state_ref, norm_ref,
                  step_ref, kernel_ref, offset_ref, state_kernel_ref, state_offset_ref, bias_ref, decay_ref,
                  skip_ref, gain_ref):
    heads = step_ref.shape[0]
    first = digits[digits.shape[0] - 1] == 0
    width = value_ref.shape[0]
    plan = pack_plan(width)
    half = own_ref.shape[0]
    mine = pl.ds(pl.multiple_of(digits[0] * half, 8), half)
    other = pl.ds(pl.multiple_of((1 - digits[0]) * half, 8), half)
    value_ref[mine, : 2 * WIDTH] = own_ref[...]
    value_ref[other, : 2 * WIDTH] = came_ref[...]
    for start, stop, lane in plan["value"]:
        value_ref[:, 2 * WIDTH + lane : 2 * WIDTH + lane + 128] = small_ref[start:stop, :]
    ((start, stop, _),) = plan["state"]
    here, there = small_ref[start:stop, :], other_ref[start:stop, :]
    state_ref[:, :STATE] = jnp.where(first, here, there)
    state_ref[:, STATE:] = jnp.where(first, there, here)
    ((start, stop, _),) = plan["state_rows"]
    here, there = small_ref[start:stop, :], other_ref[start:stop, :]
    rows = jnp.concatenate([jnp.where(first, here, there), jnp.where(first, there, here)], axis=1)
    state_kernel_ref[...] = rows[:TAPS]
    state_offset_ref[...] = rows[TAPS : TAPS + 1].reshape(2 * STATE)
    whole = lambda name: jnp.concatenate([small_ref[start:stop, :] for start, stop, _ in plan[name]], axis=1)
    norm = whole("norm") + jnp.concatenate([other_ref[start:stop, :] for start, stop, _ in plan["norm"]], axis=1)
    norm_ref[...] = (norm[0:1] / vectors_ref[NORM : NORM + 1, :]).reshape(width)
    step_ref[...] = whole("step")[:heads]
    rows = whole("value_rows")
    kernel_ref[...] = rows[:TAPS]
    offset_ref[...] = rows[TAPS : TAPS + 1].reshape(width)
    gain_ref[...] = whole("gain")[0:1].reshape(width)
    rows_of_heads = whole("heads")
    bias_ref[...] = rows_of_heads[0:1, :heads].reshape(heads)
    decay_ref[...] = rows_of_heads[1:2, :heads].reshape(heads)
    down = lax.broadcasted_iota(jnp.int32, (width, 128), 0)
    begin = lax.broadcasted_iota(jnp.int32, (width, 128), 1) * HEAD_DIM
    picks = jnp.where((down >= begin) & (down < begin + HEAD_DIM), 1.0, 0.0).astype(BF16)
    high, middle, low = split3(rows)
    skip_rows = dot_nn(high, picks) + dot_nn(middle, picks) + dot_nn(low, picks)
    skip_ref[...] = skip_rows[TAPS + 1 : TAPS + 2, :heads].reshape(heads)


def prepare_kernel(
    norm_ref, offset_ref, gain_ref, skip_ref, kernel_ref, state_kernel_ref, state_offset_ref, bias_ref, decay_ref,
    step_ref, vectors_ref, state_vectors_ref, heads_ref, step_rows_ref,
):
    heads = step_ref.shape[0]
    width = norm_ref.shape[0]
    row = lambda ref: ref[...].reshape(1, ref.shape[0])
    vectors_ref[NORM : NORM + 1, :] = row(norm_ref)
    vectors_ref[OFFSET : OFFSET + 1, :] = row(offset_ref)
    vectors_ref[GAIN : GAIN + 1, :] = row(gain_ref)
    vectors_ref[KERNEL : KERNEL + TAPS, :] = kernel_ref[...]
    state_vectors_ref[...] = jnp.zeros_like(state_vectors_ref)
    state_vectors_ref[:TAPS, :] = state_kernel_ref[...]
    state_vectors_ref[TAPS : TAPS + 1, :] = row(state_offset_ref)
    heads_ref[...] = jnp.zeros_like(heads_ref)
    heads_ref[0:1, :heads] = row(bias_ref)
    heads_ref[1:2, :heads] = -jnp.exp(row(decay_ref))
    heads_ref[2:3, :heads] = row(skip_ref)
    lanes = lax.broadcasted_iota(jnp.int32, (128, width), 1)
    start = lax.broadcasted_iota(jnp.int32, (128, width), 0) * HEAD_DIM
    picks = jnp.where((lanes >= start) & (lanes < start + HEAD_DIM), 1.0, 0.0).astype(BF16)
    high, middle, low = split3(heads_ref[...])
    spread_rows = dot_nn(high, picks) + dot_nn(middle, picks) + dot_nn(low, picks)
    vectors_ref[SKIP : SKIP + 1, :] = spread_rows[2:3]
    step_rows_ref[...] = jnp.concatenate(
        [step_ref[...].astype(F32), jnp.zeros((128 - heads, width), F32)], axis=0
    ).astype(BF16)


def run_prepare(*arrays):
    width = arrays[0].shape[0]
    shapes = [shape_of(8, width), shape_of(8, 2 * STATE), shape_of(8, 128), shape_of(128, width, dtype=BF16)]
    return pl.pallas_call(
        prepare_kernel,
        out_shape=shapes,
        cost_estimate=cost(2),
        name="prepare",
    )(*arrays)


SWAP = [(0, 1), (1, 0)]
SCAN_PARTS = (1, 1, 2)
IN_PARTS = 2
LAST_PARTS = 4


def swap(value):
    return lax.ppermute(value, "tensor", SWAP)


def body(hidden, cotangent, norm_weight, gate_in, value_in, state_in, step_in, value_kernel, value_offset,
         state_kernel, state_offset, step_bias, log_decay, skip_weight, gated_norm, out_weight):
    core = lax.axis_index("tensor").astype(jnp.int32)
    tokens, width = hidden.shape
    channels = gate_in.shape[1]
    heads = step_in.shape[1]
    inner = 2 * channels
    count = lax.axis_size("dp")
    core_index = core.reshape(1)
    if count & (count - 1) == 0 and width % (8 * count) == 0 and PACK_ROWS % (8 * count) == 0:
        reduction = Reduction
        position = lax.axis_index("dp").astype(jnp.int32)
        bits = [
            jnp.where(core == 0, (position >> low) & 1, (position >> high) & 1)
            for low, high in zip(*bit_orders(count), strict=True)
        ]
    else:
        reduction = PlainReduction
        bits = [jnp.int32(0)]
    digits = jnp.stack(bits + [core])
    vectors, state_vectors, head_rows, step_rows = run_prepare(
        norm_weight, value_offset, gated_norm, skip_weight, value_kernel, state_kernel, state_offset, step_bias,
        log_decay, step_in.T,
    )

    (normed, state_raw, conv, pair_t, value_raw, gate_raw, mixed, gated, grad_scaled, step_pre, steps, log, sums) = run_forward(
        hidden, cotangent, vectors, state_vectors, head_rows, gate_in, value_in, state_in, step_rows, out_weight
    )
    grad_mixed, gate_low, partial_out, grad_gain, norm_gate, *pieces = run_norm_back(
        digits, normed, gated, mixed, gate_raw, grad_scaled, cotangent, sums, swap(sums), vectors, gate_in, out_weight, inner
    )
    weights_sum = reduction(pieces, digits, count, "weights")
    other_out = swap(partial_out)
    groups = channels // WIDTH
    value_low = grad_pair = first_value = None
    row_sums, column_sums, direct, value_rows, norm_rows = [], [], [], [], [norm_gate]
    ready = normed
    for group in range(groups):
        last = group == groups - 1
        extra = (conv, step_pre, head_rows, step_rows, row_sums, column_sums, direct) if last else None
        before = []
        parts = SCAN_PARTS[group % len(SCAN_PARTS)]
        for part in range(parts):
            value_low, *results = run_scan_back(
                group, groups, part, parts, digits, ready, pair_t, value_raw, grad_mixed, steps, log, vectors,
                value_in, value_low, grad_pair, first_value, extra, before,
            )
            wholes, totals = (results[:3], results[3:]) if last else (results[:4], results[4:])
            if part < parts - 1:
                before = [*wholes, totals[-1], *totals[:-1]]
            weights_sum.advance(value_low)
            if last:
                value_sum.advance(value_low)
            ready = tie(normed, value_low, weights_sum.held, other_out, *([value_sum.held] if last else []))
        value_rows.append(totals.pop(0))
        norm_rows.append(totals.pop(-1))
        if last:
            step_low, mine, outgoing = wholes
            grad_step, grad_heads, first_value = totals
        else:
            grad_pair = wholes[0]
            for kept, whole in zip((row_sums, column_sums, direct), wholes[1:], strict=True):
                kept.append(whole)
            if group == 1:
                value_sum = reduction(totals, digits, count, "value")
            else:
                (first_value,) = totals
    came = swap(tie(outgoing, weights_sum.held, value_sum.held))
    state_low, *pieces = run_state(
        digits, core, mine, came, state_raw, ready, state_in, state_vectors, first_value, grad_step, grad_gain,
        grad_heads, value_rows, norm_rows,
    )
    small_sum = reduction(pieces, digits, count, "small")
    value_sum.advance(state_low)
    weights_sum.advance(state_low)
    partials = []
    for part in range(IN_PARTS):
        low = tie(state_low, value_sum.held, weights_sum.held, small_sum.held)
        partial_in = run_in(
            part, IN_PARTS, core_index, gate_low, value_low, step_low, low, gate_in, value_in, step_rows, state_in
        )
        partials.append((partial_in, swap(partial_in)))
        small_sum.advance(partial_in)
        weights_sum.advance(partial_in)
        value_sum.advance(partial_in)
    results = []
    for part in range(LAST_PARTS):
        ready = tie(vectors, value_sum.held, weights_sum.held, small_sum.held)
        results = run_last(
            part, LAST_PARTS, results, hidden, cotangent, *partials[part * IN_PARTS // LAST_PARTS], partial_out,
            other_out, ready,
        )
        small_sum.advance(results[0])
        weights_sum.advance(results[0])
        value_sum.advance(results[0])
    block_out, grad_hidden = results
    grad_out_weight, grad_gate_in = small_call(
        join_weights_kernel, digits, list(weights_sum.halves()), [shape_of(channels, width), shape_of(width, channels)], "weights_last"
    )
    value_halves = value_sum.halves()
    small_sum.advance(value_halves[1])
    held, came = small_sum.halves()
    small, shared = small_call(
        join_small_kernel, digits, [tie(held, grad_out_weight), came], [shape_of(PACK_ROWS, 128), shape_of(SHARED_ROWS, 128)], "small_last"
    )
    (grad_value_in, grad_state_in, grad_norm, grad_step_in, grad_value_kernel, grad_value_offset, grad_state_kernel,
     grad_state_offset, grad_step_bias, grad_log_decay, grad_skip, grad_gain) = small_call(
        finish_kernel, digits, [*value_halves, small, swap(shared), vectors],
        [shape_of(width, channels), shape_of(width, 2 * STATE), shape_of(width), shape_of(heads, width),
         shape_of(TAPS, channels), shape_of(channels), shape_of(TAPS, 2 * STATE), shape_of(2 * STATE),
         shape_of(heads), shape_of(heads), shape_of(heads), shape_of(channels)], "finish",
    )
    return (
        block_out,
        grad_hidden,
        grad_norm,
        grad_gate_in,
        grad_value_in,
        grad_state_in,
        grad_step_in.T,
        grad_value_kernel,
        grad_value_offset,
        grad_state_kernel,
        grad_state_offset,
        grad_step_bias,
        grad_log_decay,
        grad_skip,
        grad_gain,
        grad_out_weight,
    )


def solution(mesh):
    in_specs = (
        P("dp", None),
        P("dp", None),
        P(),
        P(None, "tensor"),
        P(None, "tensor"),
        P(),
        P(None, "tensor"),
        P(None, "tensor"),
        P("tensor"),
        P(),
        P(),
        P("tensor"),
        P("tensor"),
        P("tensor"),
        P("tensor"),
        P("tensor", None),
    )
    out_specs = (
        P("dp", None),
        P("dp", None),
        P(),
        P(None, "tensor"),
        P(None, "tensor"),
        P(),
        P(None, "tensor"),
        P(None, "tensor"),
        P("tensor"),
        P(),
        P(),
        P("tensor"),
        P("tensor"),
        P("tensor"),
        P("tensor"),
        P("tensor", None),
    )
    return jax.shard_map(body, mesh=mesh, in_specs=in_specs, out_specs=out_specs, check_vma=False)
```
